32 devices in a mesh: dp: 8 (over y, x, core), replica: 4 (over z).
Axes of the slice: x: 2, y: 2, z: 4, core: 2. Of those that a mesh axis runs over, the one named last changes fastest.
Arguments:
- tokens: bfloat16 [128, 128, 768], P(('dp', 'replica')), may hold values from -6 to 6
- encodings: bfloat16 [128, 64, 768], P(('dp', 'replica')), may hold values from -6 to 6
- lengths: int32 [128], P(('dp', 'replica')), may hold values from 1 to 128, 8192 in all
- memory_ids: int32 [128, 10], P(('dp', 'replica')), may hold values from 0 to 31, all different within a row
- memory_keys: bfloat16 [32, 768], replicated, may hold values from -6 to 6
- memory_values: bfloat16 [32, 768], replicated, may hold values from -6 to 6
- gain_self: float32 [768], replicated, may hold values from 0.5 to 1.5
- gain_cross: float32 [768], replicated, may hold values from 0.5 to 1.5
- gain_ff: float32 [768], replicated, may hold values from 0.5 to 1.5
- rel_bias: float32 [32, 12], replicated, may hold values from -4 to 4
- self_qkv: bfloat16 [768, 2304], replicated, may hold values from -0.109375 to 0.109375
- self_out: bfloat16 [768, 768], replicated, may hold values from -0.875 to 0.875
- cross_q: bfloat16 [768, 768], replicated, may hold values from -0.0546875 to 0.0546875
- cross_kv: bfloat16 [768, 1536], replicated, may hold values from -0.21875 to 0.21875
- cross_out: bfloat16 [768, 768], replicated, may hold values from -0.875 to 0.875
- ff_in: bfloat16 [768, 3072], replicated, may hold values from -0.21875 to 0.21875
- ff_out: bfloat16 [3072, 768], replicated, may hold values from -0.109375 to 0.109375
- cotangent: bfloat16 [128, 128, 768], P(('dp', 'replica')), may hold values from -6 to 6
Outputs:
- layer_output: bfloat16 [128, 128, 768], P(('dp', 'replica'))
- grad_tokens: bfloat16 [128, 128, 768], P(('dp', 'replica'))
- grad_encodings: bfloat16 [128, 64, 768], P(('dp', 'replica'))
- grad_gain_self: float32 [768], P('dp')
- grad_gain_cross: float32 [768], P('dp')
- grad_gain_ff: float32 [768], P('dp')
- grad_rel_bias: float32 [32, 12], replicated
- grad_self_qkv: float32 [768, 2304], P('dp')
- grad_self_out: float32 [768, 768], P('dp')
- grad_cross_q: float32 [768, 768], P('dp')
- grad_cross_kv: float32 [768, 1536], P('dp')
- grad_cross_out: float32 [768, 768], P('dp')
- grad_ff_in: float32 [768, 3072], P('dp')
- grad_ff_out: float32 [3072, 768], P('dp')
- grad_memory_keys: float32 [32, 768], P('dp')
- grad_memory_values: float32 [32, 768], P('dp')
The draws below stay inside these ranges and needn't reach their ends.
Inputs may be any that keep to these rules, and one draw needn't show every extreme that they name: `lengths`: some question fills all 128 slots. `memory_ids`: each question names 10 different memory entries.
All inputs are finite; a program needn't handle non-finite values. No bound on the sum of `lengths` on one device may be relied on, other than what follows from the above.
Results may differ from the reference program's by a relative error of at most 0.023.
The reference program's roundings to bfloat16 on the way count: a program that leaves them out, or rounds other values in their place, can miss the bound.
Values sent between devices are 32-bit elements; how exact they have to be, the bound alone decides.
A program may use at most 192 MiB of HBM per device.

```python
import math
import jax
import jax.numpy as jnp
import numpy as np
from jax import lax

D = 768
H = 12
DH = 64
FF = 3072
NB = 32
MAXDIST = 128
LMAX = 128
ENC = 64
TOPK = 10
QUESTIONS = 128
MEM = 32


def block_levels(rng, extent, cuts, least, high):
    loudness, own = 1.0, jax.random.fold_in(rng, 6)
    for dim, blocks in cuts:
        steps = jnp.exp(jax.random.uniform(jax.random.fold_in(own, dim), (blocks,), jnp.float32, least / len(cuts), high / len(cuts)))
        loudness = loudness * jnp.repeat(steps, extent[dim] // blocks).reshape([-1 if axis == dim else 1 for axis in range(len(extent))])
    return loudness


def choose_distinct(own_key, rows, amount, top, lift):
    ranking = jax.random.permutation(jax.random.fold_in(own_key, 1), amount)
    favour = ranking
    for power in range(3):
        favour = favour * favour // amount
    favour = favour * lift // amount
    tickets = jax.random.randint(jax.random.fold_in(own_key, 2), (rows, amount), 0, 4096) + favour
    fixed_rows = jax.random.permutation(jax.random.fold_in(own_key, 3), rows)[jnp.arange(amount) % rows]
    tickets = jnp.where(jnp.arange(rows)[:, None] == fixed_rows[None, :], 1 << 14, tickets)
    merit = tickets * amount + jnp.arange(amount)
    return lax.top_k(merit.astype(jnp.int32), top)[1].astype(jnp.int32)


def profile(amount, total, reach, lean):
    loads = [(1 << 20) // math.isqrt(standing ** lean) + 1 for standing in range(2, amount + 1)]
    surplus, given = total - reach - (amount - 1), [1] * (amount - 1)
    while surplus > 0:
        candidates = [i for i in range(amount - 1) if given[i] < reach]
        whole, left = sum([loads[i] for i in candidates]), surplus
        for i in candidates:
            extra = min(reach - given[i], max(1, left * loads[i] // whole), surplus)
            given[i] = given[i] + extra
            surplus = surplus - extra
    return np.array([reach] + given)


def uneven(rng, count, total, bound, skew):
    if count == 2:
        one = jax.random.randint(rng, (), max(1, total - bound), min(bound, total - 1) + 1)
        return jnp.stack([one, total - one])
    sizes = jnp.asarray(profile(count, total, bound, skew), jnp.int32)
    pairs = (count - 1) // 2
    donor, taker = sizes[1:1 + 2 * pairs:2], sizes[2:2 + 2 * pairs:2]
    room = jnp.minimum(donor - 1, bound - taker)
    moved = jax.random.randint(jax.random.fold_in(rng, 1), (pairs,), 0, 1 << 20) % (room + 1)
    sizes = sizes.at[1:1 + 2 * pairs:2].set(donor - moved).at[2:2 + 2 * pairs:2].set(taker + moved)
    return sizes[jax.random.permutation(jax.random.fold_in(rng, 2), count)]


def noise(key, dims, scale, limit, cuts=(), kind=jnp.bfloat16):
    values = scale * jax.random.normal(key, dims, jnp.float32)
    if cuts:
        values = values * block_levels(key, dims, cuts, -0.22, 0.18)
    return jnp.clip(values, -limit, limit).astype(kind)


def setup_inputs(seed: int = 0) -> dict:
    arg_keys = jax.random.split(jax.random.key(seed), 19)
    tokens = noise(arg_keys[0], (QUESTIONS, LMAX, D), 1.0, 6.0, ((0, 32),))
    encodings = noise(arg_keys[1], (QUESTIONS, ENC, D), 1.0, 6.0, ((0, 32),))
    lengths = uneven(arg_keys[2], QUESTIONS, QUESTIONS * LMAX // 2, LMAX, 2).astype(jnp.int32)
    memory_ids = choose_distinct(arg_keys[3], QUESTIONS, MEM, TOPK, 2560)
    memory_keys = noise(arg_keys[4], (MEM, D), 1.0, 6.0)
    memory_values = noise(arg_keys[5], (MEM, D), 1.0, 6.0)
    gain_self = jnp.clip(1.0 + 0.1 * jax.random.normal(arg_keys[6], (D,), jnp.float32), 0.5, 1.5)
    gain_cross = jnp.clip(1.0 + 0.1 * jax.random.normal(arg_keys[7], (D,), jnp.float32), 0.5, 1.5)
    gain_ff = jnp.clip(1.0 + 0.1 * jax.random.normal(arg_keys[8], (D,), jnp.float32), 0.5, 1.5)
    rel_bias = noise(arg_keys[9], (NB, H), 1.0, 4.0, (), jnp.float32)
    self_qkv = noise(arg_keys[10], (D, 3 * D), (4 * D) ** -0.5, 0.109375)
    self_out = noise(arg_keys[11], (D, D), (D // 16) ** -0.5, 0.875)
    cross_q = noise(arg_keys[12], (D, D), (16 * D) ** -0.5, 0.0546875)
    cross_kv = noise(arg_keys[13], (D, 2 * D), D ** -0.5, 0.21875)
    cross_out = noise(arg_keys[14], (D, D), (D // 16) ** -0.5, 0.875)
    ff_in = noise(arg_keys[15], (D, FF), D ** -0.5, 0.21875)
    ff_out = noise(arg_keys[16], (FF, D), FF ** -0.5, 0.109375)
    cotangent = noise(arg_keys[17], (QUESTIONS, LMAX, D), 1.0, 6.0, ((0, 32),))
    return {"tokens": tokens, "encodings": encodings, "lengths": lengths, "memory_ids": memory_ids, "memory_keys": memory_keys, "memory_values": memory_values, "gain_self": gain_self, "gain_cross": gain_cross, "gain_ff": gain_ff, "rel_bias": rel_bias, "self_qkv": self_qkv, "self_out": self_out, "cross_q": cross_q, "cross_kv": cross_kv, "cross_out": cross_out, "ff_in": ff_in, "ff_out": ff_out, "cotangent": cotangent}


EPSILON = 1e-06
NEGATIVE = -1000000000.0
PRECISE = lax.Precision.HIGHEST

@jax.custom_vjp
def low(v):
    return lax.optimization_barrier(v.astype(jnp.bfloat16)).astype(jnp.float32)

@jax.custom_vjp
def low_back(v):
    return v

def low_keep(v):
    return (low(v), None)

def low_pass(kept, grad):
    return (grad,)

def back_keep(v):
    return (v, None)

def back_low(kept, grad):
    return (low(grad),)
low.defvjp(low_keep, low_pass)
low_back.defvjp(back_keep, back_low)

def bucket_table(length, buckets, distance):
    exact = buckets // 2
    apart = np.arange(length)[:, None] - np.arange(length)[None, :]
    apart = np.maximum(apart, 0)
    spread = np.log(np.maximum(apart, 1) / exact) / np.log(distance / exact) * (buckets - exact)
    larger = np.minimum(exact + np.floor(np.maximum(spread, 0.0)).astype(np.int64), buckets - 1)
    return np.where(apart < exact, apart, larger).astype(np.int32)

def rms_norm(values, gain):
    return values * lax.rsqrt(lax.optimization_barrier(jnp.mean(values * values, axis=-1, keepdims=True)) + EPSILON) * gain

def block_forward(tokens, encodings, params, lengths, memory_ids):
    gain_self, gain_cross, gain_ff, rel_bias, self_qkv, self_out, cross_q, cross_kv, cross_out, ff_in, ff_out, memory_keys, memory_values = params
    groups, length = (tokens.shape[0], tokens.shape[1])
    positions = jnp.arange(length).astype(jnp.int32)
    causal = positions[None, :] <= positions[:, None]
    buckets = jnp.asarray(bucket_table(length, NB, MAXDIST)).astype(jnp.int32)
    normed_one = low(rms_norm(tokens, gain_self))
    qkv_all = jnp.einsum('gtd,de->gte', normed_one, self_qkv, precision=PRECISE)
    qkv_all = low_back(low(qkv_all)).reshape(groups, length, 3, H, DH)
    queries, key_rows, val_rows = (qkv_all[:, :, 0], qkv_all[:, :, 1], qkv_all[:, :, 2])
    pos_bias = jnp.transpose(rel_bias[buckets], (2, 0, 1))
    scores = jnp.einsum('gthe,guhe->ghtu', queries, key_rows, precision=PRECISE) + pos_bias[None]
    scores = jnp.where(causal[None, None], low_back(scores), NEGATIVE)
    weights = low(jax.nn.softmax(scores, axis=-1))
    attended = jnp.einsum('ghtu,guhe->gthe', weights, val_rows, precision=PRECISE).reshape(groups, length, D)
    attended = low_back(low(attended))
    hidden_one = tokens + low_back(jnp.einsum('gtd,de->gte', attended, self_out, precision=PRECISE))
    normed_two = low(rms_norm(hidden_one, gain_cross))
    cross_query = jnp.einsum('gtd,de->gte', normed_two, cross_q, precision=PRECISE)
    cross_query = low_back(low(cross_query)).reshape(groups, length, H, DH)
    enc_kv = low_back(low(jnp.einsum('ged,df->gef', encodings, cross_kv, precision=PRECISE)))
    mem_index = memory_ids.astype(jnp.int32)
    mem_keys = memory_keys[mem_index]
    mem_vals = memory_values[mem_index]
    all_keys = jnp.concatenate([mem_keys, enc_kv[..., :D]], axis=1).reshape(groups, TOPK + ENC, H, DH)
    all_vals = jnp.concatenate([mem_vals, enc_kv[..., D:]], axis=1).reshape(groups, TOPK + ENC, H, DH)
    cross_scores = low_back(jnp.einsum('gthe,gkhe->ghtk', cross_query, all_keys, precision=PRECISE))
    cross_weights = low(jax.nn.softmax(cross_scores, axis=-1))
    cross_att = jnp.einsum('ghtk,gkhe->gthe', cross_weights, all_vals, precision=PRECISE).reshape(groups, length, D)
    cross_att = low_back(low(cross_att))
    hidden_two = hidden_one + low_back(jnp.einsum('gtd,de->gte', cross_att, cross_out, precision=PRECISE))
    normed_three = low(rms_norm(hidden_two, gain_ff))
    pre_act = low_back(jnp.einsum('gtd,df->gtf', normed_three, ff_in, precision=PRECISE))
    inner = low_back(low(jax.nn.gelu(pre_act, approximate=False)))
    final = hidden_two + low_back(jnp.einsum('gtf,fd->gtd', inner, ff_out, precision=PRECISE))
    valid = (positions[None, :] < lengths.astype(jnp.int32)[:, None])[..., None]
    return jnp.where(valid, final, jnp.zeros_like(final))

def reference(tokens, encodings, lengths, memory_ids, memory_keys, memory_values, gain_self, gain_cross, gain_ff, rel_bias, self_qkv, self_out, cross_q, cross_kv, cross_out, ff_in, ff_out, cotangent):
    params = tuple((weight_arr.astype(jnp.float32) for weight_arr in (gain_self, gain_cross, gain_ff, rel_bias, self_qkv, self_out, cross_q, cross_kv, cross_out, ff_in, ff_out, memory_keys, memory_values)))
    group_size = math.gcd(QUESTIONS, max(1, 4096 // LMAX))
    group_count = QUESTIONS // group_size

    def split_groups(array):
        return array.reshape((group_count, group_size) + array.shape[1:])

    def group_step(totals, batch):
        tok_part, enc_part, len_part, ids_part, cot_part = batch

        def forward(tok_float, enc_float, prm_float):
            return block_forward(tok_float, enc_float, prm_float, len_part, ids_part)
        result, pull = jax.vjp(forward, tok_part.astype(jnp.float32), enc_part.astype(jnp.float32), params)
        d_tokens, d_enc, d_params = pull(cot_part.astype(jnp.float32))
        totals = tuple((total + grad.astype(jnp.float32) for total, grad in zip(totals, d_params)))
        return (totals, (result.astype(jnp.bfloat16), d_tokens.astype(jnp.bfloat16), d_enc.astype(jnp.bfloat16)))
    zero_grads = tuple((jnp.zeros(weight_arr.shape, jnp.float32) for weight_arr in params))
    totals, (results, grad_tok, grad_enc) = lax.scan(group_step, zero_grads, (split_groups(tokens), split_groups(encodings), split_groups(lengths.astype(jnp.int32)), split_groups(memory_ids.astype(jnp.int32)), split_groups(cotangent)))
    layer_output = results.reshape(QUESTIONS, LMAX, D)
    grad_tokens = grad_tok.reshape(QUESTIONS, LMAX, D)
    grad_encodings = grad_enc.reshape(QUESTIONS, ENC, D)
    return (layer_output, grad_tokens, grad_encodings, totals[0], totals[1], totals[2], totals[3], totals[4], totals[5], totals[6], totals[7], totals[8], totals[9], totals[10], totals[11], totals[12])
```

```python
import jax
import jax.numpy as jnp
import numpy as np
from jax import lax
from jax.sharding import PartitionSpec as P
from jax.experimental import pallas as pl
from jax.experimental.pallas import tpu as pltpu
import functools

MAXDIST = 128


EPSILON = 1e-06
NEGATIVE = -1000000000.0


def bucket_table(length, buckets, distance):
    exact = buckets // 2
    apart = np.arange(length)[:, None] - np.arange(length)[None, :]
    apart = np.maximum(apart, 0)
    spread = np.log(np.maximum(apart, 1) / exact) / np.log(distance / exact) * (buckets - exact)
    larger = np.minimum(exact + np.floor(np.maximum(spread, 0.0)).astype(np.int64), buckets - 1)
    return np.where(apart < exact, apart, larger).astype(np.int32)


def rms_norm(values, gain):
    return values * lax.rsqrt(jnp.mean(values * values, axis=-1, keepdims=True) + EPSILON) * gain


def norm_back(values, gain, upstream):
    unused_out, pull = jax.vjp(rms_norm, values, gain)
    d_values, d_gain = pull(upstream)
    return (d_values, d_gain)


def gelu_exact(values):
    return jax.nn.gelu(values, approximate=False)


def gelu_back(values, upstream):
    unused_out, pull = jax.vjp(gelu_exact, values)
    return pull(upstream)[0]


def matmul_plain(left, right):
    return jnp.dot(left, right, preferred_element_type=jnp.float32)


def contract_rows(left, right):
    return lax.dot_general(
        left, right, (((0,), (0,)), ((), ())), preferred_element_type=jnp.float32
    )


def matmul_right_t(left, right):
    return lax.dot_general(
        left, right, (((1,), (1,)), ((), ())), preferred_element_type=jnp.float32
    )


def own_rows(vector):
    rows = vector.shape[0] // lax.axis_size("dp")
    return lax.dynamic_slice_in_dim(vector, lax.axis_index("dp") * rows, rows, 0)


MESH_ID = pl.DeviceIdType.MESH
SLAB = 128
CHUNK_COLS = 384
DEPTHS = dict(own=12, snd=3, r0=3, r1=4, r2=4, r3=4, r4=4)
LAG = dict(one=1, two=2, three=2, four=2, five=2, six=2)


class Reducer:
    def __init__(self, count, rows, bufs, sems, out_ref):
        self.count, self.rows, self.half = count, rows, rows // 2
        self.b, self.s, self.out = bufs, sems, out_ref
        dp, z = lax.axis_index("dp"), lax.axis_index("replica")
        self.core = lax.rem(dp, 2)
        self.x = lax.rem(dp // 2, 2)
        self.y = dp // 4
        self.inner = lax.rem((z + 1) // 2, 2) == 1
        self.end = lax.rem((z + 1) // 2, 2) == 0
        self.to_core = {"dp": dp + 1 - 2 * self.core, "replica": z}
        self.to_x = {"dp": dp + 2 - 4 * self.x, "replica": z}
        self.to_y = {"dp": dp + 4 - 8 * self.y, "replica": z}
        self.to_pair = {"dp": dp, "replica": z + 1 - 2 * lax.rem(z, 2)}
        self.to_mid = {"dp": dp, "replica": 3 - z}

    def enter(self):
        bar = pltpu.get_barrier_semaphore()
        for target in (self.to_core, self.to_x, self.to_y, self.to_pair, self.to_mid):
            pl.semaphore_signal(bar, inc=1, device_id=target, device_id_type=MESH_ID)
        pl.semaphore_wait(bar, 5)

    def copy(self, src, dst, send, recv, target):
        return pltpu.make_async_remote_copy(
            src_ref=src, dst_ref=dst, send_sem=send, recv_sem=recv, device_id=target,
            device_id_type=MESH_ID,
        )

    def core_copy(self, k):
        a, r = lax.rem(k, DEPTHS["snd"]), lax.rem(k, DEPTHS["r0"])
        return self.copy(self.b["snd"].at[a], self.b["r0"].at[r], self.s["snd"].at[a],
                         self.s["r0"].at[r], self.to_core)

    def first_copies(self, k):
        o, r = lax.rem(k, DEPTHS["own"]), lax.rem(k, DEPTHS["r1"])
        own, low, high = self.b["own"], pl.ds(0, self.half), pl.ds(self.half, self.half)
        return (
            self.copy(own.at[o, :, 1 - self.x, low, :], self.b["r1x"].at[r],
                      self.s["s1x"].at[r], self.s["r1x"].at[r], self.to_x),
            self.copy(own.at[o, 1 - self.y, :, high, :], self.b["r1y"].at[r],
                      self.s["s1y"].at[r], self.s["r1y"].at[r], self.to_y),
        )

    def second_copies(self, k):
        o, r = lax.rem(k, DEPTHS["own"]), lax.rem(k, DEPTHS["r2"])
        own, low, high = self.b["own"], pl.ds(0, self.half), pl.ds(self.half, self.half)
        return (
            self.copy(own.at[o, self.y, 1 - self.x, high, :], self.b["r2x"].at[r],
                      self.s["s2x"].at[r], self.s["r2x"].at[r], self.to_x),
            self.copy(own.at[o, 1 - self.y, self.x, low, :], self.b["r2y"].at[r],
                      self.s["s2y"].at[r], self.s["r2y"].at[r], self.to_y),
        )

    def mine(self, k):
        return self.b["own"].at[lax.rem(k, DEPTHS["own"]), self.y, self.x]

    def inward_copy(self, k):
        r = lax.rem(k, DEPTHS["r3"])
        return self.copy(self.mine(k), self.b["r3"].at[r], self.s["s3"].at[r], self.s["r3"].at[r],
                         self.to_pair)

    def middle_copy(self, k):
        r = lax.rem(k, DEPTHS["r4"])
        return self.copy(self.mine(k), self.b["r4"].at[r], self.s["s4"].at[r], self.s["r4"].at[r],
                         self.to_mid)

    def outward_copy(self, k):
        r = lax.rem(k, DEPTHS["r4"])
        return self.copy(self.mine(k), self.out.at[k], self.s["s5"].at[r], self.s["out"].at[k],
                         self.to_pair)

    def keep_copy(self, k):
        return pltpu.make_async_copy(self.mine(k), self.out.at[k], self.s["out"].at[k])

    def grant(self, name, k, depth, target):
        @pl.when(k + depth < self.count)
        def _():
            pl.semaphore_signal(self.s[name], inc=1, device_id=target, device_id_type=MESH_ID)

    def need(self, name, k, depth):
        @pl.when(k >= depth)
        def _():
            pl.semaphore_wait(self.s[name], 1)

    def fill(self, k, half_product):
        a, o = lax.rem(k, DEPTHS["snd"]), lax.rem(k, DEPTHS["own"])

        @pl.when(k >= DEPTHS["snd"])
        def _():
            self.core_copy(k - DEPTHS["snd"]).wait_send()

        rows = self.rows // 3
        away = half_product(1 - self.core)
        for g in range(4):
            for j in range(3):
                self.b["snd"][a, g, j * rows:(j + 1) * rows, :] = (
                    away[g * rows:(g + 1) * rows, j * SLAB:(j + 1) * SLAB])
        self.need("c0", k, DEPTHS["r0"])
        self.core_copy(k).start()
        here = half_product(self.core)
        for g in range(4):
            for j in range(3):
                self.b["own"][o, g // 2, g % 2, j * rows:(j + 1) * rows, :] = (
                    here[g * rows:(g + 1) * rows, j * SLAB:(j + 1) * SLAB])

    def stage_one(self, k):
        o, r = lax.rem(k, DEPTHS["own"]), lax.rem(k, DEPTHS["r0"])
        self.core_copy(k).wait_recv()
        own = self.b["own"]
        for g in range(4):
            own[o, g // 2, g % 2] += self.b["r0"][r, g]
        self.grant("c0", k, DEPTHS["r0"], self.to_core)
        self.need("c1x", k, DEPTHS["r1"])
        self.need("c1y", k, DEPTHS["r1"])
        for copy in self.first_copies(k):
            copy.start()

    def stage_two(self, k):
        o, r = lax.rem(k, DEPTHS["own"]), lax.rem(k, DEPTHS["r1"])
        low, high = slice(0, self.half), slice(self.half, self.rows)
        by_x, by_y = self.first_copies(k)
        own = self.b["own"]
        by_x.wait_recv()
        for g in range(2):
            own[o, g, self.x, low, :] += self.b["r1x"][r, g]
        by_y.wait_recv()
        for g in range(2):
            own[o, self.y, g, high, :] += self.b["r1y"][r, g]
        self.grant("c1x", k, DEPTHS["r1"], self.to_x)
        self.grant("c1y", k, DEPTHS["r1"], self.to_y)
        by_x.wait_send()
        by_y.wait_send()
        self.need("c2x", k, DEPTHS["r2"])
        self.need("c2y", k, DEPTHS["r2"])
        for copy in self.second_copies(k):
            copy.start()

    def stage_three(self, k):
        r = lax.rem(k, DEPTHS["r2"])
        low, high = slice(0, self.half), slice(self.half, self.rows)
        by_x, by_y = self.second_copies(k)
        mine = self.mine(k)
        by_x.wait_recv()
        mine[high, :] += self.b["r2x"][r]
        by_y.wait_recv()
        mine[low, :] += self.b["r2y"][r]
        self.grant("c2x", k, DEPTHS["r2"], self.to_x)
        self.grant("c2y", k, DEPTHS["r2"], self.to_y)
        by_x.wait_send()
        by_y.wait_send()

        @pl.when(self.end)
        def _():
            self.need("c3", k, DEPTHS["r3"])
            self.inward_copy(k).start()

    def stage_four(self, k):
        r = lax.rem(k, DEPTHS["r3"])

        @pl.when(self.end)
        def _():
            self.inward_copy(k).wait_send()

        @pl.when(self.inner)
        def _():
            self.inward_copy(k).wait_recv()
            self.mine(k)[...] += self.b["r3"][r]
            self.grant("c3", k, DEPTHS["r3"], self.to_pair)
            self.need("c4", k, DEPTHS["r4"])
            self.middle_copy(k).start()

    def stage_five(self, k):
        r = lax.rem(k, DEPTHS["r4"])

        @pl.when(self.inner)
        def _():
            self.middle_copy(k).wait()
            self.mine(k)[...] += self.b["r4"][r]
            self.grant("c4", k, DEPTHS["r4"], self.to_mid)
            self.outward_copy(k).start()
            self.keep_copy(k).start()

    def stage_six(self, k):
        @pl.when(self.inner)
        def _():
            self.outward_copy(k).wait_send()
        self.keep_copy(k).wait()

    def step(self, t, half_product=None):
        behind = 0
        due = []
        for name, stage in (("one", self.stage_one), ("two", self.stage_two), ("three", self.stage_three),
                            ("four", self.stage_four), ("five", self.stage_five), ("six", self.stage_six)):
            behind += LAG[name]
            due.append((behind, stage))
        for behind, stage in reversed(due):
            def run(behind=behind, stage=stage):
                stage(t - behind)
            pl.when((t >= behind) & (t - behind < self.count))(run)
        if half_product is not None:
            pl.when(t < self.count)(lambda: self.fill(t, half_product))

    def drain_send(self):
        for back in range(DEPTHS["snd"]):
            self.core_copy(self.count - 1 - back).wait_send()


TAIL = sum(LAG.values())


def reducer_scratch(count, rows):
    half = rows // 2
    vmem = lambda *shape: pltpu.VMEM(shape, jnp.float32)
    dma = lambda n: pltpu.SemaphoreType.DMA((n,))
    d = DEPTHS
    bufs = {
        "own": vmem(d["own"], 2, 2, rows, SLAB), "snd": vmem(d["snd"], 4, rows, SLAB),
        "r0": vmem(d["r0"], 4, rows, SLAB),
        "r1x": vmem(d["r1"], 2, half, SLAB), "r1y": vmem(d["r1"], 2, half, SLAB),
        "r2x": vmem(d["r2"], half, SLAB), "r2y": vmem(d["r2"], half, SLAB),
        "r3": vmem(d["r3"], rows, SLAB), "r4": vmem(d["r4"], rows, SLAB),
    }
    sems = {"snd": dma(d["snd"]), "r0": dma(d["r0"]), "out": dma(count),
            "s1x": dma(d["r1"]), "r1x": dma(d["r1"]), "s1y": dma(d["r1"]), "r1y": dma(d["r1"]),
            "s2x": dma(d["r2"]), "r2x": dma(d["r2"]), "s2y": dma(d["r2"]), "r2y": dma(d["r2"]),
            "s3": dma(d["r3"]), "r3": dma(d["r3"]), "s4": dma(d["r4"]), "r4": dma(d["r4"]),
            "s5": dma(d["r4"])}
    for name in ("c0", "c1x", "c1y", "c2x", "c2y", "c3", "c4"):
        sems[name] = pltpu.SemaphoreType.REGULAR
    return bufs, sems


CHUNKS, CHUNK_ROWS = 32, 288


def chunk_place(t):
    u = t - 16
    late = jnp.where(u < 4, 1 + u // 2, jnp.where(u < 8, 3, jnp.where(u < 10, 4, 5)))
    left = jnp.where(t < 8, 0, jnp.where(t < 16, 6 + (t - 8) // 2, late))
    col = jnp.where(t < 8, t * 384, jnp.where(t < 16, 3072 + lax.rem(t, 2) * 384, 3840 + u * 384))
    return left, pl.multiple_of(col, SLAB)


def reduce_kernel(keys, left_ref, right_ref, out_ref, *scratch):
    bufs = dict(zip(keys[0], scratch))
    sems = dict(zip(keys[1], scratch[len(keys[0]):]))
    reducer = Reducer(CHUNKS, CHUNK_ROWS, bufs, sems, out_ref)
    reducer.enter()

    def body(t, carry):
        left, col = chunk_place(t)

        def product(parity):
            return jnp.dot(left_ref[left, parity], right_ref[:, pl.ds(col, CHUNK_COLS)],
                           preferred_element_type=jnp.float32)

        reducer.step(t, product)
        return carry

    lax.fori_loop(0, CHUNKS + TAIL, body, 0)
    reducer.drain_send()


def reduced_products(left, right):
    bufs, sems = reducer_scratch(CHUNKS, CHUNK_ROWS)
    return pl.pallas_call(
        functools.partial(reduce_kernel, (list(bufs), list(sems))),
        out_shape=jax.ShapeDtypeStruct((CHUNKS, CHUNK_ROWS, SLAB), jnp.float32),
        in_specs=[pl.BlockSpec(memory_space=pltpu.VMEM)] * 2,
        out_specs=pl.BlockSpec(memory_space=pl.ANY),
        scratch_shapes=list(bufs.values()) + list(sems.values()),
        compiler_params=pltpu.CompilerParams(
            collective_id=0, has_side_effects=True, vmem_limit_bytes=60 * 2**20),
    )(left, right)


def unpack(chunks):
    count = chunks.shape[0]
    return chunks.reshape(count, 3, 96, SLAB).transpose(2, 0, 1, 3).reshape(96, count * 3 * SLAB)


def lefts(rows):
    turned = rows.T
    return turned.reshape(-1, 4, 2, 96, turned.shape[1]).transpose(0, 2, 1, 3, 4).reshape(
        -1, 2, 384, turned.shape[1])


def custom_reduce(normed_three, d_pre, inner, grad_low, cross_att, branch_two, normed_two, d_query,
                  enc_flat, d_enc_kv, attended, branch_one, normed_one, d_qkv):
    pad = normed_three.shape[0] - enc_flat.shape[0]
    enc_pad = jnp.pad(enc_flat, ((0, pad), (0, 0)))
    turned = inner.T.reshape(4, 2, 4, 96, inner.shape[0]).transpose(2, 1, 0, 3, 4)
    left = jnp.concatenate(
        [lefts(normed_three), lefts(cross_att), lefts(normed_two), lefts(enc_pad), lefts(attended),
         lefts(normed_one), turned.reshape(4, 2, 384, inner.shape[0])], axis=0)
    right = jnp.concatenate(
        [d_pre, grad_low, branch_two, d_query, jnp.pad(d_enc_kv, ((0, pad), (0, 0))), branch_one, d_qkv],
        axis=1)
    out = reduced_products(left, right)
    ff_out = out[8:16].reshape(4, 2, 3, 96, SLAB).transpose(0, 3, 1, 2, 4).reshape(384, 768)
    return (unpack(out[:8]), ff_out, unpack(out[16:18]), unpack(out[18:20]), unpack(out[20:24]),
            unpack(out[24:26]), unpack(out[26:32]))


def on_device(
    tokens,
    encodings,
    lengths,
    memory_ids,
    memory_keys,
    memory_values,
    gain_self,
    gain_cross,
    gain_ff,
    rel_bias,
    self_qkv,
    self_out,
    cross_q,
    cross_kv,
    cross_out,
    ff_in,
    ff_out,
    cotangent,
):
    questions, length, width = tokens.shape
    enc_len = encodings.shape[1]
    top_count = memory_ids.shape[1]
    num_buckets, heads = rel_bias.shape
    head_dim = width // heads
    token_rows = questions * length
    mem_rows = memory_keys.shape[0]
    positions = jnp.arange(length)
    causal = positions[None, :] <= positions[:, None]
    valid = (positions[None, :] < lengths[:, None]).reshape(token_rows, 1)
    buckets = jnp.asarray(bucket_table(length, num_buckets, MAXDIST)).astype(jnp.int32)
    one_hot = (buckets[:, :, None] == jnp.arange(num_buckets)[None, None, :]).astype(jnp.float32)
    pos_bias = jnp.transpose(rel_bias[buckets], (2, 0, 1))
    tok_flat = tokens.reshape(token_rows, width).astype(jnp.float32)
    normed_one = rms_norm(tok_flat, gain_self).astype(jnp.bfloat16)
    qkv_all = (
        matmul_plain(normed_one, self_qkv)
        .astype(jnp.bfloat16)
        .reshape(questions, length, 3, heads, head_dim)
    )
    queries, key_rows, val_rows = (qkv_all[:, :, 0], qkv_all[:, :, 1], qkv_all[:, :, 2])

    def self_scores():
        raw = (
            jnp.einsum("qthe,quhe->qhtu", queries, key_rows, preferred_element_type=jnp.float32)
            + pos_bias[None]
        )
        return jnp.where(causal[None, None], raw, NEGATIVE)

    scores = self_scores()
    self_lse = jax.nn.logsumexp(scores, axis=-1, keepdims=True)
    probs = jnp.exp(scores - self_lse)
    attended = jnp.einsum(
        "qhtu,quhe->qthe", probs.astype(jnp.bfloat16), val_rows, preferred_element_type=jnp.float32
    )
    attended = attended.astype(jnp.bfloat16).reshape(token_rows, width)
    hidden_one = tok_flat + matmul_plain(attended, self_out)
    normed_two = rms_norm(hidden_one, gain_cross).astype(jnp.bfloat16)
    cross_query = (
        matmul_plain(normed_two, cross_q)
        .astype(jnp.bfloat16)
        .reshape(questions, length, heads, head_dim)
    )
    enc_flat = encodings.reshape(questions * enc_len, width)
    enc_kv = (
        matmul_plain(enc_flat, cross_kv).astype(jnp.bfloat16).reshape(questions, enc_len, 2 * width)
    )
    mem_keys = jnp.take(memory_keys, memory_ids, axis=0)
    mem_vals = jnp.take(memory_values, memory_ids, axis=0)
    key_count = top_count + enc_len
    all_keys = jnp.concatenate([mem_keys, enc_kv[:, :, :width]], axis=1).reshape(
        questions, key_count, heads, head_dim
    )
    all_vals = jnp.concatenate([mem_vals, enc_kv[:, :, width:]], axis=1).reshape(
        questions, key_count, heads, head_dim
    )

    def cross_scores_of():
        return jnp.einsum(
            "qthe,qkhe->qhtk", cross_query, all_keys, preferred_element_type=jnp.float32
        )

    cross_scores = cross_scores_of()
    cross_lse = jax.nn.logsumexp(cross_scores, axis=-1, keepdims=True)
    cross_probs = jnp.exp(cross_scores - cross_lse)
    cross_att = jnp.einsum(
        "qhtk,qkhe->qthe",
        cross_probs.astype(jnp.bfloat16),
        all_vals,
        preferred_element_type=jnp.float32,
    )
    cross_att = cross_att.astype(jnp.bfloat16).reshape(token_rows, width)
    hidden_two = hidden_one + matmul_plain(cross_att, cross_out)
    normed_three = rms_norm(hidden_two, gain_ff).astype(jnp.bfloat16)
    pre_act = matmul_plain(normed_three, ff_in)
    inner = gelu_exact(pre_act).astype(jnp.bfloat16)
    final = hidden_two + matmul_plain(inner, ff_out)
    layer_output = (
        jnp.where(valid, final, 0.0).astype(jnp.bfloat16).reshape(questions, length, width)
    )
    grad_rows = jnp.where(valid, cotangent.reshape(token_rows, width).astype(jnp.float32), 0.0)
    grad_low = grad_rows.astype(jnp.bfloat16)
    d_ff_out = contract_rows(inner, grad_low)
    d_inner = matmul_right_t(grad_low, ff_out).astype(jnp.bfloat16)
    d_pre = gelu_back(pre_act, d_inner.astype(jnp.float32)).astype(jnp.bfloat16)
    d_ff_in = contract_rows(normed_three, d_pre)
    d_normed_three = matmul_right_t(d_pre, ff_in)
    d_back_three, d_gain_ff = norm_back(hidden_two, gain_ff, d_normed_three)
    grad_two = grad_rows + d_back_three
    branch_two = grad_two.astype(jnp.bfloat16)
    d_cross_out = contract_rows(cross_att, branch_two)
    d_cross_att = (
        matmul_right_t(branch_two, cross_out)
        .astype(jnp.bfloat16)
        .reshape(questions, length, heads, head_dim)
    )
    cross_again = jnp.exp(cross_scores_of() - cross_lse)
    d_all_vals = jnp.einsum(
        "qhtk,qthe->qkhe",
        cross_again.astype(jnp.bfloat16),
        d_cross_att,
        preferred_element_type=jnp.float32,
    )
    d_cross_probs = jnp.einsum(
        "qthe,qkhe->qhtk", d_cross_att, all_vals, preferred_element_type=jnp.float32
    )
    cross_delta = jnp.sum(cross_again * d_cross_probs, axis=-1, keepdims=True)
    d_cross_scores = (cross_again * (d_cross_probs - cross_delta)).astype(jnp.bfloat16)
    d_query = jnp.einsum(
        "qhtk,qkhe->qthe", d_cross_scores, all_keys, preferred_element_type=jnp.float32
    )
    d_query = d_query.astype(jnp.bfloat16).reshape(token_rows, width)
    d_all_keys = jnp.einsum(
        "qhtk,qthe->qkhe", d_cross_scores, cross_query, preferred_element_type=jnp.float32
    )
    d_all_keys = d_all_keys.reshape(questions, key_count, width)
    d_all_vals = d_all_vals.reshape(questions, key_count, width)
    d_enc_kv = jnp.concatenate([d_all_keys[:, top_count:], d_all_vals[:, top_count:]], axis=-1)
    d_enc_kv = d_enc_kv.astype(jnp.bfloat16).reshape(questions * enc_len, 2 * width)
    d_cross_kv = contract_rows(enc_flat, d_enc_kv)
    grad_encodings = (
        matmul_right_t(d_enc_kv, cross_kv).astype(jnp.bfloat16).reshape(questions, enc_len, width)
    )
    d_cross_q = contract_rows(normed_two, d_query)
    d_normed_two = matmul_right_t(d_query, cross_q)
    flat_ids = memory_ids.reshape(questions * top_count)
    d_mem_keys = (
        jnp.zeros((mem_rows, width), jnp.float32)
        .at[flat_ids]
        .add(d_all_keys[:, :top_count].reshape(questions * top_count, width))
    )
    d_mem_vals = (
        jnp.zeros((mem_rows, width), jnp.float32)
        .at[flat_ids]
        .add(d_all_vals[:, :top_count].reshape(questions * top_count, width))
    )
    d_back_two, d_gain_cross = norm_back(hidden_one, gain_cross, d_normed_two)
    grad_one = grad_two + d_back_two
    sum_mem_keys, sum_mem_vals = lax.psum(
        (lax.psum_scatter(d_mem_keys, "dp", scatter_dimension=0, tiled=True),
         lax.psum_scatter(d_mem_vals, "dp", scatter_dimension=0, tiled=True)), "replica")
    branch_one = grad_one.astype(jnp.bfloat16)
    d_self_out = contract_rows(attended, branch_one)
    d_attended = (
        matmul_right_t(branch_one, self_out)
        .astype(jnp.bfloat16)
        .reshape(questions, length, heads, head_dim)
    )
    self_again = jnp.exp(self_scores() - self_lse)
    d_val_rows = jnp.einsum(
        "qhtu,qthe->quhe",
        self_again.astype(jnp.bfloat16),
        d_attended,
        preferred_element_type=jnp.float32,
    )
    d_self_probs = jnp.einsum(
        "qthe,quhe->qhtu", d_attended, val_rows, preferred_element_type=jnp.float32
    )
    self_delta = jnp.sum(self_again * d_self_probs, axis=-1, keepdims=True)
    d_self_scores = (self_again * (d_self_probs - self_delta)).astype(jnp.bfloat16)
    d_bias_cells = jnp.sum(d_self_scores.astype(jnp.float32), axis=0)
    d_rel_bias = jnp.einsum("tun,htu->nh", one_hot, d_bias_cells, precision=lax.Precision.HIGHEST)
    d_queries = jnp.einsum(
        "qhtu,quhe->qthe", d_self_scores, key_rows, preferred_element_type=jnp.float32
    )
    d_key_rows = jnp.einsum(
        "qhtu,qthe->quhe", d_self_scores, queries, preferred_element_type=jnp.float32
    )
    d_qkv = (
        jnp.stack([d_queries, d_key_rows, d_val_rows], axis=2)
        .astype(jnp.bfloat16)
        .reshape(token_rows, 3 * width)
    )
    d_self_qkv = contract_rows(normed_one, d_qkv)
    d_normed_one = matmul_right_t(d_qkv, self_qkv)
    d_back_one, d_gain_self = norm_back(tok_flat, gain_self, d_normed_one)
    grad_tokens = (grad_one + d_back_one).astype(jnp.bfloat16).reshape(questions, length, width)
    if lax.axis_size("dp") == 8 and lax.axis_size("replica") == 4:
        (sum_ff_in, sum_ff_out, sum_cross_out, sum_cross_q, sum_cross_kv, sum_self_out,
         sum_self_qkv) = custom_reduce(
            normed_three, d_pre, inner, grad_low, cross_att, branch_two, normed_two, d_query,
            enc_flat, d_enc_kv, attended, branch_one, normed_one, d_qkv)
    else:
        parts = (d_ff_in, d_ff_out, d_cross_out, d_cross_q, d_cross_kv, d_self_out, d_self_qkv)
        (sum_ff_in, sum_ff_out, sum_cross_out, sum_cross_q, sum_cross_kv, sum_self_out,
         sum_self_qkv) = lax.psum(
            tuple(lax.psum_scatter(p, "dp", scatter_dimension=0, tiled=True) for p in parts),
            "replica")
    sum_rel_bias, all_gain_self, all_gain_cross, all_gain_ff = lax.psum(
        (d_rel_bias, d_gain_self, d_gain_cross, d_gain_ff), ("dp", "replica")
    )
    sum_gain_self = own_rows(all_gain_self)
    sum_gain_cross = own_rows(all_gain_cross)
    sum_gain_ff = own_rows(all_gain_ff)
    return (
        layer_output,
        grad_tokens,
        grad_encodings,
        sum_gain_self,
        sum_gain_cross,
        sum_gain_ff,
        sum_rel_bias,
        sum_self_qkv,
        sum_self_out,
        sum_cross_q,
        sum_cross_kv,
        sum_cross_out,
        sum_ff_in,
        sum_ff_out,
        sum_mem_keys,
        sum_mem_vals,
    )


def solution(mesh):
    placed = (
        P(("dp", "replica"), None, None),
        P(("dp", "replica"), None, None),
        P(("dp", "replica")),
        P(("dp", "replica"), None),
        P(),
        P(),
        P(),
        P(),
        P(),
        P(),
        P(),
        P(),
        P(),
        P(),
        P(),
        P(),
        P(),
        P(("dp", "replica"), None, None),
    )
    return jax.shard_map(
        on_device,
        mesh=mesh,
        in_specs=placed,
        out_specs=(
            P(("dp", "replica"), None, None),
            P(("dp", "replica"), None, None),
            P(("dp", "replica"), None, None),
            P("dp"),
            P("dp"),
            P("dp"),
            P(),
            P("dp", None),
            P("dp", None),
            P("dp", None),
            P("dp", None),
            P("dp", None),
            P("dp", None),
            P("dp", None),
            P("dp", None),
            P("dp", None),
        ),
        check_vma=False,
    )
```

```python
import functools
from types import SimpleNamespace as Bunch

import jax
import jax.numpy as jnp
import numpy as np
from jax import lax
from jax.experimental import pallas as pl
from jax.experimental.pallas import tpu as pltpu
from jax.sharding import PartitionSpec as P

F32, BF16 = jnp.float32, jnp.bfloat16
EPSILON = 1e-06
NEGATIVE = -1000000000.0
MAXDIST = 128
LANES = 128
E3, B2, CQ, EKV, B1, QKV, RIGHT = 0, 768, 1536, 2304, 3840, 4608, 6912
L_H3, L_O2, L_H2, L_ENC, L_O, L_H1, L_R = 0, 1, 2, 3, 4, 5, 6
FF_TILE = 384
MEM_PAD = 16


def nn(a, b, **kw):
    return lax.dot_general(a, b, (((1,), (0,)), ((), ())), preferred_element_type=F32, **kw)


def nt(a, b, **kw):
    return lax.dot_general(a, b, (((1,), (1,)), ((), ())), preferred_element_type=F32, **kw)


def tn(a, b, **kw):
    return lax.dot_general(a, b, (((0,), (0,)), ((), ())), preferred_element_type=F32, **kw)


def bucket_of(apart, buckets, distance):
    exact = buckets // 2
    spread = np.log(np.maximum(apart, 1) / exact) / np.log(distance / exact) * (buckets - exact)
    larger = np.minimum(exact + np.floor(np.maximum(spread, 0.0)).astype(np.int64), buckets - 1)
    return np.where(apart < exact, apart, larger).astype(np.int32)


def bucket_tables(length, buckets):
    lane = np.arange(length)
    spread = [bucket_of((length - lane) % length, buckets, MAXDIST), bucket_of(length - 1 - lane, buckets, MAXDIST)]
    return np.stack([(np.arange(buckets)[:, None] == row[None]).astype(np.float32) for row in spread])


def root_scale(v):
    return lax.rsqrt(jnp.mean(v * v, axis=-1, keepdims=True) + EPSILON)


def normed(v, gain):
    return (v * root_scale(v) * gain).astype(BF16)


def norm_pull(v, gain, w):
    scale = root_scale(v)
    gw = w * gain
    back = scale * gw - v * (scale * scale * scale) * jnp.mean(gw * v, axis=-1, keepdims=True)
    return back, jnp.sum(w * v * scale, axis=0, keepdims=True)


def head_masks():
    lane = lax.broadcasted_iota(jnp.int32, (1, LANES), 1)
    first = jnp.where(lane < LANES // 2, 1.0, 0.0)
    return first.astype(BF16), (1.0 - first).astype(BF16), first > 0.5


def stacked(rows, m0, m1):
    return jnp.concatenate([rows * m0, rows * m1], axis=0)


def pair_softmax(s):
    parts = []
    for part in (s[:, :LANES], s[:, LANES:]):
        e = jnp.exp(part - jnp.max(part, axis=-1, keepdims=True))
        parts.append(e * (1.0 / jnp.sum(e, axis=-1, keepdims=True)))
    return jnp.concatenate(parts, axis=1)


def pair_pull(p, dp):
    parts = []
    for lo in (0, LANES):
        a, b = p[:, lo:lo + LANES], dp[:, lo:lo + LANES]
        parts.append((a * (b - jnp.sum(a * b, axis=-1, keepdims=True))).astype(BF16))
    return jnp.concatenate(parts, axis=1)


class Layer:
    def __init__(self, given, hbm, out, vm, load, store):
        vars(self).update(vars(given))
        vars(self).update(vars(vm))
        self.hbm, self.out, self.store = hbm, out, store
        self.questions, self.length, self.enc_len = 4, 128, 64
        self.rows = self.questions * self.length
        self.load = Bunch(**{name: pltpu.make_async_copy(vars(hbm)[name], vars(vm)[name], sem)
                             for name, sem in vars(load).items()})

    def ff_loads(self, j):
        slot = lax.rem(j, 2)
        at = pl.ds(pl.multiple_of(j * FF_TILE, FF_TILE), FF_TILE)
        return (
            pltpu.make_async_copy(self.hbm.ff_in.at[:, at], self.wi.at[slot], self.wi_sem.at[slot]),
            pltpu.make_async_copy(self.hbm.ff_out.at[at, :], self.wo.at[slot], self.wo_sem.at[slot]),
        )

    def q_rows(self, q, n=128):
        return pl.ds(pl.multiple_of(q * n, n), n)

    def put_left(self, index, q, rows):
        turned = rows.T
        width = turned.shape[1]
        at = self.q_rows(q, width)
        for b in range(8):
            self.left[index, b % 2, (b // 2) * 96:(b // 2 + 1) * 96, at] = turned[b * 96:(b + 1) * 96]

    def bias_tables(self):
        table = nn(self.rel_bias[...], self.tables[0], precision=lax.Precision.HIGHEST)
        for p in range(6):
            for k in range(2):
                row = table[2 * p + k:2 * p + k + 1, :]
                self.bias[p, :, k * LANES:(k + 1) * LANES] = pltpu.roll(
                    jnp.broadcast_to(row, (LANES, LANES)), 0, 1, stride=1, stride_axis=0)

    def memory_rows(self):
        entries = self.memory_keys.shape[0]
        slot = lax.broadcasted_iota(jnp.int32, (MEM_PAD, entries), 0)
        entry = lax.broadcasted_iota(jnp.int32, (MEM_PAD, entries), 1)
        for q in range(self.questions):
            wanted = jnp.full((MEM_PAD, entries), -1, jnp.int32)
            for i in range(self.ids.shape[1]):
                wanted = jnp.where(slot == i, self.ids[q, i], wanted)
            pick = jnp.where(wanted == entry, 1.0, 0.0).astype(BF16)
            self.mem_k[q] = nn(pick, self.memory_keys[...]).astype(BF16)
            self.mem_v[q] = nn(pick, self.memory_values[...]).astype(BF16)

    def causal(self):
        row = lax.broadcasted_iota(jnp.int32, (LANES, 2 * LANES), 0)
        col = lax.rem(lax.broadcasted_iota(jnp.int32, (LANES, 2 * LANES), 1), LANES)
        return col <= row

    def self_probs(self, q2, k2, p, allowed):
        return pair_softmax(jnp.where(allowed, nt(q2, k2) + self.bias[p], NEGATIVE))

    def cross_probs(self, q2, k2, present):
        return pair_softmax(jnp.where(present, nt(q2, k2), -1e30))

    def present(self):
        col = lax.rem(lax.broadcasted_iota(jnp.int32, (1, 2 * LANES), 1), LANES)
        return col < self.enc_len + self.ids.shape[1]

    def cross_side(self, q, p, memory, base):
        enc = self.right[self.q_rows(q, self.enc_len), base + p * LANES:base + (p + 1) * LANES]
        mem = memory[q, :, p * LANES:(p + 1) * LANES]
        return jnp.concatenate([enc, mem, jnp.zeros((LANES - 64 - MEM_PAD, LANES), BF16)], axis=0)

    def forward(self, enter):
        load = self.load
        for copy in (load.tokens, load.self_qkv, load.encodings, load.cross_kv, load.memory_keys, load.memory_values,
                     load.self_out, load.cross_q, load.cross_out):
            copy.start()
        for copy in self.ff_loads(0) + self.ff_loads(1):
            copy.start()
        load.cotangent.start()
        enter()
        for n, gain in enumerate((self.gain_self, self.gain_cross, self.gain_ff)):
            self.gains[n:n + 1, :] = gain[...].reshape(1, gain.shape[0])
        right = self.right
        self.bias_tables()
        self.load.tokens.wait()

        def norm_one(q, c):
            at = self.q_rows(q)
            self.hid[at] = normed(self.tokens[at].astype(F32), self.gains[0:1])
            return c
        lax.fori_loop(0, 4, norm_one, 0)
        self.load.self_qkv.wait()

        def qkv_tile(j, c):
            at = self.q_rows(j, 256)
            right[:, pl.ds(pl.multiple_of(QKV + j * 256, 256), 256)] = nn(self.hid[...], self.self_qkv[:, at]).astype(BF16)
            return c
        lax.fori_loop(0, 9, qkv_tile, 0)

        m0, m1, _ = head_masks()
        allowed = self.causal()

        def self_attention(q, c):
            at = self.q_rows(q)
            for p in range(6):
                lo = p * LANES
                q2, k2, v2 = (right[at, QKV + 768 * i + lo:QKV + 768 * i + lo + LANES] for i in range(3))
                probs = self.self_probs(q2, stacked(k2, m0, m1), p, allowed).astype(BF16)
                self.att[at, lo:lo + LANES] = nn(probs, stacked(v2, m0, m1)).astype(BF16)
            return c
        lax.fori_loop(0, 4, self_attention, 0)

        self.load.encodings.wait()
        self.load.cross_kv.wait()
        enc_rows = self.questions * self.enc_len

        def ekv_tile(j, c):
            at = self.q_rows(j, 256)
            col = pl.ds(pl.multiple_of(EKV + j * 256, 256), 256)
            right[0:enc_rows, col] = nn(self.encodings[...], self.cross_kv[:, at]).astype(BF16)
            return c
        lax.fori_loop(0, 6, ekv_tile, 0)
        self.load.memory_keys.wait()
        self.load.memory_values.wait()
        self.memory_rows()
        self.load.self_out.wait()

        def out_tile(j, c):
            at = self.q_rows(j, 256)
            self.y1[:, at] = self.tokens[:, at].astype(F32) + nn(self.att[...], self.self_out[:, at])
            return c
        lax.fori_loop(0, 3, out_tile, 0)

        def norm_two(q, c):
            at = self.q_rows(q)
            self.hid[at] = normed(self.y1[at], self.gains[1:2])
            return c
        lax.fori_loop(0, 4, norm_two, 0)
        self.load.cross_q.wait()

        def cq_tile(j, c):
            at = self.q_rows(j, 256)
            right[:, pl.ds(pl.multiple_of(CQ + j * 256, 256), 256)] = nn(self.hid[...], self.cross_q[:, at]).astype(BF16)
            return c
        lax.fori_loop(0, 3, cq_tile, 0)
        present = self.present()

        def cross_attention(q, c):
            at = self.q_rows(q)
            for p in range(6):
                lo = p * LANES
                keys = self.cross_side(q, p, self.mem_k, EKV)
                vals = self.cross_side(q, p, self.mem_v, EKV + 768)
                probs = self.cross_probs(right[at, CQ + lo:CQ + lo + LANES], stacked(keys, m0, m1), present)
                self.att2[at, lo:lo + LANES] = nn(probs.astype(BF16), stacked(vals, m0, m1)).astype(BF16)
            return c
        lax.fori_loop(0, 4, cross_attention, 0)
        self.load.cross_out.wait()

        def out2_tile(j, c):
            at = self.q_rows(j, 256)
            self.y2[:, at] = self.y1[:, at] + nn(self.att2[...], self.cross_out[:, at])
            return c
        lax.fori_loop(0, 3, out2_tile, 0)
        self.load.cotangent.wait()

        def norm_three(q, c):
            at = self.q_rows(q)
            h3 = normed(self.y2[at], self.gains[2:3])
            self.hid[at] = h3
            self.put_left(L_H3, q, h3)
            valid = lax.broadcasted_iota(jnp.int32, (LANES, 1), 0) < self.lengths[q]
            cot = jnp.where(valid, self.cotangent[at].astype(F32), 0.0)
            right[at, E3:E3 + 768] = cot.astype(BF16)
            return c
        lax.fori_loop(0, 4, norm_three, 0)

    def feed_forward(self):
        right = self.right
        self.y3[...] = self.y2[...]
        self.dh3[...] = jnp.zeros_like(self.dh3)

        def tile(j, c):
            slot = lax.rem(j, 2)
            for copy in self.ff_loads(j):
                copy.wait()
            self.z[...] = nn(self.hid[...], self.wi[slot])
            self.dr[...] = nt(right[:, E3:E3 + 768], self.wo[slot])

            def gelu(i, c):
                at = pl.ds(pl.multiple_of(i * 32, 32), 32)
                z = self.z[at]
                cdf = 0.5 * (1.0 + lax.erf(z * 0.7071067811865476))
                pdf = jnp.exp(-0.5 * z * z) * 0.3989422804014327
                self.act[at] = (z * cdf).astype(BF16)
                dr = self.dr[at].astype(BF16).astype(F32)
                self.dz[at] = (dr * (cdf + z * pdf)).astype(BF16)
                return c
            lax.fori_loop(0, 16, gelu, 0)

            act = self.act[...]
            dz = self.dz[...]

            self.advance(j, 0, lambda: dz)
            turned = act.T
            for g in range(4):
                at = pl.ds(pl.multiple_of((j // 2) * 96, 96), 96)
                self.left[L_R + g, lax.rem(j, 2), at, :] = turned[g * 96:(g + 1) * 96]
            for n in range(3):
                at = slice(n * 256, (n + 1) * 256)
                self.y3[:, at] += nn(act, self.wo[slot][:, at])
                self.dh3[:, at] += nt(dz, self.wi[slot][at])

            @pl.when(j + 2 < 8)
            def _():
                for copy in self.ff_loads(j + 2):
                    copy.start()
            return c
        lax.fori_loop(0, 8, tile, 0)

        def finish(q, c):
            at = self.q_rows(q)
            valid = lax.broadcasted_iota(jnp.int32, (LANES, 1), 0) < self.lengths[q]
            self.layer_output[at] = jnp.where(valid, self.y3[at], 0.0).astype(BF16)
            return c
        lax.fori_loop(0, 4, finish, 0)
        self.stores()[0].start()

    def stores(self):
        return [pltpu.make_async_copy(vars(self)[name], vars(self.out)[name], sem) for name, sem in vars(self.store).items()]

    def backward_cross(self):
        right = self.right
        m0, m1, low_lanes = head_masks()
        present = self.present()
        enc_rows = self.questions * self.enc_len
        self.dgains[...] = jnp.zeros_like(self.dgains)
        self.left[L_ENC, :, :, enc_rows:] = jnp.zeros((2, 384, self.rows - enc_rows), BF16)
        turned = self.encodings[...].T
        for b in range(8):
            self.left[L_ENC, b % 2, (b // 2) * 96:(b // 2 + 1) * 96, 0:enc_rows] = turned[b * 96:(b + 1) * 96]
        right[enc_rows:, EKV:EKV + 1536] = jnp.zeros((self.rows - enc_rows, 1536), BF16)

        def pick(both):
            return jnp.where(low_lanes, both[:LANES], both[LANES:])

        def question(q, c):
            at = self.q_rows(q)
            enc_at = self.q_rows(q, self.enc_len)
            mem_at = self.q_rows(q, MEM_PAD)
            back, gain = norm_pull(self.y2[at], self.gains[2:3], self.dh3[at])
            self.dgains[2:3] += gain
            e2 = right[at, E3:E3 + 768].astype(F32) + back
            self.y3[at] = e2
            b2 = e2.astype(BF16)
            right[at, B2:B2 + 768] = b2
            self.up[...] = nt(b2, self.cross_out[...]).astype(BF16)
            for p in range(6):
                lo = p * LANES
                pair = slice(lo, lo + LANES)
                keys = stacked(self.cross_side(q, p, self.mem_k, EKV), m0, m1)
                vals = stacked(self.cross_side(q, p, self.mem_v, EKV + 768), m0, m1)
                cq = right[at, CQ + lo:CQ + lo + LANES]
                probs = self.cross_probs(cq, keys, present)
                up = self.up[:, pair]
                dvals = pick(tn(probs.astype(BF16), up))
                ds = pair_pull(probs, nt(up, vals))
                dkeys = pick(tn(ds, cq))
                right[at, CQ + lo:CQ + lo + LANES] = nn(ds, keys).astype(BF16)
                right[enc_at, EKV + lo:EKV + lo + LANES] = dkeys[:64].astype(BF16)
                right[enc_at, EKV + 768 + lo:EKV + 768 + lo + LANES] = dvals[:64].astype(BF16)
                self.dmem_k[mem_at, pair] = dkeys[64:64 + MEM_PAD]
                self.dmem_v[mem_at, pair] = dvals[64:64 + MEM_PAD]
                if p == 2:
                    self.advance(8 + 2 * q)
            self.grad_encodings[enc_at] = nt(right[enc_at, EKV:EKV + 1536], self.cross_kv[...]).astype(BF16)
            y1 = self.y1[at]
            back, gain = norm_pull(y1, self.gains[1:2], nt(right[at, CQ:CQ + 768], self.cross_q[...]))
            self.dgains[1:2] += gain
            self.y3[at] += back
            self.put_left(L_H2, q, normed(y1, self.gains[1:2]))
            self.put_left(L_O2, q, self.att2[at])
            self.advance(9 + 2 * q)
            return c
        lax.fori_loop(0, 4, question, 0)

    def backward_self(self):
        right = self.right
        m0, m1, low_lanes = head_masks()
        allowed = self.causal()
        self.dbias[...] = jnp.zeros_like(self.dbias)

        def pick(both):
            return jnp.where(low_lanes, both[:LANES], both[LANES:])

        def question(q, c):
            at = self.q_rows(q)
            b1 = self.y3[at].astype(BF16)
            right[at, B1:B1 + 768] = b1
            self.up[...] = nt(b1, self.self_out[...]).astype(BF16)
            for p in range(6):
                lo = p * LANES
                pair = slice(lo, lo + LANES)
                q2, k2, v2 = (right[at, QKV + 768 * i + lo:QKV + 768 * i + lo + LANES] for i in range(3))
                keys = stacked(k2, m0, m1)
                probs = self.self_probs(q2, keys, p, allowed)
                up = self.up[:, pair]
                dval = pick(tn(probs.astype(BF16), up))
                ds = pair_pull(probs, nt(up, stacked(v2, m0, m1)))
                self.dbias[p] += ds.astype(F32)
                right[at, QKV + lo:QKV + lo + LANES] = nn(ds, keys).astype(BF16)
                right[at, QKV + 768 + lo:QKV + 768 + lo + LANES] = pick(tn(ds, q2)).astype(BF16)
                right[at, QKV + 1536 + lo:QKV + 1536 + lo + LANES] = dval.astype(BF16)
                if p == 2:
                    self.advance(16 + 2 * q)
            tok = self.tokens[at].astype(F32)
            back, gain = norm_pull(tok, self.gains[0:1], nt(right[at, QKV:QKV + 2304], self.self_qkv[...]))
            self.dgains[0:1] += gain
            self.grad_tokens[at] = (self.y3[at] + back).astype(BF16)
            self.put_left(L_H1, q, normed(tok, self.gains[0:1]))
            self.put_left(L_O, q, self.att[at])
            self.advance(17 + 2 * q)
            return c
        lax.fori_loop(0, 4, question, 0)
        for copy in self.stores()[1:]:
            copy.start()

    def bias_rows(self):
        row = lax.broadcasted_iota(jnp.int32, (LANES, LANES), 0)
        col = lax.broadcasted_iota(jnp.int32, (LANES, LANES), 1)
        flip = jnp.where(row + col == LANES - 1, 1.0, 0.0)
        out = []
        for p in range(6):
            turned = nn(flip, self.dbias[p], precision=lax.Precision.HIGHEST)
            for k in range(2):
                rolled = pltpu.roll(turned[:, k * LANES:(k + 1) * LANES], 0, 1, stride=1, stride_axis=0)
                out.append(jnp.sum(rolled, axis=0, keepdims=True))
        return out

    def spread_ids(self, width):
        slot = lax.broadcasted_iota(jnp.int32, (4 * MEM_PAD, width), 0)
        wanted = jnp.full((4 * MEM_PAD, width), -1, jnp.int32)
        for q in range(self.questions):
            for i in range(self.ids.shape[1]):
                wanted = jnp.where(slot == q * MEM_PAD + i, self.ids[q, i], wanted)
        return wanted

    def advance(self, t, fixed=None, right=None):
        left, value = self.place(t)
        if fixed is not None:
            left, value = fixed, right

        def product(parity):
            return nn(self.left[left, parity], value())
        self.reducer.step(t, product)

    def place(self, d):
        u = d - 16
        late = jnp.where(u < 4, 1 + u // 2, jnp.where(u < 8, 3, jnp.where(u < 10, 4, 5)))
        left = jnp.where(d < 16, L_R + (d - 8) // 2, late)
        col = pl.multiple_of(jnp.where(d < 16, E3 + lax.rem(d, 2) * 384, B2 + u * 384), LANES)
        return left, lambda: self.right[:, pl.ds(col, 384)]


MESH_ID = pl.DeviceIdType.MESH
CHUNK_ROWS, CHUNK_COLS, PAIR_ROWS, SMALL_ROWS = 96, 384, 48, 32
PERIOD, GAP, LAST_PAIR, SMALL_AT = 5, 31, 26, 33
CHUNKS = 32
DEPTH = Bunch(own=12, mid=8, snd=3, r0=3, rp=2, r1=4, r2=4, r3=4, r4=4)
LAG = Bunch(one=1, two=2, three=2, four=2, five=2, six=2)
TAIL = sum(vars(LAG).values())


def number_of(d):
    if d == CHUNKS - 1:
        return GAP + 1
    return d + PERIOD if d % PERIOD == 1 else d


class Reducer:
    def __init__(self, bufs, sems, out_ref):
        self.b, self.s, self.out = bufs, sems, out_ref
        dp, z = lax.axis_index("dp"), lax.axis_index("replica")
        here = Bunch(dp=dp, replica=z)
        self.core = lax.rem(dp, 2)
        self.x = lax.rem(dp // 2, 2)
        self.y = dp // 4
        self.inner = lax.rem((z + 1) // 2, 2) == 1
        self.end = lax.rem((z + 1) // 2, 2) == 0
        self.near = pl.multiple_of(PAIR_ROWS * lax.rem(z, 2), PAIR_ROWS)
        self.far = pl.multiple_of(PAIR_ROWS * (1 - lax.rem(z, 2)), PAIR_ROWS)
        self.to_core = dict(vars(here), dp=dp + 1 - 2 * self.core)
        self.to_x = dict(vars(here), dp=dp + 2 - 4 * self.x)
        self.to_y = dict(vars(here), dp=dp + 4 - 8 * self.y)
        self.to_pair = dict(vars(here), replica=z + 1 - 2 * lax.rem(z, 2))
        self.to_mid = dict(vars(here), replica=3 - z)

    def enter(self):
        bar = pltpu.get_barrier_semaphore()
        for target in (self.to_core, self.to_x, self.to_y, self.to_pair, self.to_mid):
            pl.semaphore_signal(bar, inc=1, device_id=target, device_id_type=MESH_ID)
        pl.semaphore_wait(bar, 5)

    def copy(self, src, dst, send, recv, target):
        return pltpu.make_async_remote_copy(
            src_ref=src, dst_ref=dst, send_sem=send, recv_sem=recv, device_id=target, device_id_type=MESH_ID)

    def core_copy(self, k, n):
        a, r, rows = lax.rem(k, DEPTH.snd), lax.rem(k, DEPTH.r0), pl.ds(0, n)
        return self.copy(self.b.snd.at[a, :, rows], self.b.r0.at[r, :, rows], self.s.snd.at[a], self.s.r0.at[r],
                         self.to_core)

    def pair_copy(self, d):
        o, r = lax.rem(d + PERIOD, DEPTH.own), lax.rem(d // PERIOD, DEPTH.rp)
        return self.copy(self.b.own.at[o, :, :, pl.ds(self.far, PAIR_ROWS)], self.b.rp.at[r], self.s.sp.at[r],
                         self.s.rp.at[r], self.to_pair)

    def first_copies(self, k, n, base):
        o, r = lax.rem(k, DEPTH.own), lax.rem(k, DEPTH.r1)
        half = n // 2
        low, high, into = pl.ds(base, half), pl.ds(base + half, half), pl.ds(0, half)
        return (
            self.copy(self.b.own.at[o, :, 1 - self.x, low], self.b.r1x.at[r, :, into], self.s.s1x.at[r],
                      self.s.r1x.at[r], self.to_x),
            self.copy(self.b.own.at[o, 1 - self.y, :, high], self.b.r1y.at[r, :, into], self.s.s1y.at[r],
                      self.s.r1y.at[r], self.to_y),
        )

    def second_copies(self, k, n, base):
        o, r = lax.rem(k, DEPTH.own), lax.rem(k, DEPTH.r2)
        half = n // 2
        low, high, into = pl.ds(base, half), pl.ds(base + half, half), pl.ds(0, half)
        return (
            self.copy(self.b.own.at[o, self.y, 1 - self.x, high], self.b.r2x.at[r, into], self.s.s2x.at[r],
                      self.s.r2x.at[r], self.to_x),
            self.copy(self.b.own.at[o, 1 - self.y, self.x, low], self.b.r2y.at[r, into], self.s.s2y.at[r],
                      self.s.r2y.at[r], self.to_y),
        )

    def mine(self, k, n, base=0):
        return self.b.mid.at[lax.rem(k, DEPTH.mid), pl.ds(base, n)]

    def inward_copy(self, k, n, base):
        r = lax.rem(k, DEPTH.r3)
        return self.copy(self.mine(k, n, base), self.b.r3.at[r, pl.ds(0, n)], self.s.s3.at[r], self.s.r3.at[r],
                         self.to_pair)

    def middle_copy(self, k, n):
        r = lax.rem(k, DEPTH.r4)
        return self.copy(self.mine(k, n), self.b.r4.at[r, pl.ds(0, n)], self.s.s4.at[r], self.s.r4.at[r], self.to_mid)

    def outward_copy(self, k, n):
        r = lax.rem(k, DEPTH.r4)
        return self.copy(self.mine(k, n), self.out.at[k, pl.ds(0, n)], self.s.s5.at[r], self.s.out.at[k], self.to_pair)

    def keep_copy(self, k, n):
        return pltpu.make_async_copy(self.mine(k, n), self.out.at[k, pl.ds(0, n)], self.s.out.at[k])

    def grant(self, sem, k, depth, target):
        @pl.when(k + depth <= SMALL_AT)
        def _():
            pl.semaphore_signal(sem, inc=1, device_id=target, device_id_type=MESH_ID)

    def need(self, sem, k, depth):
        @pl.when((k >= depth) & (k != depth + 1))
        def _():
            pl.semaphore_wait(sem, 1)

    def fill(self, t, half_product):
        n = CHUNK_ROWS
        early = (lax.rem(t, PERIOD) == 1) & (t <= LAST_PAIR)
        a, o = lax.rem(t, DEPTH.snd), lax.rem(jnp.where(early, t + PERIOD, t), DEPTH.own)

        @pl.when(t >= DEPTH.snd)
        def _():
            self.core_copy(t - DEPTH.snd, n).wait_send()

        away = half_product(1 - self.core)
        for g in range(4):
            self.b.snd[a, g] = away[g * n:(g + 1) * n]

        @pl.when(t >= DEPTH.r0)
        def _():
            pl.semaphore_wait(self.s.c0, 1)
        self.core_copy(t, n).start()
        here = half_product(self.core)
        for g in range(4):
            self.b.own[o, g // 2, g % 2] = here[g * n:(g + 1) * n]

    def fill_small(self, small):
        k, n = SMALL_AT, SMALL_ROWS
        a, o = k % DEPTH.snd, k % DEPTH.own
        self.core_copy(k - DEPTH.snd, CHUNK_ROWS).wait_send()
        for g in range(4):
            self.b.snd[a, g, 0:n, :] = small[1 - self.core, g]
            self.b.own[o, g // 2, g % 2, 0:n, :] = small[self.core, g]
        pl.semaphore_wait(self.s.c0, 1)
        self.core_copy(k, n).start()

    def add_core(self, d, o, n):
        r = lax.rem(d, DEPTH.r0)
        self.core_copy(d, n).wait_recv()
        for g in range(4):
            self.b.own[o, g // 2, g % 2, 0:n] += self.b.r0[r, g, 0:n]

        @pl.when((d + DEPTH.r0 <= SMALL_AT) & (d + DEPTH.r0 != GAP))
        def _():
            pl.semaphore_signal(self.s.c0, inc=1, device_id=self.to_core, device_id_type=MESH_ID)

    def start_first(self, k, n, base):
        self.need(self.s.c1x, k, DEPTH.r1)
        self.need(self.s.c1y, k, DEPTH.r1)
        for copy in self.first_copies(k, n, base):
            copy.start()

    def stage_one(self, k, n):
        self.add_core(k, lax.rem(k, DEPTH.own), n)
        self.start_first(k, n, 0)

    def stage_pair(self, d):
        self.add_core(d, lax.rem(d + PERIOD, DEPTH.own), CHUNK_ROWS)

        @pl.when(d // PERIOD >= DEPTH.rp)
        def _():
            pl.semaphore_wait(self.s.cp, 1)
        self.pair_copy(d).start()

    def stage_one_pair(self, k):
        d = k - PERIOD
        o, r = lax.rem(k, DEPTH.own), lax.rem(d // PERIOD, DEPTH.rp)
        self.pair_copy(d).wait()
        rows = pl.ds(self.near, PAIR_ROWS)
        for g in range(4):
            self.b.own[o, g // 2, g % 2, rows] += self.b.rp[r, g // 2, g % 2]

        @pl.when(d + DEPTH.rp * PERIOD <= LAST_PAIR)
        def _():
            pl.semaphore_signal(self.s.cp, inc=1, device_id=self.to_pair, device_id_type=MESH_ID)
        self.start_first(k, PAIR_ROWS, self.near)

    def stage_two(self, k, n, base):
        o, r, half = lax.rem(k, DEPTH.own), lax.rem(k, DEPTH.r1), n // 2
        low, high = pl.ds(base, half), pl.ds(base + half, half)
        by_x, by_y = self.first_copies(k, n, base)
        by_x.wait_recv()
        for g in range(2):
            self.b.own[o, g, self.x, low, :] += self.b.r1x[r, g, 0:half]
        by_y.wait_recv()
        for g in range(2):
            self.b.own[o, self.y, g, high, :] += self.b.r1y[r, g, 0:half]
        self.grant(self.s.c1x, k, DEPTH.r1, self.to_x)
        self.grant(self.s.c1y, k, DEPTH.r1, self.to_y)
        by_x.wait_send()
        by_y.wait_send()
        self.need(self.s.c2x, k, DEPTH.r2)
        self.need(self.s.c2y, k, DEPTH.r2)
        for copy in self.second_copies(k, n, base):
            copy.start()

    def stage_three(self, k, n, base):
        o, r, half = lax.rem(k, DEPTH.own), lax.rem(k, DEPTH.r2), n // 2
        low, high = pl.ds(base, half), pl.ds(base + half, half)
        m = lax.rem(k, DEPTH.mid)
        by_x, by_y = self.second_copies(k, n, base)
        by_x.wait_recv()
        self.b.mid[m, high, :] = self.b.own[o, self.y, self.x, high, :] + self.b.r2x[r, 0:half]
        by_y.wait_recv()
        self.b.mid[m, low, :] = self.b.own[o, self.y, self.x, low, :] + self.b.r2y[r, 0:half]
        self.grant(self.s.c2x, k, DEPTH.r2, self.to_x)
        self.grant(self.s.c2y, k, DEPTH.r2, self.to_y)
        by_x.wait_send()
        by_y.wait_send()

        @pl.when(self.end)
        def _():
            self.need(self.s.c3, k, DEPTH.r3)
            self.inward_copy(k, n, base).start()

    def stage_four(self, k, n, paired):
        r = lax.rem(k, DEPTH.r3)
        part = PAIR_ROWS if paired else n

        @pl.when(self.end)
        def _():
            self.inward_copy(k, part, self.near if paired else 0).wait_send()

        @pl.when(self.inner)
        def _():
            self.inward_copy(k, part, 0).wait_recv()
            if paired:
                self.b.mid[lax.rem(k, DEPTH.mid), pl.ds(self.far, part), :] = self.b.r3[r, 0:part]
            else:
                self.mine(k, n)[...] += self.b.r3[r, 0:n]
            self.grant(self.s.c3, k, DEPTH.r3, self.to_pair)
            self.need(self.s.c4, k, DEPTH.r4)
            self.middle_copy(k, n).start()

    def stage_five(self, k, n):
        r = lax.rem(k, DEPTH.r4)

        @pl.when(self.inner)
        def _():
            self.middle_copy(k, n).wait()
            self.mine(k, n)[...] += self.b.r4[r, 0:n]
            self.grant(self.s.c4, k, DEPTH.r4, self.to_mid)
            self.outward_copy(k, n).start()
            self.keep_copy(k, n).start()

    def stage_six(self, k, n):
        @pl.when(self.inner)
        def _():
            self.outward_copy(k, n).wait_send()
        self.keep_copy(k, n).wait()

    def move(self, t):
        n = CHUNK_ROWS
        stages = (
            (LAG.one, lambda k: self.stage_one(k, n), self.stage_one_pair, lambda k: self.stage_one(k, SMALL_ROWS)),
            (LAG.two, lambda k: self.stage_two(k, n, 0), lambda k: self.stage_two(k, PAIR_ROWS, self.near),
             lambda k: self.stage_two(k, SMALL_ROWS, 0)),
            (LAG.three, lambda k: self.stage_three(k, n, 0), lambda k: self.stage_three(k, PAIR_ROWS, self.near),
             lambda k: self.stage_three(k, SMALL_ROWS, 0)),
            (LAG.four, lambda k: self.stage_four(k, n, False), lambda k: self.stage_four(k, n, True),
             lambda k: self.stage_four(k, SMALL_ROWS, False)),
            (LAG.five, lambda k: self.stage_five(k, n), None, lambda k: self.stage_five(k, SMALL_ROWS)),
            (LAG.six, lambda k: self.stage_six(k, n), None, lambda k: self.stage_six(k, SMALL_ROWS)),
        )
        behind = TAIL
        for lag, usual, paired, small in reversed(stages):
            k = t - behind
            odd = lax.rem(k + PERIOD, PERIOD) == 1
            if paired is None:
                pl.when((k >= 0) & (k < SMALL_AT) & (k != 1))(functools.partial(usual, k))
            else:
                pl.when((k >= 0) & (k < SMALL_AT) & jnp.logical_not(odd))(functools.partial(usual, k))
                pl.when(odd & (k > 1) & (k < SMALL_AT))(functools.partial(paired, k))
            pl.when(k == SMALL_AT)(functools.partial(small, k))
            behind -= lag
        d = t - LAG.one
        pl.when((lax.rem(d + PERIOD, PERIOD) == 1) & (d >= 0) & (d <= LAST_PAIR))(functools.partial(self.stage_pair, d))

    def step(self, t, half_product):
        self.move(t)
        self.fill(t, half_product)

    def finish(self, small):
        self.move(SMALL_AT)
        self.fill_small(small)

        def body(t, c):
            self.move(t)
            return c
        lax.fori_loop(SMALL_AT + 1, SMALL_AT + 1 + TAIL, body, 0)
        self.core_copy(GAP - DEPTH.snd, CHUNK_ROWS).wait_send()
        self.core_copy(GAP + 1, CHUNK_ROWS).wait_send()
        self.core_copy(SMALL_AT, SMALL_ROWS).wait_send()


def reducer_scratch():
    rows, cols, half, count, d = CHUNK_ROWS, CHUNK_COLS, CHUNK_ROWS // 2, SMALL_AT + 1, DEPTH
    vmem = lambda *shape: pltpu.VMEM(shape, jnp.float32)
    dma = lambda n: pltpu.SemaphoreType.DMA((n,))
    plain = pltpu.SemaphoreType.REGULAR
    bufs = Bunch(
        own=vmem(d.own, 2, 2, rows, cols), mid=vmem(d.mid, rows, cols), snd=vmem(d.snd, 4, rows, cols),
        r0=vmem(d.r0, 4, rows, cols), rp=vmem(d.rp, 2, 2, PAIR_ROWS, cols), r1x=vmem(d.r1, 2, half, cols),
        r1y=vmem(d.r1, 2, half, cols), r2x=vmem(d.r2, half, cols), r2y=vmem(d.r2, half, cols),
        r3=vmem(d.r3, rows, cols), r4=vmem(d.r4, rows, cols))
    sems = Bunch(
        snd=dma(d.snd), r0=dma(d.r0), sp=dma(d.rp), rp=dma(d.rp), out=dma(count), s1x=dma(d.r1), r1x=dma(d.r1),
        s1y=dma(d.r1), r1y=dma(d.r1), s2x=dma(d.r2), r2x=dma(d.r2), s2y=dma(d.r2), r2y=dma(d.r2), s3=dma(d.r3),
        r3=dma(d.r3), s4=dma(d.r4), r4=dma(d.r4), s5=dma(d.r4), c0=plain, cp=plain, c1x=plain, c1y=plain, c2x=plain,
        c2y=plain, c3=plain, c4=plain)
    return bufs, sems


class PartWriter:
    def __init__(self, bufs, sems, out_ref):
        self.b, self.s, self.out = bufs, sems, out_ref

    def enter(self):
        pass

    def step(self, t, half_product):
        for parity in range(2):
            value = half_product(parity)
            for g in range(4):
                self.b.own[parity, g // 2, g % 2] = value[g * 96:(g + 1) * 96]
        copy = pltpu.make_async_copy(self.b.own, self.out.at[t], self.s.out.at[0])
        copy.start()
        copy.wait()


def regroup(groups, refs):
    result, first = [], 0
    for names in groups:
        result.append(Bunch(**dict(zip(names, refs[first:first + len(names)]))))
        first += len(names)
    return result


def layer_kernel(groups, alone, *refs):
    given, hbm, out, vm, load, store, bufs, sems = regroup(groups, refs)
    reducer = (PartWriter if alone else Reducer)(bufs, sems, out.chunks)
    layer = Layer(given, hbm, out, vm, load, store)
    layer.reducer = reducer
    layer.forward(reducer.enter)
    layer.feed_forward()
    layer.backward_cross()
    layer.backward_self()

    if alone:
        def body(t, c):
            layer.advance(t)
            return c
        lax.fori_loop(24, CHUNKS, body, 0)
        entries = vm.memory_keys.shape[0]
        entry = lax.broadcasted_iota(jnp.int32, (4 * MEM_PAD, entries), 1)
        hit = jnp.where(layer.spread_ids(entries) == entry, 1.0, 0.0)
        out.mem_k[...] = tn(hit, vm.dmem_k[...], precision=lax.Precision.HIGHEST)
        out.mem_v[...] = tn(hit, vm.dmem_v[...], precision=lax.Precision.HIGHEST)
        out.gains[...] = vm.dgains[...]
        for h, row in enumerate(layer.bias_rows()):
            out.bias[h:h + 1, :] = row
    else:
        fill_small_rows(layer, vm)

        def body(t, c):
            left, value = layer.place(jnp.where(t > GAP, CHUNKS - 1, t))
            reducer.move(t)

            @pl.when(t != GAP)
            def _():
                reducer.fill(t, lambda parity: nn(vm.left[left, parity], value()))
            return c
        lax.fori_loop(24, SMALL_AT, body, 0)
        reducer.finish(vm.small)
    for copy in layer.stores():
        copy.wait()


def fill_small_rows(layer, vm):
    out_row = lax.broadcasted_iota(jnp.int32, (4 * MEM_PAD, 64), 1)
    entry = 4 * (out_row // 8) + lax.rem(out_row, 4)
    same = layer.spread_ids(64) == entry
    keys_row = lax.rem(out_row // 4, 2) == 0
    hit_k = jnp.where(same & keys_row, 1.0, 0.0)
    hit_v = jnp.where(same & jnp.logical_not(keys_row), 1.0, 0.0)
    memory = (tn(hit_k, vm.dmem_k[...], precision=lax.Precision.HIGHEST)
              + tn(hit_v, vm.dmem_v[...], precision=lax.Precision.HIGHEST))
    bias = jnp.concatenate(layer.bias_rows() + [jnp.zeros((4, LANES), F32)], axis=0)
    gains = jnp.concatenate([vm.dgains[...], jnp.zeros((5, 768), F32)], axis=0)
    for b in range(8):
        block = vm.small.at[b % 2, b // 2]
        for j in range(6):
            row, col = 8 * (j % 4), LANES * (j // 4)
            block[row:row + 8, col:col + LANES] = memory[8 * b:8 * b + 8, j * LANES:(j + 1) * LANES]
        turned = gains if b == 0 else pltpu.roll(gains, 768 - 96 * b, 1)
        block[16:24, LANES:2 * LANES] = turned[:, :LANES]
        block[24:32, LANES:2 * LANES] = jnp.zeros((8, LANES), F32)
        block[0:16, 2 * LANES:] = bias
        block[16:32, 2 * LANES:] = jnp.zeros((16, LANES), F32)


def call_grouped(kernel, ins, outs, scratch, **options):
    groups = [list(vars(g)) for g in ins + outs + scratch]
    pairs = lambda gs, i: [v[i] for g in gs for v in vars(g).values()]
    space = lambda gs: [pl.BlockSpec(memory_space=s) for s in pairs(gs, 1)]
    result = pl.pallas_call(
        functools.partial(kernel, groups), out_shape=pairs(outs, 0), in_specs=space(ins), out_specs=space(outs),
        scratch_shapes=[v for g in scratch for v in vars(g).values()], **options)(*pairs(ins, 0))
    return regroup(groups[len(ins):len(ins) + len(outs)], result)[0]


def in_space(space, **values):
    return Bunch(**{name: (value, space) for name, value in values.items()})


def run_layer(alone, hbm, given, tables):
    rows, width = hbm.tokens.shape
    enc_rows = hbm.encodings.shape[0]
    entries = hbm.memory_keys.shape[0]
    shape = jax.ShapeDtypeStruct
    outs = in_space(pl.ANY, layer_output=shape((rows, width), BF16), grad_tokens=shape((rows, width), BF16),
                    grad_encodings=shape((enc_rows, width), BF16))
    if alone:
        part = shape((entries, width), F32)
        vars(outs).update(vars(in_space(pl.ANY, chunks=shape((CHUNKS, 2, 2, 2, CHUNK_ROWS, CHUNK_COLS), F32))))
        vars(outs).update(vars(in_space(pltpu.VMEM, mem_k=part, mem_v=part, gains=shape((3, width), F32),
                                        bias=shape((12, LANES), F32))))
    else:
        vars(outs).update(vars(in_space(pl.ANY, chunks=shape((SMALL_AT + 1, CHUNK_ROWS, CHUNK_COLS), F32))))
    loaded = [name for name in vars(hbm) if vars(hbm)[name] is not hbm.ff_in and vars(hbm)[name] is not hbm.ff_out]
    vm = Bunch(**{name: pltpu.VMEM(vars(hbm)[name].shape, BF16) for name in loaded})
    big = lambda cols, kind: pltpu.VMEM((rows, cols), kind)
    vars(vm).update(
        wi=pltpu.VMEM((2, width, FF_TILE), BF16), wo=pltpu.VMEM((2, FF_TILE, width), BF16),
        hid=big(width, BF16), att=big(width, BF16), att2=big(width, BF16), right=big(RIGHT, BF16),
        left=pltpu.VMEM((10, 2, 384, rows), BF16),
        y1=big(width, F32), y2=big(width, F32), y3=big(width, F32), dh3=big(width, F32),
        z=big(FF_TILE, F32), dr=big(FF_TILE, F32), act=big(FF_TILE, BF16), dz=big(FF_TILE, BF16),
        bias=pltpu.VMEM((6, LANES, 2 * LANES), F32), dbias=pltpu.VMEM((6, LANES, 2 * LANES), F32),
        gains=pltpu.VMEM((3, width), F32), dgains=pltpu.VMEM((3, width), F32), up=pltpu.VMEM((LANES, width), BF16),
        mem_k=pltpu.VMEM((4, MEM_PAD, width), BF16), mem_v=pltpu.VMEM((4, MEM_PAD, width), BF16),
        dmem_k=pltpu.VMEM((4 * MEM_PAD, width), F32), dmem_v=pltpu.VMEM((4 * MEM_PAD, width), F32),
        layer_output=big(width, BF16), grad_tokens=big(width, BF16), grad_encodings=pltpu.VMEM((enc_rows, width), BF16),
        wi_sem=pltpu.SemaphoreType.DMA((2,)), wo_sem=pltpu.SemaphoreType.DMA((2,)))
    one = pltpu.SemaphoreType.DMA
    load = Bunch(**{name: one for name in loaded})
    store = Bunch(layer_output=one, grad_tokens=one, grad_encodings=one)
    bufs, sems = reducer_scratch()
    extra = dict(collective_id=0)
    if alone:
        bufs, sems = Bunch(own=pltpu.VMEM((2, 2, 2, CHUNK_ROWS, CHUNK_COLS), F32)), Bunch(out=pltpu.SemaphoreType.DMA((1,)))
        extra = {}
    else:
        vm.small = pltpu.VMEM((2, 4, SMALL_ROWS, CHUNK_COLS), F32)
    ins = [Bunch(**vars(in_space(pltpu.SMEM, lengths=given.lengths, ids=given.ids)),
                 **vars(in_space(pltpu.VMEM, gain_self=given.gain_self, gain_cross=given.gain_cross,
                                 gain_ff=given.gain_ff, rel_bias=given.rel_bias, tables=tables))),
           in_space(pl.ANY, **vars(hbm))]
    return call_grouped(
        lambda groups, *refs: layer_kernel(groups, alone, *refs), ins, [outs], [vm, load, store, bufs, sems],
        compiler_params=pltpu.CompilerParams(has_side_effects=True, vmem_limit_bytes=62 * 2**20, **extra),
        cost_estimate=pl.CostEstimate(flops=30 * 10**9, bytes_accessed=35 * 10**6, transcendentals=5 * 10**6))


FF_IN_AT, FF_OUT_AT, CROSS_OUT_AT, CROSS_Q_AT, CROSS_KV_AT, SELF_OUT_AT, SELF_QKV_AT = 0, 8, 16, 18, 20, 24, 26


def place_kernel(groups, *refs):
    given, tables, out, vm = regroup(groups, refs)
    slots = vm.sem
    chunk_in = lambda k: pltpu.make_async_copy(given.chunks.at[k], vm.chunks.at[k], slots.at[k])
    through = [(given.layer_output, vm.a, out.layer_output), (given.grad_tokens, vm.b, out.grad_tokens),
               (given.grad_encodings, vm.c, out.grad_encodings)]
    order = [SMALL_AT] + [number_of(d) for d in range(CHUNKS)]
    for k in order:
        chunk_in(k).start()
    for n, (src, mid, _) in enumerate(through):
        pltpu.make_async_copy(src, mid, slots.at[SMALL_AT + 1 + n]).start()
    made = []

    def send(src, dst):
        copy = pltpu.make_async_copy(src, dst, slots.at[SMALL_AT + 4 + len(made)])
        copy.start()
        made.append(copy)

    chunk_in(SMALL_AT).wait()
    small = vm.chunks[SMALL_AT, 0:SMALL_ROWS, :]
    for j in range(6):
        row, col = 8 * (j % 4), LANES * (j // 4)
        out.mem_k[:, j * LANES:(j + 1) * LANES] = small[row:row + 4, col:col + LANES]
        out.mem_v[:, j * LANES:(j + 1) * LANES] = small[row + 4:row + 8, col:col + LANES]
    for n, gain in enumerate((out.gain_self, out.gain_cross, out.gain_ff)):
        gain[...] = small[16 + n, LANES:LANES + 96]
    out.rel_bias[...] = nt(small[0:16, 2 * LANES:], tables.tables[1], precision=lax.Precision.HIGHEST)[0:12]
    pieces = ((out.ff_in, FF_IN_AT), (out.cross_out, CROSS_OUT_AT), (out.cross_q, CROSS_Q_AT),
              (out.cross_kv, CROSS_KV_AT), (out.self_out, SELF_OUT_AT), (out.self_qkv, SELF_QKV_AT))
    target = {}
    for ref, first in pieces:
        for k in range(ref.shape[1] // 384):
            target[first + k] = (ref, slice(0, 96), k * 384)
    for k in range(8):
        target[FF_OUT_AT + k] = (out.ff_out, slice((k // 2) * 96, (k // 2) * 96 + 96), (k % 2) * 384)
    for d in range(CHUNKS):
        k = number_of(d)
        chunk_in(k).wait()
        ref, at, col = target[d]
        send(vm.chunks.at[k], ref.at[at, col:col + CHUNK_COLS])
    for n, (src, mid, dst) in enumerate(through):
        pltpu.make_async_copy(src, mid, slots.at[SMALL_AT + 1 + n]).wait()
        send(mid, dst)
    for copy in made:
        copy.wait()


def place(done, tables):
    shape = jax.ShapeDtypeStruct
    outs = in_space(
        pl.ANY, layer_output=shape(done.layer_output.shape, BF16), grad_tokens=shape(done.grad_tokens.shape, BF16),
        grad_encodings=shape(done.grad_encodings.shape, BF16), ff_in=shape((96, 3072), F32), ff_out=shape((384, 768), F32),
        cross_out=shape((96, 768), F32), cross_q=shape((96, 768), F32), cross_kv=shape((96, 1536), F32),
        self_out=shape((96, 768), F32), self_qkv=shape((96, 2304), F32))
    gain = shape((96,), F32)
    vars(outs).update(vars(in_space(
        pltpu.VMEM, mem_k=shape((4, 768), F32), mem_v=shape((4, 768), F32), gain_self=gain, gain_cross=gain,
        gain_ff=gain, rel_bias=shape((12, 32), F32))))
    scratch = Bunch(
        chunks=pltpu.VMEM(done.chunks.shape, F32), a=pltpu.VMEM(done.layer_output.shape, BF16),
        b=pltpu.VMEM(done.grad_tokens.shape, BF16), c=pltpu.VMEM(done.grad_encodings.shape, BF16),
        sem=pltpu.SemaphoreType.DMA((SMALL_AT + 4 + CHUNKS + 3,)))
    return call_grouped(
        place_kernel, [in_space(pl.ANY, **vars(done)), in_space(pltpu.VMEM, tables=tables)], [outs], [scratch],
        compiler_params=pltpu.CompilerParams(vmem_limit_bytes=62 * 2**20),
        cost_estimate=pl.CostEstimate(flops=0, bytes_accessed=15 * 10**6, transcendentals=0))


def sum_alone(done, tables):
    chunks = done.chunks.transpose(0, 2, 3, 1, 4, 5).reshape(CHUNKS, 768, CHUNK_COLS)

    def whole(first, cols):
        part = chunks[first:first + cols // 384]
        return part.transpose(1, 0, 2).reshape(768, cols)

    ff_out = chunks[8:16].reshape(4, 2, 8, 96, CHUNK_COLS)
    parts = Bunch(
        ff_in=whole(FF_IN_AT, 3072), ff_out=ff_out.transpose(2, 0, 3, 1, 4).reshape(3072, 768),
        cross_out=whole(CROSS_OUT_AT, 768), cross_q=whole(CROSS_Q_AT, 768), cross_kv=whole(CROSS_KV_AT, 1536),
        self_out=whole(SELF_OUT_AT, 768), self_qkv=whole(SELF_QKV_AT, 2304), mem_k=done.mem_k, mem_v=done.mem_v,
        gain_self=done.gains[0], gain_cross=done.gains[1], gain_ff=done.gains[2])
    out = Bunch(**{name: lax.psum(lax.psum_scatter(value, "dp", scatter_dimension=0, tiled=True), "replica")
                   for name, value in vars(parts).items()})
    bias = lax.psum(done.bias, ("dp", "replica"))
    out.rel_bias = lax.dot_general(bias, tables[1], (((1,), (1,)), ((), ())), precision=lax.Precision.HIGHEST)
    out.layer_output, out.grad_tokens, out.grad_encodings = done.layer_output, done.grad_tokens, done.grad_encodings
    return out


def on_device(tokens, encodings, lengths, memory_ids, memory_keys, memory_values, gain_self, gain_cross, gain_ff,
              rel_bias, self_qkv, self_out, cross_q, cross_kv, cross_out, ff_in, ff_out, cotangent):
    width = tokens.shape[-1]
    alone = not (lax.axis_size("dp") == 8 and lax.axis_size("replica") == 4)
    hbm = Bunch(tokens=tokens.reshape(-1, width), encodings=encodings.reshape(-1, width),
                cotangent=cotangent.reshape(-1, width), memory_keys=memory_keys, memory_values=memory_values,
                self_qkv=self_qkv, self_out=self_out, cross_q=cross_q, cross_kv=cross_kv, cross_out=cross_out,
                ff_in=ff_in, ff_out=ff_out)
    given = Bunch(lengths=lengths, ids=memory_ids, gain_self=gain_self, gain_cross=gain_cross, gain_ff=gain_ff,
                  rel_bias=rel_bias.T)
    tables = jnp.asarray(bucket_tables(LANES, rel_bias.shape[0]))
    done = run_layer(alone, hbm, given, tables)
    out = sum_alone(done, tables) if alone else place(done, tables)
    return (
        out.layer_output.reshape(tokens.shape), out.grad_tokens.reshape(tokens.shape),
        out.grad_encodings.reshape(encodings.shape), out.gain_self, out.gain_cross, out.gain_ff, out.rel_bias.T,
        out.self_qkv, out.self_out, out.cross_q, out.cross_kv, out.cross_out, out.ff_in, out.ff_out, out.mem_k,
        out.mem_v)


def solution(mesh):
    split, whole = P(("dp", "replica")), P()
    return jax.shard_map(
        on_device,
        mesh=mesh,
        in_specs=(split,) * 4 + (whole,) * 13 + (split,),
        out_specs=(split,) * 3 + (P("dp"),) * 3 + (whole,) + (P("dp"),) * 9,
        check_vma=False,
    )
```

```python
import functools
import itertools
from types import SimpleNamespace as Bunch

import jax
import jax.numpy as jnp
import numpy as np
from jax import lax
from jax.experimental import pallas as pl
from jax.experimental.pallas import tpu as pltpu
from jax.sharding import PartitionSpec as P

F32, BF16 = jnp.float32, jnp.bfloat16
EPSILON = 1e-06
NEGATIVE = -1000000000.0
MAXDIST = 128
LANES = 128
E3, B2, CQ, EKV, B1, QKV, RIGHT = 0, 768, 1536, 2304, 3840, 4608, 6912
L_H3, L_O2, L_H2, L_ENC, L_O, L_H1, L_R = 0, 1, 2, 3, 4, 5, 6
FF_TILE = 384
MEM_PAD = 16


def nn(a, b, **kw):
    return lax.dot_general(a, b, (((1,), (0,)), ((), ())), preferred_element_type=F32, **kw)


def nt(a, b, **kw):
    return lax.dot_general(a, b, (((1,), (1,)), ((), ())), preferred_element_type=F32, **kw)


def tn(a, b, **kw):
    return lax.dot_general(a, b, (((0,), (0,)), ((), ())), preferred_element_type=F32, **kw)


def bucket_of(apart, buckets, distance):
    exact = buckets // 2
    spread = np.log(np.maximum(apart, 1) / exact) / np.log(distance / exact) * (buckets - exact)
    larger = np.minimum(exact + np.floor(np.maximum(spread, 0.0)).astype(np.int64), buckets - 1)
    return np.where(apart < exact, apart, larger).astype(np.int32)


def bucket_tables(length, buckets):
    lane = np.arange(length)
    spread = [bucket_of((length - lane) % length, buckets, MAXDIST), bucket_of(length - 1 - lane, buckets, MAXDIST)]
    return np.stack([(np.arange(buckets)[:, None] == row[None]).astype(np.float32) for row in spread])


def root_scale(v):
    return lax.rsqrt(jnp.mean(v * v, axis=-1, keepdims=True) + EPSILON)


def normed(v, gain):
    return (v * root_scale(v) * gain).astype(BF16)


def norm_pull(v, gain, w):
    scale = root_scale(v)
    gw = w * gain
    back = scale * gw - v * (scale * scale * scale) * jnp.mean(gw * v, axis=-1, keepdims=True)
    return back, jnp.sum(w * v * scale, axis=0, keepdims=True)


def head_masks():
    lane = lax.broadcasted_iota(jnp.int32, (1, LANES), 1)
    first = jnp.where(lane < LANES // 2, 1.0, 0.0)
    return first.astype(BF16), (1.0 - first).astype(BF16), first > 0.5


def stacked(rows, m0, m1):
    return jnp.concatenate([rows * m0, rows * m1], axis=0)


def pair_softmax(s):
    parts = []
    for part in (s[:, :LANES], s[:, LANES:]):
        e = jnp.exp(part - jnp.max(part, axis=-1, keepdims=True))
        parts.append(e * (1.0 / jnp.sum(e, axis=-1, keepdims=True)))
    return jnp.concatenate(parts, axis=1)


def pair_pull(p, dp):
    parts = []
    for lo in (0, LANES):
        a, b = p[:, lo:lo + LANES], dp[:, lo:lo + LANES]
        parts.append((a * (b - jnp.sum(a * b, axis=-1, keepdims=True))).astype(BF16))
    return jnp.concatenate(parts, axis=1)


class Layer:
    def __init__(self, given, hbm, out, vm, load, store):
        vars(self).update(vars(given))
        vars(self).update(vars(vm))
        self.hbm, self.out, self.store = hbm, out, store
        self.layer_output, self.grad_tokens = vm.cotangent, vm.att2
        self.questions, self.length, self.enc_len = 4, 128, 64
        self.rows = self.questions * self.length
        self.load = Bunch(**{name: pltpu.make_async_copy(vars(hbm)[name], vars(vm)[name], sem)
                             for name, sem in vars(load).items()})

    def ff_loads(self, j):
        slot = lax.rem(j, 2)
        at = pl.ds(pl.multiple_of(j * FF_TILE, FF_TILE), FF_TILE)
        return (
            pltpu.make_async_copy(self.hbm.ff_in.at[:, at], self.wi.at[slot], self.wi_sem.at[slot]),
            pltpu.make_async_copy(self.hbm.ff_out.at[at, :], self.wo.at[slot], self.wo_sem.at[slot]),
        )

    def q_rows(self, q, n=128):
        return pl.ds(pl.multiple_of(q * n, n), n)

    def put_left(self, index, q, rows):
        turned = rows.T
        width = turned.shape[1]
        at = self.q_rows(q, width)
        for b in range(8):
            self.left[index, b % 2, (b // 2) * 96:(b // 2 + 1) * 96, at] = turned[b * 96:(b + 1) * 96]

    def bias_tables(self):
        table = nn(self.rel_bias[...], self.tables[0], precision=lax.Precision.HIGHEST)
        for p in range(6):
            for k in range(2):
                row = table[2 * p + k:2 * p + k + 1, :]
                self.bias[p, :, k * LANES:(k + 1) * LANES] = pltpu.roll(
                    jnp.broadcast_to(row, (LANES, LANES)), 0, 1, stride=1, stride_axis=0)

    def memory_rows(self):
        entries = self.memory_keys.shape[0]
        slot = lax.broadcasted_iota(jnp.int32, (MEM_PAD, entries), 0)
        entry = lax.broadcasted_iota(jnp.int32, (MEM_PAD, entries), 1)
        for q in range(self.questions):
            wanted = jnp.full((MEM_PAD, entries), -1, jnp.int32)
            for i in range(self.ids.shape[1]):
                wanted = jnp.where(slot == i, self.ids[q, i], wanted)
            pick = jnp.where(wanted == entry, 1.0, 0.0).astype(BF16)
            self.mem_k[q] = nn(pick, self.memory_keys[...]).astype(BF16)
            self.mem_v[q] = nn(pick, self.memory_values[...]).astype(BF16)

    def causal(self):
        row = lax.broadcasted_iota(jnp.int32, (LANES, 2 * LANES), 0)
        col = lax.rem(lax.broadcasted_iota(jnp.int32, (LANES, 2 * LANES), 1), LANES)
        return col <= row

    def self_probs(self, q2, k2, p, allowed):
        return pair_softmax(jnp.where(allowed, nt(q2, k2) + self.bias[p], NEGATIVE))

    def cross_probs(self, q2, k2, present):
        return pair_softmax(jnp.where(present, nt(q2, k2), -1e30))

    def present(self):
        col = lax.rem(lax.broadcasted_iota(jnp.int32, (1, 2 * LANES), 1), LANES)
        return col < self.enc_len + self.ids.shape[1]

    def cross_side(self, q, p, memory, base):
        enc = self.right[self.q_rows(q, self.enc_len), base + p * LANES:base + (p + 1) * LANES]
        mem = memory[q, :, p * LANES:(p + 1) * LANES]
        return jnp.concatenate([enc, mem, jnp.zeros((LANES - 64 - MEM_PAD, LANES), BF16)], axis=0)

    def forward(self, enter):
        load = self.load
        for copy in (load.tokens, load.self_qkv, load.encodings, load.cross_kv):
            copy.start()
        enter()
        for n, gain in enumerate((self.gain_self, self.gain_cross, self.gain_ff)):
            self.gains[n:n + 1, :] = gain[...].reshape(1, gain.shape[0])
        right = self.right
        self.bias_tables()
        self.load.tokens.wait()

        def norm_one(q, c):
            at = self.q_rows(q)
            self.hid[at] = normed(self.tokens[at].astype(F32), self.gains[0:1])
            return c
        lax.fori_loop(0, 4, norm_one, 0, unroll=4)
        self.load.self_qkv.wait()
        for copy in (load.memory_keys, load.memory_values, load.self_out, load.cross_q, load.cross_out, load.cotangent):
            copy.start()
        for copy in self.ff_loads(0) + self.ff_loads(1):
            copy.start()

        def qkv_tile(j, c):
            at = self.q_rows(j, 768)
            right[:, pl.ds(pl.multiple_of(QKV + j * 768, 768), 768)] = nn(self.hid[...], self.self_qkv[:, at]).astype(BF16)
            return c
        lax.fori_loop(0, 3, qkv_tile, 0, unroll=3)

        self.load.encodings.wait()
        self.load.cross_kv.wait()
        enc_rows = self.questions * self.enc_len

        def ekv_tile(j, c):
            at = self.q_rows(j, 768)
            col = pl.ds(pl.multiple_of(EKV + j * 768, 768), 768)
            right[0:enc_rows, col] = nn(self.encodings[...], self.cross_kv[:, at]).astype(BF16)
            return c
        lax.fori_loop(0, 2, ekv_tile, 0, unroll=2)
        self.load.memory_keys.wait()
        self.load.memory_values.wait()
        self.memory_rows()
        m0, m1, _ = head_masks()
        allowed = self.causal()

        def self_attention(q, c):
            at = self.q_rows(q)
            for p in range(6):
                lo = p * LANES
                q2, k2, v2 = (right[at, QKV + 768 * i + lo:QKV + 768 * i + lo + LANES] for i in range(3))
                probs = self.self_probs(q2, stacked(k2, m0, m1), p, allowed).astype(BF16)
                self.att[at, lo:lo + LANES] = nn(probs, stacked(v2, m0, m1)).astype(BF16)
            return c
        lax.fori_loop(0, 4, self_attention, 0, unroll=4)

        self.load.self_out.wait()

        def out_tile(j, c):
            at = self.q_rows(j, 768)
            self.y1[:, at] = self.tokens[:, at].astype(F32) + nn(self.att[...], self.self_out[:, at])
            return c
        lax.fori_loop(0, 1, out_tile, 0, unroll=1)

        def norm_two(q, c):
            at = self.q_rows(q)
            self.hid[at] = normed(self.y1[at], self.gains[1:2])
            return c
        lax.fori_loop(0, 4, norm_two, 0, unroll=4)
        self.load.cross_q.wait()

        def cq_tile(j, c):
            at = self.q_rows(j, 768)
            right[:, pl.ds(pl.multiple_of(CQ + j * 768, 768), 768)] = nn(self.hid[...], self.cross_q[:, at]).astype(BF16)
            return c
        lax.fori_loop(0, 1, cq_tile, 0, unroll=1)
        present = self.present()

        def cross_attention(q, c):
            at = self.q_rows(q)
            for p in range(6):
                lo = p * LANES
                keys = self.cross_side(q, p, self.mem_k, EKV)
                vals = self.cross_side(q, p, self.mem_v, EKV + 768)
                probs = self.cross_probs(right[at, CQ + lo:CQ + lo + LANES], stacked(keys, m0, m1), present)
                self.att2[at, lo:lo + LANES] = nn(probs.astype(BF16), stacked(vals, m0, m1)).astype(BF16)
            return c
        lax.fori_loop(0, 4, cross_attention, 0, unroll=4)
        self.load.cross_out.wait()

        def out2_tile(j, c):
            at = self.q_rows(j, 768)
            self.y2[:, at] = self.y1[:, at] + nn(self.att2[...], self.cross_out[:, at])
            return c
        lax.fori_loop(0, 1, out2_tile, 0, unroll=1)
        self.load.cotangent.wait()

        def norm_three(q, c):
            at = self.q_rows(q)
            h3 = normed(self.y2[at], self.gains[2:3])
            self.hid[at] = h3
            self.put_left(L_H3, q, h3)
            valid = lax.broadcasted_iota(jnp.int32, (LANES, 1), 0) < self.lengths[q]
            cot = jnp.where(valid, self.cotangent[at].astype(F32), 0.0)
            right[at, E3:E3 + 768] = cot.astype(BF16)
            return c
        lax.fori_loop(0, 4, norm_three, 0, unroll=4)

    def feed_forward(self):
        right = self.right
        self.y3[...] = self.y2[...]
        self.dh3[...] = jnp.zeros_like(self.dh3)

        def tile(j, c):
            slot = lax.rem(j, 2)
            for copy in self.ff_loads(j):
                copy.wait()
            for i in range(0, self.rows, 256):
                at = slice(i, i + 256)
                z = nn(self.hid[at], self.wi[slot])
                dr = nt(right[at, E3:E3 + 768], self.wo[slot]).astype(BF16).astype(F32)
                cdf = 0.5 * (1.0 + lax.erf(z * 0.7071067811865476))
                pdf = jnp.exp(-0.5 * z * z) * 0.3989422804014327
                self.act[at] = (z * cdf).astype(BF16)
                self.dz[at] = (dr * (cdf + z * pdf)).astype(BF16)
            act = self.act[...]
            dz = self.dz[...]

            self.advance(j, 0, lambda: dz)
            turned = act.T
            for g in range(4):
                at = pl.ds(pl.multiple_of((j // 2) * 96, 96), 96)
                self.left[L_R + g, lax.rem(j, 2), at, :] = turned[g * 96:(g + 1) * 96]
            self.y3[...] += nn(act, self.wo[slot])
            self.dh3[...] += nt(dz, self.wi[slot])

            @pl.when(j + 2 < 8)
            def _():
                for copy in self.ff_loads(j + 2):
                    copy.start()
            return c
        lax.fori_loop(0, 8, tile, 0)

        def finish(q, c):
            at = self.q_rows(q)
            valid = lax.broadcasted_iota(jnp.int32, (LANES, 1), 0) < self.lengths[q]
            self.layer_output[at] = jnp.where(valid, self.y3[at], 0.0).astype(BF16)
            return c
        lax.fori_loop(0, 4, finish, 0, unroll=4)
        self.stores()[0].start()

    def stores(self):
        return [pltpu.make_async_copy(vars(self)[name], vars(self.out)[name], sem) for name, sem in vars(self.store).items()]

    def put_lefts(self, index, rows):
        turned = rows.T
        for b in range(8):
            self.left[index, b % 2, (b // 2) * 96:(b // 2 + 1) * 96, 0:rows.shape[0]] = turned[b * 96:(b + 1) * 96]

    def row_blocks(self):
        return [slice(q * LANES, (q + 1) * LANES) for q in range(self.questions)]

    def in_steps(self, first, parts):
        count = sum(n for n, _ in parts)

        def step(i, c):
            at = 0
            for n, part in parts:
                pl.when((i >= at) & (i < at + n))(functools.partial(part, i - at))
                at += n
            self.advance(first + i)
            return c
        lax.fori_loop(0, count, step, 0)

    def backward_cross(self):
        right = self.right
        m0, m1, low_lanes = head_masks()
        present = self.present()
        enc_rows = self.questions * self.enc_len

        def pick(both):
            return jnp.where(low_lanes, both[:LANES], both[LANES:])

        def before(_):
            total = jnp.zeros((1, 768), F32)
            for at in self.row_blocks():
                back, gain = norm_pull(self.y2[at], self.gains[2:3], self.dh3[at])
                total += gain
                e2 = right[at, E3:E3 + 768].astype(F32) + back
                self.y3[at] = e2
                right[at, B2:B2 + 768] = e2.astype(BF16)
            self.dgains[2:3] = total
            self.up[...] = nt(right[:, B2:B2 + 768], self.cross_out[...]).astype(BF16)

        def attention(q):
            at = self.q_rows(q)
            enc_at = self.q_rows(q, self.enc_len)
            mem_at = self.q_rows(q, MEM_PAD)
            for p in range(6):
                lo = p * LANES
                pair = slice(lo, lo + LANES)
                keys = stacked(self.cross_side(q, p, self.mem_k, EKV), m0, m1)
                vals = stacked(self.cross_side(q, p, self.mem_v, EKV + 768), m0, m1)
                cq = right[at, CQ + lo:CQ + lo + LANES]
                probs = self.cross_probs(cq, keys, present)
                up = self.up[at, pair]
                dvals = pick(tn(probs.astype(BF16), up))
                ds = pair_pull(probs, nt(up, vals))
                dkeys = pick(tn(ds, cq))
                right[at, CQ + lo:CQ + lo + LANES] = nn(ds, keys).astype(BF16)
                right[enc_at, EKV + lo:EKV + lo + LANES] = dkeys[:64].astype(BF16)
                right[enc_at, EKV + 768 + lo:EKV + 768 + lo + LANES] = dvals[:64].astype(BF16)
                self.dmem_k[mem_at, pair] = dkeys[64:64 + MEM_PAD]
                self.dmem_v[mem_at, pair] = dvals[64:64 + MEM_PAD]

        def after(_):
            self.dh3[...] = nt(right[:, CQ:CQ + 768], self.cross_q[...])
            total = jnp.zeros((1, 768), F32)
            for at in self.row_blocks():
                back, gain = norm_pull(self.y1[at], self.gains[1:2], self.dh3[at])
                total += gain
                self.y3[at] += back
            self.dgains[1:2] = total

        def turn(_):
            for at in self.row_blocks():
                self.hid[at] = normed(self.y1[at], self.gains[1:2])
            self.put_lefts(L_H2, self.hid[...])
            self.put_lefts(L_O2, self.att2[...])

        def encodings(_):
            self.put_lefts(L_ENC, self.encodings[...])
            self.left[L_ENC, :, :, enc_rows:] = jnp.zeros((2, 384, self.rows - enc_rows), BF16)
            right[enc_rows:, EKV:EKV + 1536] = jnp.zeros((self.rows - enc_rows, 1536), BF16)
            self.grad_encodings[...] = nt(right[0:enc_rows, EKV:EKV + 1536], self.cross_kv[...]).astype(BF16)

        self.in_steps(8, ((1, before), (4, attention), (1, after), (1, turn), (1, encodings)))

    def backward_self(self):
        right = self.right
        m0, m1, low_lanes = head_masks()
        allowed = self.causal()

        def pick(both):
            return jnp.where(low_lanes, both[:LANES], both[LANES:])

        def before(_):
            self.dbias[...] = jnp.zeros_like(self.dbias)
            right[:, B1:B1 + 768] = self.y3[...].astype(BF16)
            self.up[...] = nt(right[:, B1:B1 + 768], self.self_out[...]).astype(BF16)

        def attention(q):
            at = self.q_rows(q)
            for p in range(6):
                lo = p * LANES
                q2, k2, v2 = (right[at, QKV + 768 * i + lo:QKV + 768 * i + lo + LANES] for i in range(3))
                keys = stacked(k2, m0, m1)
                probs = self.self_probs(q2, keys, p, allowed)
                up = self.up[at, lo:lo + LANES]
                dval = pick(tn(probs.astype(BF16), up))
                ds = pair_pull(probs, nt(up, stacked(v2, m0, m1)))
                self.dbias[p] += ds.astype(F32)
                right[at, QKV + lo:QKV + lo + LANES] = nn(ds, keys).astype(BF16)
                right[at, QKV + 768 + lo:QKV + 768 + lo + LANES] = pick(tn(ds, q2)).astype(BF16)
                right[at, QKV + 1536 + lo:QKV + 1536 + lo + LANES] = dval.astype(BF16)

        def after(_):
            self.dh3[...] = nt(right[:, QKV:QKV + 2304], self.self_qkv[...])

        def finish(_):
            total = jnp.zeros((1, 768), F32)
            for at in self.row_blocks():
                tok = self.tokens[at].astype(F32)
                back, gain = norm_pull(tok, self.gains[0:1], self.dh3[at])
                total += gain
                self.grad_tokens[at] = (self.y3[at] + back).astype(BF16)
            self.dgains[0:1] = total

        def turn(_):
            for at in self.row_blocks():
                self.hid[at] = normed(self.tokens[at].astype(F32), self.gains[0:1])
            self.put_lefts(L_H1, self.hid[...])
            self.put_lefts(L_O, self.att[...])

        self.in_steps(16, ((1, before), (4, attention), (1, after), (1, finish), (1, turn)))
        for copy in self.stores()[1:]:
            copy.start()

    def bias_rows(self):
        row = lax.broadcasted_iota(jnp.int32, (LANES, LANES), 0)
        col = lax.broadcasted_iota(jnp.int32, (LANES, LANES), 1)
        flip = jnp.where(row + col == LANES - 1, 1.0, 0.0)
        out = []
        for p in range(6):
            turned = nn(flip, self.dbias[p], precision=lax.Precision.HIGHEST)
            for k in range(2):
                rolled = pltpu.roll(turned[:, k * LANES:(k + 1) * LANES], 0, 1, stride=1, stride_axis=0)
                out.append(jnp.sum(rolled, axis=0, keepdims=True))
        return out

    def spread_ids(self, width):
        slot = lax.broadcasted_iota(jnp.int32, (4 * MEM_PAD, width), 0)
        wanted = jnp.full((4 * MEM_PAD, width), -1, jnp.int32)
        for q in range(self.questions):
            for i in range(self.ids.shape[1]):
                wanted = jnp.where(slot == q * MEM_PAD + i, self.ids[q, i], wanted)
        return wanted

    def advance(self, t, fixed=None, right=None):
        left, value = self.place(t)
        if fixed is not None:
            left, value = fixed, right

        def product(parity):
            return nn(self.left[left, parity], value())
        self.reducer.step(t, product)

    def place(self, d):
        u = d - 16
        late = jnp.where(u < 4, 1 + u // 2, jnp.where(u < 8, 3, jnp.where(u < 10, 4, 5)))
        left = jnp.where(d < 16, L_R + (d - 8) // 2, late)
        col = pl.multiple_of(jnp.where(d < 16, E3 + lax.rem(d, 2) * 384, B2 + u * 384), LANES)
        return left, lambda: self.right[:, pl.ds(col, 384)]


MESH_ID = pl.DeviceIdType.MESH
CHUNK_ROWS, CHUNK_COLS, PAIR_ROWS, SMALL_ROWS = 96, 384, 48, 48
PERIOD, GAP, LAST_PAIR, SMALL_FROM, LAST = 5, 26, 21, 29, 37
CHUNKS, SPLIT = 32, 4
DEPTH = Bunch(own=12, mid=10, snd=3, r0=3, rp=2, r1=6, r2=5, r3=5, r4=5)
LAG = Bunch(one=1, two=3, three=2, four=2, five=2, six=3)
LATE = Bunch(one=1, two=3, three=2, four=2, five=3, six=3)


def after(lags):
    return list(itertools.accumulate(vars(lags).values()))


def data_of(k):
    pair = (lax.rem(k, PERIOD) == 1) & (k <= GAP)
    return jnp.where(pair, k - PERIOD, jnp.where(k > GAP, k - 1, k))


class Reducer:
    def __init__(self, bufs, sems, out_ref):
        self.b, self.s, self.out = bufs, sems, out_ref
        dp, z = lax.axis_index("dp"), lax.axis_index("replica")
        here = Bunch(dp=dp, replica=z)
        self.core = lax.rem(dp, 2)
        self.x = lax.rem(dp // 2, 2)
        self.y = dp // 4
        self.inner = lax.rem((z + 1) // 2, 2) == 1
        self.end = lax.rem((z + 1) // 2, 2) == 0
        self.near = pl.multiple_of(PAIR_ROWS * lax.rem(z, 2), PAIR_ROWS)
        self.far = pl.multiple_of(PAIR_ROWS * (1 - lax.rem(z, 2)), PAIR_ROWS)
        self.to_core = dict(vars(here), dp=dp + 1 - 2 * self.core)
        self.to_x = dict(vars(here), dp=dp + 2 - 4 * self.x)
        self.to_y = dict(vars(here), dp=dp + 4 - 8 * self.y)
        self.to_pair = dict(vars(here), replica=z + 1 - 2 * lax.rem(z, 2))
        self.to_mid = dict(vars(here), replica=3 - z)

    def enter(self):
        bar = pltpu.get_barrier_semaphore()
        for target in (self.to_core, self.to_x, self.to_y, self.to_pair, self.to_mid):
            pl.semaphore_signal(bar, inc=1, device_id=target, device_id_type=MESH_ID)
        pl.semaphore_wait(bar, 5)

    def copy(self, src, dst, send, recv, target):
        return pltpu.make_async_remote_copy(
            src_ref=src, dst_ref=dst, send_sem=send, recv_sem=recv, device_id=target, device_id_type=MESH_ID)

    def core_copy(self, k, n):
        a, r, rows = lax.rem(k, DEPTH.snd), lax.rem(k, DEPTH.r0), pl.ds(0, n)
        return self.copy(self.b.snd.at[a, :, rows], self.b.r0.at[r, :, rows], self.s.snd.at[a], self.s.r0.at[r],
                         self.to_core)

    def pair_copy(self, d):
        o, r = lax.rem(d + PERIOD, DEPTH.own), lax.rem(d // PERIOD, DEPTH.rp)
        return self.copy(self.b.own.at[o, :, :, pl.ds(self.far, PAIR_ROWS)], self.b.rp.at[r], self.s.sp.at[r],
                         self.s.rp.at[r], self.to_pair)

    def first_copies(self, k, n, base):
        o, r = lax.rem(k, DEPTH.own), lax.rem(k, DEPTH.r1)
        half = n // 2
        low, high, into = pl.ds(base, half), pl.ds(base + half, half), pl.ds(0, half)
        return (
            self.copy(self.b.own.at[o, :, 1 - self.x, low], self.b.r1x.at[r, :, into], self.s.s1x.at[r],
                      self.s.r1x.at[r], self.to_x),
            self.copy(self.b.own.at[o, 1 - self.y, :, high], self.b.r1y.at[r, :, into], self.s.s1y.at[r],
                      self.s.r1y.at[r], self.to_y),
        )

    def second_copies(self, k, n, base):
        o, r = lax.rem(k, DEPTH.own), lax.rem(k, DEPTH.r2)
        half = n // 2
        low, high, into = pl.ds(base, half), pl.ds(base + half, half), pl.ds(0, half)
        return (
            self.copy(self.b.own.at[o, self.y, 1 - self.x, high], self.b.r2x.at[r, into], self.s.s2x.at[r],
                      self.s.r2x.at[r], self.to_x),
            self.copy(self.b.own.at[o, 1 - self.y, self.x, low], self.b.r2y.at[r, into], self.s.s2y.at[r],
                      self.s.r2y.at[r], self.to_y),
        )

    def mine(self, k, n, base=0):
        return self.b.mid.at[lax.rem(k, DEPTH.mid), pl.ds(base, n)]

    def inward_copy(self, k, n, base):
        r = lax.rem(k, DEPTH.r3)
        return self.copy(self.mine(k, n, base), self.b.r3.at[r, pl.ds(0, n)], self.s.s3.at[r], self.s.r3.at[r],
                         self.to_pair)

    def middle_copy(self, k, n):
        r = lax.rem(k, DEPTH.r4)
        return self.copy(self.mine(k, n), self.b.r4.at[r, pl.ds(0, n)], self.s.s4.at[r], self.s.r4.at[r], self.to_mid)

    def result(self, k, n):
        if n == SMALL_ROWS:
            last = k == LAST
            u = k - SMALL_FROM
            row, d = jnp.where(last, 0, lax.rem(u, 2) * SMALL_ROWS), jnp.where(last, CHUNKS, CHUNKS - SPLIT + u // 2)
        else:
            row, d = 0, data_of(k)
        return self.out.at[pl.ds(pl.multiple_of(row, 8), n), pl.ds(pl.multiple_of(d * CHUNK_COLS, LANES), CHUNK_COLS)]

    def outward_copy(self, k, n):
        r = lax.rem(k, DEPTH.r4)
        return self.copy(self.mine(k, n), self.result(k, n), self.s.s5.at[r], self.s.out.at[k], self.to_pair)

    def keep_copy(self, k, n):
        return pltpu.make_async_copy(self.mine(k, n), self.result(k, n), self.s.out.at[k])

    def grant(self, sem, k, depth, target):
        @pl.when(k + depth <= LAST)
        def _():
            pl.semaphore_signal(sem, inc=1, device_id=target, device_id_type=MESH_ID)

    def need(self, sem, k, depth):
        @pl.when((k >= depth) & (k != depth + 1))
        def _():
            pl.semaphore_wait(sem, 1)

    def before(self, t):
        return t - jnp.where(t == GAP + DEPTH.snd, 2 * DEPTH.snd, DEPTH.snd)

    def fill(self, t, half_product):
        n = CHUNK_ROWS
        early = (lax.rem(t, PERIOD) == 1) & (t <= LAST_PAIR)
        a, o = lax.rem(t, DEPTH.snd), lax.rem(jnp.where(early, t + PERIOD, t), DEPTH.own)

        @pl.when(t >= DEPTH.snd)
        def _():
            self.core_copy(self.before(t), n).wait_send()

        away = half_product(1 - self.core)
        for g in range(4):
            self.b.snd[a, g] = away[g * n:(g + 1) * n]

        @pl.when((t >= DEPTH.r0) & (t != GAP + DEPTH.r0))
        def _():
            pl.semaphore_wait(self.s.c0, 1)
        self.core_copy(t, n).start()
        here = half_product(self.core)
        for g in range(4):
            self.b.own[o, g // 2, g % 2] = here[g * n:(g + 1) * n]

    def fill_small(self, k, part):
        n = SMALL_ROWS
        a, o = lax.rem(k, DEPTH.snd), lax.rem(k, DEPTH.own)

        @pl.when(k - DEPTH.snd < SMALL_FROM)
        def _():
            self.core_copy(self.before(k), CHUNK_ROWS).wait_send()

        @pl.when(k - DEPTH.snd >= SMALL_FROM)
        def _():
            self.core_copy(k - DEPTH.snd, n).wait_send()
        self.b.snd[a, :, 0:n, :] = part(1 - self.core)

        @pl.when(k != GAP + DEPTH.r0)
        def _():
            pl.semaphore_wait(self.s.c0, 1)
        self.core_copy(k, n).start()
        here = part(self.core)
        for g in range(4):
            self.b.own[o, g // 2, g % 2, 0:n, :] = here[g]

    def add_core(self, d, o, n):
        r = lax.rem(d, DEPTH.r0)
        self.core_copy(d, n).wait_recv()
        for g in range(4):
            self.b.own[o, g // 2, g % 2, 0:n] += self.b.r0[r, g, 0:n]

        @pl.when((d + DEPTH.r0 <= LAST) & (d + DEPTH.r0 != GAP))
        def _():
            pl.semaphore_signal(self.s.c0, inc=1, device_id=self.to_core, device_id_type=MESH_ID)

    def start_first(self, k, n, base):
        self.need(self.s.c1x, k, DEPTH.r1)
        self.need(self.s.c1y, k, DEPTH.r1)
        for copy in self.first_copies(k, n, base):
            copy.start()

    def stage_one(self, k, n):
        self.add_core(k, lax.rem(k, DEPTH.own), n)
        self.start_first(k, n, 0)

    def stage_pair(self, d):
        self.add_core(d, lax.rem(d + PERIOD, DEPTH.own), CHUNK_ROWS)

        @pl.when(d // PERIOD >= DEPTH.rp)
        def _():
            pl.semaphore_wait(self.s.cp, 1)
        self.pair_copy(d).start()

    def stage_one_pair(self, k):
        d = k - PERIOD
        o, r = lax.rem(k, DEPTH.own), lax.rem(d // PERIOD, DEPTH.rp)
        self.pair_copy(d).wait()
        rows = pl.ds(self.near, PAIR_ROWS)
        for g in range(4):
            self.b.own[o, g // 2, g % 2, rows] += self.b.rp[r, g // 2, g % 2]

        @pl.when(d + DEPTH.rp * PERIOD <= LAST_PAIR)
        def _():
            pl.semaphore_signal(self.s.cp, inc=1, device_id=self.to_pair, device_id_type=MESH_ID)
        self.start_first(k, PAIR_ROWS, self.near)

    def stage_two(self, k, n, base):
        o, r, half = lax.rem(k, DEPTH.own), lax.rem(k, DEPTH.r1), n // 2
        low, high = pl.ds(base, half), pl.ds(base + half, half)
        by_x, by_y = self.first_copies(k, n, base)
        by_x.wait_recv()
        for g in range(2):
            self.b.own[o, g, self.x, low, :] += self.b.r1x[r, g, 0:half]
        by_y.wait_recv()
        for g in range(2):
            self.b.own[o, self.y, g, high, :] += self.b.r1y[r, g, 0:half]
        self.grant(self.s.c1x, k, DEPTH.r1, self.to_x)
        self.grant(self.s.c1y, k, DEPTH.r1, self.to_y)
        by_x.wait_send()
        by_y.wait_send()
        self.need(self.s.c2x, k, DEPTH.r2)
        self.need(self.s.c2y, k, DEPTH.r2)
        for copy in self.second_copies(k, n, base):
            copy.start()

    def stage_three(self, k, n, base):
        o, r, half = lax.rem(k, DEPTH.own), lax.rem(k, DEPTH.r2), n // 2
        low, high = pl.ds(base, half), pl.ds(base + half, half)
        m = lax.rem(k, DEPTH.mid)
        by_x, by_y = self.second_copies(k, n, base)
        by_x.wait_recv()
        self.b.mid[m, high, :] = self.b.own[o, self.y, self.x, high, :] + self.b.r2x[r, 0:half]
        by_y.wait_recv()
        self.b.mid[m, low, :] = self.b.own[o, self.y, self.x, low, :] + self.b.r2y[r, 0:half]
        self.grant(self.s.c2x, k, DEPTH.r2, self.to_x)
        self.grant(self.s.c2y, k, DEPTH.r2, self.to_y)
        by_x.wait_send()
        by_y.wait_send()

        @pl.when(self.end)
        def _():
            self.need(self.s.c3, k, DEPTH.r3)
            self.inward_copy(k, n, base).start()

    def stage_four(self, k, n, paired):
        r = lax.rem(k, DEPTH.r3)
        part = PAIR_ROWS if paired else n

        @pl.when(self.end)
        def _():
            self.inward_copy(k, part, self.near if paired else 0).wait_send()

        @pl.when(self.inner)
        def _():
            self.inward_copy(k, part, 0).wait_recv()
            if paired:
                self.b.mid[lax.rem(k, DEPTH.mid), pl.ds(self.far, part), :] = self.b.r3[r, 0:part]
            else:
                self.mine(k, n)[...] += self.b.r3[r, 0:n]
            self.grant(self.s.c3, k, DEPTH.r3, self.to_pair)
            self.need(self.s.c4, k, DEPTH.r4)
            self.middle_copy(k, n).start()

    def stage_five(self, k, n):
        r = lax.rem(k, DEPTH.r4)

        @pl.when(self.inner)
        def _():
            self.middle_copy(k, n).wait()
            self.mine(k, n)[...] += self.b.r4[r, 0:n]
            self.grant(self.s.c4, k, DEPTH.r4, self.to_mid)
            self.outward_copy(k, n).start()
            self.keep_copy(k, n).start()

    def stage_six(self, k, n):
        @pl.when(self.inner)
        def _():
            self.outward_copy(k, n).wait_send()
        self.keep_copy(k, n).wait()

    def stages(self):
        n, small, pair = CHUNK_ROWS, SMALL_ROWS, PAIR_ROWS
        return (
            (lambda k: self.stage_one(k, n), self.stage_one_pair, lambda k: self.stage_one(k, small)),
            (lambda k: self.stage_two(k, n, 0), lambda k: self.stage_two(k, pair, self.near),
             lambda k: self.stage_two(k, small, 0)),
            (lambda k: self.stage_three(k, n, 0), lambda k: self.stage_three(k, pair, self.near),
             lambda k: self.stage_three(k, small, 0)),
            (lambda k: self.stage_four(k, n, False), lambda k: self.stage_four(k, n, True),
             lambda k: self.stage_four(k, small, False)),
            (lambda k: self.stage_five(k, n), None, lambda k: self.stage_five(k, small)),
            (lambda k: self.stage_six(k, n), None, lambda k: self.stage_six(k, small)),
        )

    def move(self, t):
        for behind, (usual, paired, small) in reversed(list(zip(after(LAG), self.stages()))):
            k = t - behind
            odd = (lax.rem(k + PERIOD, PERIOD) == 1) & (k <= GAP)
            if paired is None:
                pl.when((k >= 0) & (k < SMALL_FROM) & (k != 1))(functools.partial(usual, k))
            else:
                pl.when((k >= 0) & (k < SMALL_FROM) & jnp.logical_not(odd))(functools.partial(usual, k))
                pl.when(odd & (k > 1))(functools.partial(paired, k))
            pl.when((k >= SMALL_FROM) & (k <= LAST))(functools.partial(small, k))
        d = t - LAG.one
        pl.when((lax.rem(d + PERIOD, PERIOD) == 1) & (d >= 0) & (d <= LAST_PAIR))(functools.partial(self.stage_pair, d))

    def drain(self):
        left = []
        for number, (due, order) in enumerate(zip(after(LAG), after(LATE))):
            left += [(k + order, -number, k) for k in range(LAST + 1) if k + due > LAST]
        for _, number, k in sorted(left):
            usual, paired, small = self.stages()[-number]
            odd = k % PERIOD == 1 and k <= GAP
            (small if k >= SMALL_FROM else paired if odd and paired is not None else usual)(jnp.int32(k))

    def step(self, t, half_product):
        self.move(t)
        self.fill(t, half_product)

    def finish(self, half, small):
        def body(k, c):
            self.move(k)
            self.fill_small(k, lambda parity: half(parity, k - SMALL_FROM))
            return c
        lax.fori_loop(SMALL_FROM, LAST, body, 0)
        self.move(LAST)
        self.fill_small(LAST, lambda parity: small[parity])

        self.drain()
        for back in range(DEPTH.snd):
            self.core_copy(LAST - back, SMALL_ROWS).wait_send()


def reducer_scratch():
    rows, cols, half, count, d = CHUNK_ROWS, CHUNK_COLS, CHUNK_ROWS // 2, LAST + 1, DEPTH
    vmem = lambda *shape: pltpu.VMEM(shape, jnp.float32)
    dma = lambda n: pltpu.SemaphoreType.DMA((n,))
    plain = pltpu.SemaphoreType.REGULAR
    bufs = Bunch(
        own=vmem(d.own, 2, 2, rows, cols), mid=vmem(d.mid, rows, cols), snd=vmem(d.snd, 4, rows, cols),
        r0=vmem(d.r0, 4, rows, cols), rp=vmem(d.rp, 2, 2, PAIR_ROWS, cols), r1x=vmem(d.r1, 2, half, cols),
        r1y=vmem(d.r1, 2, half, cols), r2x=vmem(d.r2, half, cols), r2y=vmem(d.r2, half, cols),
        r3=vmem(d.r3, rows, cols), r4=vmem(d.r4, rows, cols))
    sems = Bunch(
        snd=dma(d.snd), r0=dma(d.r0), sp=dma(d.rp), rp=dma(d.rp), out=dma(count), s1x=dma(d.r1), r1x=dma(d.r1),
        s1y=dma(d.r1), r1y=dma(d.r1), s2x=dma(d.r2), r2x=dma(d.r2), s2y=dma(d.r2), r2y=dma(d.r2), s3=dma(d.r3),
        r3=dma(d.r3), s4=dma(d.r4), r4=dma(d.r4), s5=dma(d.r4), c0=plain, cp=plain, c1x=plain, c1y=plain, c2x=plain,
        c2y=plain, c3=plain, c4=plain)
    return bufs, sems


class PartWriter:
    def __init__(self, bufs, sems, out_ref):
        self.b, self.s, self.out = bufs, sems, out_ref

    def enter(self):
        pass

    def step(self, t, half_product):
        for parity in range(2):
            value = half_product(parity)
            for g in range(4):
                self.b.own[parity, g // 2, g % 2] = value[g * 96:(g + 1) * 96]
        copy = pltpu.make_async_copy(self.b.own, self.out.at[t], self.s.out.at[0])
        copy.start()
        copy.wait()


def regroup(groups, refs):
    result, first = [], 0
    for names in groups:
        result.append(Bunch(**dict(zip(names, refs[first:first + len(names)]))))
        first += len(names)
    return result


def layer_kernel(groups, alone, *refs):
    given, hbm, out, vm, load, store, bufs, sems = regroup(groups, refs)
    reducer = (PartWriter if alone else Reducer)(bufs, sems, out.chunks)
    layer = Layer(given, hbm, out, vm, load, store)
    layer.reducer = reducer
    layer.forward(reducer.enter)
    layer.feed_forward()
    layer.backward_cross()
    layer.backward_self()

    if alone:
        def body(t, c):
            layer.advance(t)
            return c
        lax.fori_loop(24, CHUNKS, body, 0)
        entries = vm.memory_keys.shape[0]
        entry = lax.broadcasted_iota(jnp.int32, (4 * MEM_PAD, entries), 1)
        hit = jnp.where(layer.spread_ids(entries) == entry, 1.0, 0.0)
        out.mem_k[...] = tn(hit, vm.dmem_k[...], precision=lax.Precision.HIGHEST)
        out.mem_v[...] = tn(hit, vm.dmem_v[...], precision=lax.Precision.HIGHEST)
        out.gains[...] = vm.dgains[...]
        for h, row in enumerate(layer.bias_rows()):
            out.bias[h:h + 1, :] = row
    else:
        fill_small_rows(layer, vm)

        def body(t, c):
            left, value = layer.place(jnp.where(t > GAP, t - 1, t))
            reducer.move(t)

            @pl.when(t != GAP)
            def _():
                reducer.fill(t, lambda parity: nn(vm.left[left, parity], value()))
            return c
        lax.fori_loop(24, SMALL_FROM, body, 0)

        def half(parity, u):
            left, value = layer.place(CHUNKS - SPLIT + u // 2)
            at = lambda g: pl.ds(pl.multiple_of(g * 96 + lax.rem(u, 2) * SMALL_ROWS, SMALL_ROWS), SMALL_ROWS)
            rows = jnp.concatenate([vm.left[left, parity, at(g)] for g in range(4)], axis=0)
            return nn(rows, value()).reshape(4, SMALL_ROWS, CHUNK_COLS)
        reducer.finish(half, vm.small)
    for copy in layer.stores():
        copy.wait()


def fill_small_rows(layer, vm):
    out_row = lax.broadcasted_iota(jnp.int32, (4 * MEM_PAD, 64), 1)
    entry = 4 * (out_row // 8) + lax.rem(out_row, 4)
    same = layer.spread_ids(64) == entry
    keys_row = lax.rem(out_row // 4, 2) == 0
    hit_k = jnp.where(same & keys_row, 1.0, 0.0)
    hit_v = jnp.where(same & jnp.logical_not(keys_row), 1.0, 0.0)
    memory = (tn(hit_k, vm.dmem_k[...], precision=lax.Precision.HIGHEST)
              + tn(hit_v, vm.dmem_v[...], precision=lax.Precision.HIGHEST))
    bias = jnp.concatenate(layer.bias_rows() + [jnp.zeros((4, LANES), F32)], axis=0)
    gains = jnp.concatenate([vm.dgains[...], jnp.zeros((5, 768), F32)], axis=0)
    for b in range(8):
        block = vm.small.at[b % 2, b // 2]
        for j in range(6):
            row, col = 8 * (j % 4), LANES * (j // 4)
            block[row:row + 8, col:col + LANES] = memory[8 * b:8 * b + 8, j * LANES:(j + 1) * LANES]
        turned = gains if b == 0 else pltpu.roll(gains, 768 - 96 * b, 1)
        block[16:24, LANES:2 * LANES] = turned[:, :LANES]
        block[24:32, LANES:2 * LANES] = jnp.zeros((8, LANES), F32)
        block[0:16, 2 * LANES:] = bias
        block[16:32, 2 * LANES:] = jnp.zeros((16, LANES), F32)
        block[32:, :] = jnp.zeros((SMALL_ROWS - 32, CHUNK_COLS), F32)


def call_grouped(kernel, ins, outs, scratch, **options):
    groups = [list(vars(g)) for g in ins + outs + scratch]
    pairs = lambda gs, i: [v[i] for g in gs for v in vars(g).values()]
    space = lambda gs: [pl.BlockSpec(memory_space=s) for s in pairs(gs, 1)]
    result = pl.pallas_call(
        functools.partial(kernel, groups), out_shape=pairs(outs, 0), in_specs=space(ins), out_specs=space(outs),
        scratch_shapes=[v for g in scratch for v in vars(g).values()], **options)(*pairs(ins, 0))
    return regroup(groups[len(ins):len(ins) + len(outs)], result)[0]


def in_space(space, **values):
    return Bunch(**{name: (value, space) for name, value in values.items()})


def run_layer(alone, hbm, given, tables):
    rows, width = hbm.tokens.shape
    enc_rows = hbm.encodings.shape[0]
    entries = hbm.memory_keys.shape[0]
    shape = jax.ShapeDtypeStruct
    outs = in_space(pl.ANY, layer_output=shape((rows, width), BF16), grad_tokens=shape((rows, width), BF16),
                    grad_encodings=shape((enc_rows, width), BF16))
    if alone:
        part = shape((entries, width), F32)
        vars(outs).update(vars(in_space(pl.ANY, chunks=shape((CHUNKS, 2, 2, 2, CHUNK_ROWS, CHUNK_COLS), F32))))
        vars(outs).update(vars(in_space(pltpu.VMEM, mem_k=part, mem_v=part, gains=shape((3, width), F32),
                                        bias=shape((12, LANES), F32))))
    else:
        vars(outs).update(vars(in_space(pl.ANY, chunks=shape((CHUNK_ROWS, (CHUNKS + 1) * CHUNK_COLS), F32))))
    loaded = [name for name in vars(hbm) if vars(hbm)[name] is not hbm.ff_in and vars(hbm)[name] is not hbm.ff_out]
    vm = Bunch(**{name: pltpu.VMEM(vars(hbm)[name].shape, BF16) for name in loaded})
    big = lambda cols, kind: pltpu.VMEM((rows, cols), kind)
    vars(vm).update(
        wi=pltpu.VMEM((2, width, FF_TILE), BF16), wo=pltpu.VMEM((2, FF_TILE, width), BF16),
        hid=big(width, BF16), att=big(width, BF16), att2=big(width, BF16), right=big(RIGHT, BF16),
        left=pltpu.VMEM((10, 2, 384, rows), BF16),
        y1=big(width, F32), y2=big(width, F32), y3=big(width, F32), dh3=big(width, F32),
        act=big(FF_TILE, BF16), dz=big(FF_TILE, BF16),
        bias=pltpu.VMEM((6, LANES, 2 * LANES), F32), dbias=pltpu.VMEM((6, LANES, 2 * LANES), F32),
        gains=pltpu.VMEM((3, width), F32), dgains=pltpu.VMEM((3, width), F32), up=big(width, BF16),
        mem_k=pltpu.VMEM((4, MEM_PAD, width), BF16), mem_v=pltpu.VMEM((4, MEM_PAD, width), BF16),
        dmem_k=pltpu.VMEM((4 * MEM_PAD, width), F32), dmem_v=pltpu.VMEM((4 * MEM_PAD, width), F32),
        grad_encodings=pltpu.VMEM((enc_rows, width), BF16),
        wi_sem=pltpu.SemaphoreType.DMA((2,)), wo_sem=pltpu.SemaphoreType.DMA((2,)))
    one = pltpu.SemaphoreType.DMA
    load = Bunch(**{name: one for name in loaded})
    store = Bunch(layer_output=one, grad_tokens=one, grad_encodings=one)
    bufs, sems = reducer_scratch()
    extra = dict(collective_id=0)
    if alone:
        bufs, sems = Bunch(own=pltpu.VMEM((2, 2, 2, CHUNK_ROWS, CHUNK_COLS), F32)), Bunch(out=pltpu.SemaphoreType.DMA((1,)))
        extra = {}
    else:
        vm.small = pltpu.VMEM((2, 4, SMALL_ROWS, CHUNK_COLS), F32)
    ins = [Bunch(**vars(in_space(pltpu.SMEM, lengths=given.lengths, ids=given.ids)),
                 **vars(in_space(pltpu.VMEM, gain_self=given.gain_self, gain_cross=given.gain_cross,
                                 gain_ff=given.gain_ff, rel_bias=given.rel_bias, tables=tables))),
           in_space(pl.ANY, **vars(hbm))]
    return call_grouped(
        lambda groups, *refs: layer_kernel(groups, alone, *refs), ins, [outs], [vm, load, store, bufs, sems],
        compiler_params=pltpu.CompilerParams(has_side_effects=True, vmem_limit_bytes=62 * 2**20, **extra),
        cost_estimate=pl.CostEstimate(flops=30 * 10**9, bytes_accessed=35 * 10**6, transcendentals=5 * 10**6))


FF_IN_AT, FF_OUT_AT, CROSS_OUT_AT, CROSS_Q_AT, CROSS_KV_AT, SELF_OUT_AT, SELF_QKV_AT = 0, 8, 16, 18, 20, 24, 26


def place_kernel(groups, *refs):
    given, tables, out, vm = regroup(groups, refs)
    sems = iter(range(vm.sem.shape[0]))
    copy = lambda src, dst: pltpu.make_async_copy(src, dst, vm.sem.at[next(sems)])
    small_at = slice(CHUNKS * CHUNK_COLS, (CHUNKS + 1) * CHUNK_COLS)
    small = copy(given.chunks.at[0:SMALL_ROWS, small_at], vm.chunks.at[0:SMALL_ROWS, small_at])
    small.start()
    pieces = ((out.ff_in, FF_IN_AT), (out.ff_out, FF_OUT_AT), (out.cross_out, CROSS_OUT_AT), (out.cross_q, CROSS_Q_AT),
              (out.cross_kv, CROSS_KV_AT), (out.self_out, SELF_OUT_AT), (out.self_qkv, SELF_QKV_AT))
    moves = []
    for ref, first in pieces:
        cols = ref.shape[0] * ref.shape[1] // CHUNK_ROWS
        at = slice(first * CHUNK_COLS, first * CHUNK_COLS + cols)
        targets = [(vm.chunks.at[:, at], ref)]
        if first == FF_OUT_AT:
            targets = [(vm.chunks.at[:, (first + k) * CHUNK_COLS:(first + k + 1) * CHUNK_COLS],
                        ref.at[(k // 2) * 96:(k // 2) * 96 + 96, (k % 2) * CHUNK_COLS:(k % 2 + 1) * CHUNK_COLS])
                       for k in range(8)]
        moves.append((copy(given.chunks.at[:, at], vm.chunks.at[:, at]), [copy(*pair) for pair in targets]))
    for src, mid, dst in ((given.layer_output, vm.a, out.layer_output), (given.grad_tokens, vm.b, out.grad_tokens),
                          (given.grad_encodings, vm.c, out.grad_encodings)):
        moves.append((copy(src, mid), [copy(mid, dst)]))
    for into, _ in moves:
        into.start()
    small.wait()
    sums = vm.chunks[0:SMALL_ROWS, small_at]
    for j in range(6):
        row, col = 8 * (j % 4), LANES * (j // 4)
        out.mem_k[:, j * LANES:(j + 1) * LANES] = sums[row:row + 4, col:col + LANES]
        out.mem_v[:, j * LANES:(j + 1) * LANES] = sums[row + 4:row + 8, col:col + LANES]
    for n, gain in enumerate((out.gain_self, out.gain_cross, out.gain_ff)):
        gain[...] = sums[16 + n, LANES:LANES + 96]
    out.rel_bias[...] = nt(sums[0:16, 2 * LANES:], tables.tables[1], precision=lax.Precision.HIGHEST)[0:12]
    for into, onward in moves:
        into.wait()
        for move in onward:
            move.start()
    for _, onward in moves:
        for move in onward:
            move.wait()


def place(done, tables):
    shape = jax.ShapeDtypeStruct
    outs = in_space(
        pl.ANY, layer_output=shape(done.layer_output.shape, BF16), grad_tokens=shape(done.grad_tokens.shape, BF16),
        grad_encodings=shape(done.grad_encodings.shape, BF16), ff_in=shape((96, 3072), F32), ff_out=shape((384, 768), F32),
        cross_out=shape((96, 768), F32), cross_q=shape((96, 768), F32), cross_kv=shape((96, 1536), F32),
        self_out=shape((96, 768), F32), self_qkv=shape((96, 2304), F32))
    gain = shape((96,), F32)
    vars(outs).update(vars(in_space(
        pltpu.VMEM, mem_k=shape((4, 768), F32), mem_v=shape((4, 768), F32), gain_self=gain, gain_cross=gain,
        gain_ff=gain, rel_bias=shape((12, 32), F32))))
    scratch = Bunch(
        chunks=pltpu.VMEM(done.chunks.shape, F32), a=pltpu.VMEM(done.layer_output.shape, BF16),
        b=pltpu.VMEM(done.grad_tokens.shape, BF16), c=pltpu.VMEM(done.grad_encodings.shape, BF16),
        sem=pltpu.SemaphoreType.DMA((28,)))
    return call_grouped(
        place_kernel, [in_space(pl.ANY, **vars(done)), in_space(pltpu.VMEM, tables=tables)], [outs], [scratch],
        compiler_params=pltpu.CompilerParams(vmem_limit_bytes=62 * 2**20),
        cost_estimate=pl.CostEstimate(flops=0, bytes_accessed=15 * 10**6, transcendentals=0))


def sum_alone(done, tables):
    chunks = done.chunks.transpose(0, 2, 3, 1, 4, 5).reshape(CHUNKS, 768, CHUNK_COLS)

    def whole(first, cols):
        part = chunks[first:first + cols // 384]
        return part.transpose(1, 0, 2).reshape(768, cols)

    ff_out = chunks[8:16].reshape(4, 2, 8, 96, CHUNK_COLS)
    parts = Bunch(
        ff_in=whole(FF_IN_AT, 3072), ff_out=ff_out.transpose(2, 0, 3, 1, 4).reshape(3072, 768),
        cross_out=whole(CROSS_OUT_AT, 768), cross_q=whole(CROSS_Q_AT, 768), cross_kv=whole(CROSS_KV_AT, 1536),
        self_out=whole(SELF_OUT_AT, 768), self_qkv=whole(SELF_QKV_AT, 2304), mem_k=done.mem_k, mem_v=done.mem_v,
        gain_self=done.gains[0], gain_cross=done.gains[1], gain_ff=done.gains[2])
    out = Bunch(**{name: lax.psum(lax.psum_scatter(value, "dp", scatter_dimension=0, tiled=True), "replica")
                   for name, value in vars(parts).items()})
    bias = lax.psum(done.bias, ("dp", "replica"))
    out.rel_bias = lax.dot_general(bias, tables[1], (((1,), (1,)), ((), ())), precision=lax.Precision.HIGHEST)
    out.layer_output, out.grad_tokens, out.grad_encodings = done.layer_output, done.grad_tokens, done.grad_encodings
    return out


def on_device(tokens, encodings, lengths, memory_ids, memory_keys, memory_values, gain_self, gain_cross, gain_ff,
              rel_bias, self_qkv, self_out, cross_q, cross_kv, cross_out, ff_in, ff_out, cotangent):
    width = tokens.shape[-1]
    alone = not (lax.axis_size("dp") == 8 and lax.axis_size("replica") == 4)
    hbm = Bunch(tokens=tokens.reshape(-1, width), encodings=encodings.reshape(-1, width),
                cotangent=cotangent.reshape(-1, width), memory_keys=memory_keys, memory_values=memory_values,
                self_qkv=self_qkv, self_out=self_out, cross_q=cross_q, cross_kv=cross_kv, cross_out=cross_out,
                ff_in=ff_in, ff_out=ff_out)
    given = Bunch(lengths=lengths, ids=memory_ids, gain_self=gain_self, gain_cross=gain_cross, gain_ff=gain_ff,
                  rel_bias=rel_bias.T)
    tables = jnp.asarray(bucket_tables(LANES, rel_bias.shape[0]))
    done = run_layer(alone, hbm, given, tables)
    out = sum_alone(done, tables) if alone else place(done, tables)
    return (
        out.layer_output.reshape(tokens.shape), out.grad_tokens.reshape(tokens.shape),
        out.grad_encodings.reshape(encodings.shape), out.gain_self, out.gain_cross, out.gain_ff, out.rel_bias.T,
        out.self_qkv, out.self_out, out.cross_q, out.cross_kv, out.cross_out, out.ff_in, out.ff_out, out.mem_k,
        out.mem_v)


def solution(mesh):
    split, whole = P(("dp", "replica")), P()
    return jax.shard_map(
        on_device,
        mesh=mesh,
        in_specs=(split,) * 4 + (whole,) * 13 + (split,),
        out_specs=(split,) * 3 + (P("dp"),) * 3 + (whole,) + (P("dp"),) * 9,
        check_vma=False,
    )
```

```python
import functools
import itertools
from types import SimpleNamespace as Bunch

import jax
import jax.numpy as jnp
import numpy as np
from jax import lax
from jax.experimental import pallas as pl
from jax.experimental.pallas import tpu as pltpu
from jax.sharding import PartitionSpec as P

F32, BF16 = jnp.float32, jnp.bfloat16
EPSILON = 1e-06
NEGATIVE = -1000000000.0
MAXDIST = 128
LANES = 128
E3, B2, CQ, EKV, B1, QKV, RIGHT = 0, 768, 1536, 2304, 3840, 4608, 6912
L_H3, L_O2, L_H2, L_ENC, L_O, L_H1, L_R = 0, 1, 2, 3, 4, 5, 6
FF_TILE = 384
MEM_PAD = 16


def nn(a, b, **kw):
    return lax.dot_general(a, b, (((1,), (0,)), ((), ())), preferred_element_type=F32, **kw)


def nt(a, b, **kw):
    return lax.dot_general(a, b, (((1,), (1,)), ((), ())), preferred_element_type=F32, **kw)


def tn(a, b, **kw):
    return lax.dot_general(a, b, (((0,), (0,)), ((), ())), preferred_element_type=F32, **kw)


def bucket_of(apart, buckets, distance):
    exact = buckets // 2
    spread = np.log(np.maximum(apart, 1) / exact) / np.log(distance / exact) * (buckets - exact)
    larger = np.minimum(exact + np.floor(np.maximum(spread, 0.0)).astype(np.int64), buckets - 1)
    return np.where(apart < exact, apart, larger).astype(np.int32)


def bucket_tables(length, buckets):
    lane = np.arange(length)
    spread = [bucket_of((length - lane) % length, buckets, MAXDIST), bucket_of(length - 1 - lane, buckets, MAXDIST)]
    return np.stack([(np.arange(buckets)[:, None] == row[None]).astype(np.float32) for row in spread])


def root_scale(v):
    return lax.rsqrt(jnp.mean(v * v, axis=-1, keepdims=True) + EPSILON)


def normed(v, gain):
    return (v * root_scale(v) * gain).astype(BF16)


def norm_pull(v, gain, w):
    scale = root_scale(v)
    gw = w * gain
    back = scale * gw - v * (scale * scale * scale) * jnp.mean(gw * v, axis=-1, keepdims=True)
    return back, jnp.sum(w * v * scale, axis=0, keepdims=True)


def head_masks():
    lane = lax.broadcasted_iota(jnp.int32, (1, LANES), 1)
    first = jnp.where(lane < LANES // 2, 1.0, 0.0)
    return first.astype(BF16), (1.0 - first).astype(BF16), first > 0.5


def stacked(rows, m0, m1):
    return jnp.concatenate([rows * m0, rows * m1], axis=0)


def pair_softmax(s):
    parts = []
    for part in (s[:, :LANES], s[:, LANES:]):
        e = jnp.exp(part - jnp.max(part, axis=-1, keepdims=True))
        parts.append(e * (1.0 / jnp.sum(e, axis=-1, keepdims=True)))
    return jnp.concatenate(parts, axis=1)


def pair_pull(p, dp):
    parts = []
    for lo in (0, LANES):
        a, b = p[:, lo:lo + LANES], dp[:, lo:lo + LANES]
        parts.append((a * (b - jnp.sum(a * b, axis=-1, keepdims=True))).astype(BF16))
    return jnp.concatenate(parts, axis=1)


class Layer:
    def __init__(self, hbm, out, vm, load, store):
        vars(self).update(vars(vm))
        self.hbm, self.out, self.store = hbm, out, store
        self.layer_output, self.grad_tokens = vm.cotangent, vm.att2
        self.questions, self.length, self.enc_len = 4, 128, 64
        self.rows = self.questions * self.length
        self.load = Bunch(**{name: pltpu.make_async_copy(vars(hbm)[name], vars(vm)[name], sem)
                             for name, sem in vars(load).items()})

    def ff_loads(self, j):
        slot = lax.rem(j, 2)
        at = pl.ds(pl.multiple_of(j * FF_TILE, FF_TILE), FF_TILE)
        return (
            pltpu.make_async_copy(self.hbm.ff_in.at[:, at], self.wi.at[slot], self.wi_sem.at[slot]),
            pltpu.make_async_copy(self.hbm.ff_out.at[at, :], self.wo.at[slot], self.wo_sem.at[slot]),
        )

    def q_rows(self, q, n=128):
        return pl.ds(pl.multiple_of(q * n, n), n)

    def put_left(self, index, q, rows):
        turned = rows.T
        width = turned.shape[1]
        at = self.q_rows(q, width)
        for b in range(8):
            self.left[index, b % 2, (b // 2) * 96:(b // 2 + 1) * 96, at] = turned[b * 96:(b + 1) * 96]

    def bias_tables(self):
        table = nn(self.rel_bias[...], self.tables[0], precision=lax.Precision.HIGHEST)
        for p in range(6):
            for k in range(2):
                row = table[2 * p + k:2 * p + k + 1, :]
                self.bias[p, :, k * LANES:(k + 1) * LANES] = pltpu.roll(
                    jnp.broadcast_to(row, (LANES, LANES)), 0, 1, stride=1, stride_axis=0)

    def memory_rows(self):
        entries = self.memory_keys.shape[0]
        slot = lax.broadcasted_iota(jnp.int32, (MEM_PAD, entries), 0)
        entry = lax.broadcasted_iota(jnp.int32, (MEM_PAD, entries), 1)
        for q in range(self.questions):
            wanted = jnp.full((MEM_PAD, entries), -1, jnp.int32)
            for i in range(self.ids.shape[1]):
                wanted = jnp.where(slot == i, self.ids[q, i], wanted)
            pick = jnp.where(wanted == entry, 1.0, 0.0).astype(BF16)
            self.mem_k[q] = nn(pick, self.memory_keys[...]).astype(BF16)
            self.mem_v[q] = nn(pick, self.memory_values[...]).astype(BF16)

    def causal(self):
        row = lax.broadcasted_iota(jnp.int32, (LANES, 2 * LANES), 0)
        col = lax.rem(lax.broadcasted_iota(jnp.int32, (LANES, 2 * LANES), 1), LANES)
        return col <= row

    def self_probs(self, q2, k2, p, allowed):
        return pair_softmax(jnp.where(allowed, nt(q2, k2) + self.bias[p], NEGATIVE))

    def cross_probs(self, q2, k2, present):
        return pair_softmax(jnp.where(present, nt(q2, k2), -1e30))

    def present(self):
        col = lax.rem(lax.broadcasted_iota(jnp.int32, (1, 2 * LANES), 1), LANES)
        return col < self.enc_len + self.ids.shape[1]

    def cross_side(self, q, p, memory, base):
        enc = self.right[self.q_rows(q, self.enc_len), base + p * LANES:base + (p + 1) * LANES]
        mem = memory[q, :, p * LANES:(p + 1) * LANES]
        return jnp.concatenate([enc, mem, jnp.zeros((LANES - 64 - MEM_PAD, LANES), BF16)], axis=0)

    def forward(self, enter):
        load = self.load
        few = (load.gain_self, load.gain_cross, load.gain_ff, load.rel_bias, load.tables, load.lengths, load.ids)
        for copy in (load.tokens, load.self_qkv) + few + (load.encodings, load.cross_kv):
            copy.start()
        enter()
        for copy in few:
            copy.wait()
        for n, gain in enumerate((self.gain_self, self.gain_cross, self.gain_ff)):
            self.gains[n:n + 1, :] = gain[...].reshape(1, gain.shape[0])
        right = self.right
        self.bias_tables()
        self.load.tokens.wait()

        def norm_one(q, c):
            at = self.q_rows(q)
            self.hid[at] = normed(self.tokens[at].astype(F32), self.gains[0:1])
            return c
        lax.fori_loop(0, 4, norm_one, 0, unroll=4)
        self.load.self_qkv.wait()
        for copy in (load.memory_keys, load.memory_values, load.self_out, load.cross_q, load.cross_out, load.cotangent):
            copy.start()
        for copy in self.ff_loads(0) + self.ff_loads(1):
            copy.start()

        def qkv_tile(j, c):
            at = self.q_rows(j, 768)
            right[:, pl.ds(pl.multiple_of(QKV + j * 768, 768), 768)] = nn(self.hid[...], self.self_qkv[:, at]).astype(BF16)
            return c
        lax.fori_loop(0, 3, qkv_tile, 0, unroll=3)

        self.load.encodings.wait()
        self.load.cross_kv.wait()
        enc_rows = self.questions * self.enc_len

        def ekv_tile(j, c):
            at = self.q_rows(j, 768)
            col = pl.ds(pl.multiple_of(EKV + j * 768, 768), 768)
            right[0:enc_rows, col] = nn(self.encodings[...], self.cross_kv[:, at]).astype(BF16)
            return c
        lax.fori_loop(0, 2, ekv_tile, 0, unroll=2)
        self.load.memory_keys.wait()
        self.load.memory_values.wait()
        self.memory_rows()
        m0, m1, _ = head_masks()
        allowed = self.causal()

        def self_attention(q, c):
            at = self.q_rows(q)
            for p in range(6):
                lo = p * LANES
                q2, k2, v2 = (right[at, QKV + 768 * i + lo:QKV + 768 * i + lo + LANES] for i in range(3))
                probs = self.self_probs(q2, stacked(k2, m0, m1), p, allowed).astype(BF16)
                self.att[at, lo:lo + LANES] = nn(probs, stacked(v2, m0, m1)).astype(BF16)
            return c
        lax.fori_loop(0, 4, self_attention, 0, unroll=4)

        self.load.self_out.wait()

        def out_tile(j, c):
            at = self.q_rows(j, 768)
            self.y1[:, at] = self.tokens[:, at].astype(F32) + nn(self.att[...], self.self_out[:, at])
            return c
        lax.fori_loop(0, 1, out_tile, 0, unroll=1)

        def norm_two(q, c):
            at = self.q_rows(q)
            self.hid[at] = normed(self.y1[at], self.gains[1:2])
            return c
        lax.fori_loop(0, 4, norm_two, 0, unroll=4)
        self.load.cross_q.wait()

        def cq_tile(j, c):
            at = self.q_rows(j, 768)
            right[:, pl.ds(pl.multiple_of(CQ + j * 768, 768), 768)] = nn(self.hid[...], self.cross_q[:, at]).astype(BF16)
            return c
        lax.fori_loop(0, 1, cq_tile, 0, unroll=1)
        present = self.present()

        def cross_attention(q, c):
            at = self.q_rows(q)
            for p in range(6):
                lo = p * LANES
                keys = self.cross_side(q, p, self.mem_k, EKV)
                vals = self.cross_side(q, p, self.mem_v, EKV + 768)
                probs = self.cross_probs(right[at, CQ + lo:CQ + lo + LANES], stacked(keys, m0, m1), present)
                self.att2[at, lo:lo + LANES] = nn(probs.astype(BF16), stacked(vals, m0, m1)).astype(BF16)
            return c
        lax.fori_loop(0, 4, cross_attention, 0, unroll=4)
        self.load.cross_out.wait()

        def out2_tile(j, c):
            at = self.q_rows(j, 768)
            self.y2[:, at] = self.y1[:, at] + nn(self.att2[...], self.cross_out[:, at])
            return c
        lax.fori_loop(0, 1, out2_tile, 0, unroll=1)
        self.load.cotangent.wait()

        def norm_three(q, c):
            at = self.q_rows(q)
            h3 = normed(self.y2[at], self.gains[2:3])
            self.hid[at] = h3
            self.put_left(L_H3, q, h3)
            valid = lax.broadcasted_iota(jnp.int32, (LANES, 1), 0) < self.lengths[q]
            cot = jnp.where(valid, self.cotangent[at].astype(F32), 0.0)
            right[at, E3:E3 + 768] = cot.astype(BF16)
            return c
        lax.fori_loop(0, 4, norm_three, 0, unroll=4)

    def feed_forward(self):
        right = self.right
        self.y3[...] = self.y2[...]
        self.dh3[...] = jnp.zeros_like(self.dh3)

        def tile(j, c):
            slot = lax.rem(j, 2)
            for copy in self.ff_loads(j):
                copy.wait()
            for i in range(0, self.rows, 256):
                at = slice(i, i + 256)
                z = nn(self.hid[at], self.wi[slot])
                dr = nt(right[at, E3:E3 + 768], self.wo[slot]).astype(BF16).astype(F32)
                cdf = 0.5 * (1.0 + lax.erf(z * 0.7071067811865476))
                pdf = jnp.exp(-0.5 * z * z) * 0.3989422804014327
                self.act[at] = (z * cdf).astype(BF16)
                self.dz[at] = (dr * (cdf + z * pdf)).astype(BF16)
            act = self.act[...]
            dz = self.dz[...]

            self.advance(j, 0, lambda: dz)
            turned = act.T
            for g in range(4):
                at = pl.ds(pl.multiple_of((j // 2) * 96, 96), 96)
                self.left[L_R + g, lax.rem(j, 2), at, :] = turned[g * 96:(g + 1) * 96]
            self.y3[...] += nn(act, self.wo[slot])
            self.dh3[...] += nt(dz, self.wi[slot])

            @pl.when(j + 2 < 8)
            def _():
                for copy in self.ff_loads(j + 2):
                    copy.start()
            return c
        lax.fori_loop(0, 8, tile, 0)

        def finish(q, c):
            at = self.q_rows(q)
            valid = lax.broadcasted_iota(jnp.int32, (LANES, 1), 0) < self.lengths[q]
            self.layer_output[at] = jnp.where(valid, self.y3[at], 0.0).astype(BF16)
            return c
        lax.fori_loop(0, 4, finish, 0, unroll=4)
        self.stores()[0].start()

    def stores(self):
        return [pltpu.make_async_copy(vars(self)[name], vars(self.out)[name], sem) for name, sem in vars(self.store).items()]

    def put_lefts(self, index, rows):
        turned = rows.T
        for b in range(8):
            self.left[index, b % 2, (b // 2) * 96:(b // 2 + 1) * 96, 0:rows.shape[0]] = turned[b * 96:(b + 1) * 96]

    def row_blocks(self):
        return [slice(q * LANES, (q + 1) * LANES) for q in range(self.questions)]

    def in_steps(self, first, parts):
        count = sum(n for n, _ in parts)

        def step(i, c):
            at = 0
            for n, part in parts:
                pl.when((i >= at) & (i < at + n))(functools.partial(part, i - at))
                at += n
            self.advance(first + i)
            return c
        lax.fori_loop(0, count, step, 0)

    def backward_cross(self):
        right = self.right
        m0, m1, low_lanes = head_masks()
        present = self.present()
        enc_rows = self.questions * self.enc_len

        def pick(both):
            return jnp.where(low_lanes, both[:LANES], both[LANES:])

        def before(_):
            total = jnp.zeros((1, 768), F32)
            for at in self.row_blocks():
                back, gain = norm_pull(self.y2[at], self.gains[2:3], self.dh3[at])
                total += gain
                e2 = right[at, E3:E3 + 768].astype(F32) + back
                self.y3[at] = e2
                right[at, B2:B2 + 768] = e2.astype(BF16)
            self.dgains[2:3] = total
            self.up[...] = nt(right[:, B2:B2 + 768], self.cross_out[...]).astype(BF16)

        def attention(q):
            at = self.q_rows(q)
            enc_at = self.q_rows(q, self.enc_len)
            mem_at = self.q_rows(q, MEM_PAD)
            for p in range(6):
                lo = p * LANES
                pair = slice(lo, lo + LANES)
                keys = stacked(self.cross_side(q, p, self.mem_k, EKV), m0, m1)
                vals = stacked(self.cross_side(q, p, self.mem_v, EKV + 768), m0, m1)
                cq = right[at, CQ + lo:CQ + lo + LANES]
                probs = self.cross_probs(cq, keys, present)
                up = self.up[at, pair]
                dvals = pick(tn(probs.astype(BF16), up))
                ds = pair_pull(probs, nt(up, vals))
                dkeys = pick(tn(ds, cq))
                right[at, CQ + lo:CQ + lo + LANES] = nn(ds, keys).astype(BF16)
                right[enc_at, EKV + lo:EKV + lo + LANES] = dkeys[:64].astype(BF16)
                right[enc_at, EKV + 768 + lo:EKV + 768 + lo + LANES] = dvals[:64].astype(BF16)
                self.dmem_k[mem_at, pair] = dkeys[64:64 + MEM_PAD]
                self.dmem_v[mem_at, pair] = dvals[64:64 + MEM_PAD]

        def after(_):
            self.dh3[...] = nt(right[:, CQ:CQ + 768], self.cross_q[...])
            total = jnp.zeros((1, 768), F32)
            for at in self.row_blocks():
                back, gain = norm_pull(self.y1[at], self.gains[1:2], self.dh3[at])
                total += gain
                self.y3[at] += back
            self.dgains[1:2] = total

        def turn(_):
            for at in self.row_blocks():
                self.hid[at] = normed(self.y1[at], self.gains[1:2])
            self.put_lefts(L_H2, self.hid[...])
            self.put_lefts(L_O2, self.att2[...])

        def encodings(_):
            self.put_lefts(L_ENC, self.encodings[...])
            self.left[L_ENC, :, :, enc_rows:] = jnp.zeros((2, 384, self.rows - enc_rows), BF16)
            right[enc_rows:, EKV:EKV + 1536] = jnp.zeros((self.rows - enc_rows, 1536), BF16)
            self.grad_encodings[...] = nt(right[0:enc_rows, EKV:EKV + 1536], self.cross_kv[...]).astype(BF16)

        self.in_steps(8, ((1, before), (4, attention), (1, after), (1, turn), (1, encodings)))

    def backward_self(self):
        right = self.right
        m0, m1, low_lanes = head_masks()
        allowed = self.causal()

        def pick(both):
            return jnp.where(low_lanes, both[:LANES], both[LANES:])

        def before(_):
            self.dbias[...] = jnp.zeros_like(self.dbias)
            right[:, B1:B1 + 768] = self.y3[...].astype(BF16)
            self.up[...] = nt(right[:, B1:B1 + 768], self.self_out[...]).astype(BF16)

        def attention(q):
            at = self.q_rows(q)
            for p in range(6):
                lo = p * LANES
                q2, k2, v2 = (right[at, QKV + 768 * i + lo:QKV + 768 * i + lo + LANES] for i in range(3))
                keys = stacked(k2, m0, m1)
                probs = self.self_probs(q2, keys, p, allowed)
                up = self.up[at, lo:lo + LANES]
                dval = pick(tn(probs.astype(BF16), up))
                ds = pair_pull(probs, nt(up, stacked(v2, m0, m1)))
                self.dbias[p] += ds.astype(F32)
                right[at, QKV + lo:QKV + lo + LANES] = nn(ds, keys).astype(BF16)
                right[at, QKV + 768 + lo:QKV + 768 + lo + LANES] = pick(tn(ds, q2)).astype(BF16)
                right[at, QKV + 1536 + lo:QKV + 1536 + lo + LANES] = dval.astype(BF16)

        def after(_):
            self.dh3[...] = nt(right[:, QKV:QKV + 2304], self.self_qkv[...])

        def finish(_):
            total = jnp.zeros((1, 768), F32)
            for at in self.row_blocks():
                tok = self.tokens[at].astype(F32)
                back, gain = norm_pull(tok, self.gains[0:1], self.dh3[at])
                total += gain
                self.grad_tokens[at] = (self.y3[at] + back).astype(BF16)
            self.dgains[0:1] = total

        def turn(_):
            for at in self.row_blocks():
                self.hid[at] = normed(self.tokens[at].astype(F32), self.gains[0:1])
            self.put_lefts(L_H1, self.hid[...])
            self.put_lefts(L_O, self.att[...])

        self.in_steps(16, ((1, before), (4, attention), (1, after), (1, finish), (1, turn)))
        for copy in self.stores()[1:]:
            copy.start()

    def bias_rows(self):
        row = lax.broadcasted_iota(jnp.int32, (LANES, LANES), 0)
        col = lax.broadcasted_iota(jnp.int32, (LANES, LANES), 1)
        flip = jnp.where(row + col == LANES - 1, 1.0, 0.0)
        out = []
        for p in range(6):
            turned = nn(flip, self.dbias[p], precision=lax.Precision.HIGHEST)
            for k in range(2):
                rolled = pltpu.roll(turned[:, k * LANES:(k + 1) * LANES], 0, 1, stride=1, stride_axis=0)
                out.append(jnp.sum(rolled, axis=0, keepdims=True))
        return out

    def spread_ids(self, width):
        slot = lax.broadcasted_iota(jnp.int32, (4 * MEM_PAD, width), 0)
        wanted = jnp.full((4 * MEM_PAD, width), -1, jnp.int32)
        for q in range(self.questions):
            for i in range(self.ids.shape[1]):
                wanted = jnp.where(slot == q * MEM_PAD + i, self.ids[q, i], wanted)
        return wanted

    def advance(self, t, fixed=None, right=None):
        left, value = self.place(t)
        if fixed is not None:
            left, value = fixed, right

        def product(parity):
            return nn(self.left[left, parity], value())
        self.reducer.step(t, product)

    def place(self, d):
        u = d - 16
        late = jnp.where(u < 4, 1 + u // 2, jnp.where(u < 8, 3, jnp.where(u < 10, 4, 5)))
        left = jnp.where(d < 16, L_R + (d - 8) // 2, late)
        col = pl.multiple_of(jnp.where(d < 16, E3 + lax.rem(d, 2) * 384, B2 + u * 384), LANES)
        return left, lambda: self.right[:, pl.ds(col, 384)]


MESH_ID = pl.DeviceIdType.MESH
CHUNK_ROWS, CHUNK_COLS, PAIR_ROWS, SMALL_ROWS = 96, 384, 48, 48
PERIOD, GAP, LAST_PAIR, SMALL_FROM, LAST = 5, 26, 21, 29, 37
CHUNKS, SPLIT = 32, 4
DEPTH = Bunch(own=12, mid=10, snd=3, r0=3, rp=2, r1=6, r2=5, r3=5, r4=5)
LAG = Bunch(one=1, two=3, three=2, four=2, five=2, six=3)
LATE = Bunch(one=1, two=3, three=2, four=2, five=3, six=3)


def after(lags):
    return list(itertools.accumulate(vars(lags).values()))


def data_of(k):
    pair = (lax.rem(k, PERIOD) == 1) & (k <= GAP)
    return jnp.where(pair, k - PERIOD, jnp.where(k > GAP, k - 1, k))


class Reducer:
    def __init__(self, bufs, sems, out_ref):
        self.b, self.s, self.out = bufs, sems, out_ref
        dp, z = lax.axis_index("dp"), lax.axis_index("replica")
        here = Bunch(dp=dp, replica=z)
        self.core = lax.rem(dp, 2)
        self.x = lax.rem(dp // 2, 2)
        self.y = dp // 4
        self.inner = lax.rem((z + 1) // 2, 2) == 1
        self.end = lax.rem((z + 1) // 2, 2) == 0
        self.near = pl.multiple_of(PAIR_ROWS * lax.rem(z, 2), PAIR_ROWS)
        self.far = pl.multiple_of(PAIR_ROWS * (1 - lax.rem(z, 2)), PAIR_ROWS)
        self.to_core = dict(vars(here), dp=dp + 1 - 2 * self.core)
        self.to_x = dict(vars(here), dp=dp + 2 - 4 * self.x)
        self.to_y = dict(vars(here), dp=dp + 4 - 8 * self.y)
        self.to_pair = dict(vars(here), replica=z + 1 - 2 * lax.rem(z, 2))
        self.to_mid = dict(vars(here), replica=3 - z)

    def enter(self):
        bar = pltpu.get_barrier_semaphore()
        for target in (self.to_core, self.to_x, self.to_y, self.to_pair, self.to_mid):
            pl.semaphore_signal(bar, inc=1, device_id=target, device_id_type=MESH_ID)

    def entered(self):
        pl.semaphore_wait(pltpu.get_barrier_semaphore(), 5)

    def copy(self, src, dst, send, recv, target):
        return pltpu.make_async_remote_copy(
            src_ref=src, dst_ref=dst, send_sem=send, recv_sem=recv, device_id=target, device_id_type=MESH_ID)

    def core_copy(self, k, n):
        a, r, rows = lax.rem(k, DEPTH.snd), lax.rem(k, DEPTH.r0), pl.ds(0, n)
        return self.copy(self.b.snd.at[a, :, rows], self.b.r0.at[r, :, rows], self.s.snd.at[a], self.s.r0.at[r],
                         self.to_core)

    def pair_copy(self, d):
        o, r = lax.rem(d + PERIOD, DEPTH.own), lax.rem(d // PERIOD, DEPTH.rp)
        return self.copy(self.b.own.at[o, :, :, pl.ds(self.far, PAIR_ROWS)], self.b.rp.at[r], self.s.sp.at[r],
                         self.s.rp.at[r], self.to_pair)

    def first_copies(self, k, n, base):
        o, r = lax.rem(k, DEPTH.own), lax.rem(k, DEPTH.r1)
        half = n // 2
        low, high, into = pl.ds(base, half), pl.ds(base + half, half), pl.ds(0, half)
        return (
            self.copy(self.b.own.at[o, :, 1 - self.x, low], self.b.r1x.at[r, :, into], self.s.s1x.at[r],
                      self.s.r1x.at[r], self.to_x),
            self.copy(self.b.own.at[o, 1 - self.y, :, high], self.b.r1y.at[r, :, into], self.s.s1y.at[r],
                      self.s.r1y.at[r], self.to_y),
        )

    def second_copies(self, k, n, base):
        o, r = lax.rem(k, DEPTH.own), lax.rem(k, DEPTH.r2)
        half = n // 2
        low, high, into = pl.ds(base, half), pl.ds(base + half, half), pl.ds(0, half)
        return (
            self.copy(self.b.own.at[o, self.y, 1 - self.x, high], self.b.r2x.at[r, into], self.s.s2x.at[r],
                      self.s.r2x.at[r], self.to_x),
            self.copy(self.b.own.at[o, 1 - self.y, self.x, low], self.b.r2y.at[r, into], self.s.s2y.at[r],
                      self.s.r2y.at[r], self.to_y),
        )

    def mine(self, k, n, base=0):
        return self.b.mid.at[lax.rem(k, DEPTH.mid), pl.ds(base, n)]

    def inward_copy(self, k, n, base):
        r = lax.rem(k, DEPTH.r3)
        return self.copy(self.mine(k, n, base), self.b.r3.at[r, pl.ds(0, n)], self.s.s3.at[r], self.s.r3.at[r],
                         self.to_pair)

    def middle_copy(self, k, n):
        r = lax.rem(k, DEPTH.r4)
        return self.copy(self.mine(k, n), self.b.r4.at[r, pl.ds(0, n)], self.s.s4.at[r], self.s.r4.at[r], self.to_mid)

    def result(self, k, n):
        if n == SMALL_ROWS:
            sums, u = k == SMALL_FROM, k - SMALL_FROM - 1
            row, d = jnp.where(sums, 0, lax.rem(u + 2, 2) * SMALL_ROWS), jnp.where(sums, CHUNKS, CHUNKS - SPLIT + u // 2)
        else:
            row, d = 0, data_of(k)
        return self.out.at[pl.ds(pl.multiple_of(row, 8), n), pl.ds(pl.multiple_of(d * CHUNK_COLS, LANES), CHUNK_COLS)]

    def outward_copy(self, k, n):
        r = lax.rem(k, DEPTH.r4)
        return self.copy(self.mine(k, n), self.result(k, n), self.s.s5.at[r], self.s.out.at[k], self.to_pair)

    def keep_copy(self, k, n):
        return pltpu.make_async_copy(self.mine(k, n), self.result(k, n), self.s.out.at[k])

    def grant(self, sem, k, depth, target):
        @pl.when(k + depth <= LAST)
        def _():
            pl.semaphore_signal(sem, inc=1, device_id=target, device_id_type=MESH_ID)

    def need(self, sem, k, depth):
        @pl.when((k >= depth) & (k != depth + 1))
        def _():
            pl.semaphore_wait(sem, 1)

    def before(self, t):
        return t - jnp.where(t == GAP + DEPTH.snd, 2 * DEPTH.snd, DEPTH.snd)

    def fill(self, t, half_product):
        n = CHUNK_ROWS
        early = (lax.rem(t, PERIOD) == 1) & (t <= LAST_PAIR)
        a, o = lax.rem(t, DEPTH.snd), lax.rem(jnp.where(early, t + PERIOD, t), DEPTH.own)

        @pl.when(t >= DEPTH.snd)
        def _():
            self.core_copy(self.before(t), n).wait_send()

        away = half_product(1 - self.core)
        for g in range(4):
            self.b.snd[a, g] = away[g * n:(g + 1) * n]

        @pl.when((t >= DEPTH.r0) & (t != GAP + DEPTH.r0))
        def _():
            pl.semaphore_wait(self.s.c0, 1)
        self.core_copy(t, n).start()
        here = half_product(self.core)
        for g in range(4):
            self.b.own[o, g // 2, g % 2] = here[g * n:(g + 1) * n]

    def fill_small(self, k, part):
        n = SMALL_ROWS
        a, o = lax.rem(k, DEPTH.snd), lax.rem(k, DEPTH.own)

        @pl.when(k - DEPTH.snd < SMALL_FROM)
        def _():
            self.core_copy(self.before(k), CHUNK_ROWS).wait_send()

        @pl.when(k - DEPTH.snd >= SMALL_FROM)
        def _():
            self.core_copy(k - DEPTH.snd, n).wait_send()
        self.b.snd[a, :, 0:n, :] = part(1 - self.core)

        @pl.when(k != GAP + DEPTH.r0)
        def _():
            pl.semaphore_wait(self.s.c0, 1)
        self.core_copy(k, n).start()
        here = part(self.core)
        for g in range(4):
            self.b.own[o, g // 2, g % 2, 0:n, :] = here[g]

    def add_core(self, d, o, n):
        r = lax.rem(d, DEPTH.r0)
        self.core_copy(d, n).wait_recv()
        for g in range(4):
            self.b.own[o, g // 2, g % 2, 0:n] += self.b.r0[r, g, 0:n]

        @pl.when((d + DEPTH.r0 <= LAST) & (d + DEPTH.r0 != GAP))
        def _():
            pl.semaphore_signal(self.s.c0, inc=1, device_id=self.to_core, device_id_type=MESH_ID)

    def start_first(self, k, n, base):
        self.need(self.s.c1x, k, DEPTH.r1)
        self.need(self.s.c1y, k, DEPTH.r1)
        for copy in self.first_copies(k, n, base):
            copy.start()

    def stage_one(self, k, n):
        self.add_core(k, lax.rem(k, DEPTH.own), n)
        self.start_first(k, n, 0)

    def stage_pair(self, d):
        self.add_core(d, lax.rem(d + PERIOD, DEPTH.own), CHUNK_ROWS)

        @pl.when(d // PERIOD >= DEPTH.rp)
        def _():
            pl.semaphore_wait(self.s.cp, 1)
        self.pair_copy(d).start()

    def stage_one_pair(self, k):
        d = k - PERIOD
        o, r = lax.rem(k, DEPTH.own), lax.rem(d // PERIOD, DEPTH.rp)
        self.pair_copy(d).wait()
        rows = pl.ds(self.near, PAIR_ROWS)
        for g in range(4):
            self.b.own[o, g // 2, g % 2, rows] += self.b.rp[r, g // 2, g % 2]

        @pl.when(d + DEPTH.rp * PERIOD <= LAST_PAIR)
        def _():
            pl.semaphore_signal(self.s.cp, inc=1, device_id=self.to_pair, device_id_type=MESH_ID)
        self.start_first(k, PAIR_ROWS, self.near)

    def stage_two(self, k, n, base):
        o, r, half = lax.rem(k, DEPTH.own), lax.rem(k, DEPTH.r1), n // 2
        low, high = pl.ds(base, half), pl.ds(base + half, half)
        by_x, by_y = self.first_copies(k, n, base)
        by_x.wait_recv()
        for g in range(2):
            self.b.own[o, g, self.x, low, :] += self.b.r1x[r, g, 0:half]
        by_y.wait_recv()
        for g in range(2):
            self.b.own[o, self.y, g, high, :] += self.b.r1y[r, g, 0:half]
        self.grant(self.s.c1x, k, DEPTH.r1, self.to_x)
        self.grant(self.s.c1y, k, DEPTH.r1, self.to_y)
        by_x.wait_send()
        by_y.wait_send()
        self.need(self.s.c2x, k, DEPTH.r2)
        self.need(self.s.c2y, k, DEPTH.r2)
        for copy in self.second_copies(k, n, base):
            copy.start()

    def stage_three(self, k, n, base):
        o, r, half = lax.rem(k, DEPTH.own), lax.rem(k, DEPTH.r2), n // 2
        low, high = pl.ds(base, half), pl.ds(base + half, half)
        m = lax.rem(k, DEPTH.mid)
        by_x, by_y = self.second_copies(k, n, base)
        by_x.wait_recv()
        self.b.mid[m, high, :] = self.b.own[o, self.y, self.x, high, :] + self.b.r2x[r, 0:half]
        by_y.wait_recv()
        self.b.mid[m, low, :] = self.b.own[o, self.y, self.x, low, :] + self.b.r2y[r, 0:half]
        self.grant(self.s.c2x, k, DEPTH.r2, self.to_x)
        self.grant(self.s.c2y, k, DEPTH.r2, self.to_y)
        by_x.wait_send()
        by_y.wait_send()

        @pl.when(self.end)
        def _():
            self.need(self.s.c3, k, DEPTH.r3)
            self.inward_copy(k, n, base).start()

    def stage_four(self, k, n, paired):
        r = lax.rem(k, DEPTH.r3)
        part = PAIR_ROWS if paired else n

        @pl.when(self.end)
        def _():
            self.inward_copy(k, part, self.near if paired else 0).wait_send()

        @pl.when(self.inner)
        def _():
            self.inward_copy(k, part, 0).wait_recv()
            if paired:
                self.b.mid[lax.rem(k, DEPTH.mid), pl.ds(self.far, part), :] = self.b.r3[r, 0:part]
            else:
                self.mine(k, n)[...] += self.b.r3[r, 0:n]
            self.grant(self.s.c3, k, DEPTH.r3, self.to_pair)
            self.need(self.s.c4, k, DEPTH.r4)
            self.middle_copy(k, n).start()

    def stage_five(self, k, n):
        r = lax.rem(k, DEPTH.r4)

        @pl.when(self.inner)
        def _():
            self.middle_copy(k, n).wait()
            self.mine(k, n)[...] += self.b.r4[r, 0:n]
            self.grant(self.s.c4, k, DEPTH.r4, self.to_mid)
            self.outward_copy(k, n).start()
            self.keep_copy(k, n).start()

    def stage_six(self, k, n):
        @pl.when(self.inner)
        def _():
            self.outward_copy(k, n).wait_send()
        self.keep_copy(k, n).wait()

    def stages(self):
        n, small, pair = CHUNK_ROWS, SMALL_ROWS, PAIR_ROWS
        return (
            (lambda k: self.stage_one(k, n), self.stage_one_pair, lambda k: self.stage_one(k, small)),
            (lambda k: self.stage_two(k, n, 0), lambda k: self.stage_two(k, pair, self.near),
             lambda k: self.stage_two(k, small, 0)),
            (lambda k: self.stage_three(k, n, 0), lambda k: self.stage_three(k, pair, self.near),
             lambda k: self.stage_three(k, small, 0)),
            (lambda k: self.stage_four(k, n, False), lambda k: self.stage_four(k, n, True),
             lambda k: self.stage_four(k, small, False)),
            (lambda k: self.stage_five(k, n), None, lambda k: self.stage_five(k, small)),
            (lambda k: self.stage_six(k, n), None, lambda k: self.stage_six(k, small)),
        )

    def move(self, t):
        for behind, (usual, paired, small) in reversed(list(zip(after(LAG), self.stages()))):
            k = t - behind
            odd = (lax.rem(k + PERIOD, PERIOD) == 1) & (k <= GAP)
            if paired is None:
                pl.when((k >= 0) & (k < SMALL_FROM) & (k != 1))(functools.partial(usual, k))
            else:
                pl.when((k >= 0) & (k < SMALL_FROM) & jnp.logical_not(odd))(functools.partial(usual, k))
                pl.when(odd & (k > 1))(functools.partial(paired, k))
            pl.when((k >= SMALL_FROM) & (k <= LAST))(functools.partial(small, k))
        d = t - LAG.one
        pl.when((lax.rem(d + PERIOD, PERIOD) == 1) & (d >= 0) & (d <= LAST_PAIR))(functools.partial(self.stage_pair, d))

    def drain(self):
        left = []
        for number, (due, order) in enumerate(zip(after(LAG), after(LATE))):
            left += [(k + order, -number, k) for k in range(LAST + 1) if k + due > LAST]
        for _, number, k in sorted(left):
            usual, paired, small = self.stages()[-number]
            odd = k % PERIOD == 1 and k <= GAP
            (small if k >= SMALL_FROM else paired if odd and paired is not None else usual)(jnp.int32(k))

    def step(self, t, half_product):
        self.move(t)
        self.fill(t, half_product)

    def finish(self, half, small):
        self.move(SMALL_FROM)
        self.fill_small(jnp.int32(SMALL_FROM), lambda parity: small[parity])

        def body(k, c):
            self.move(k)
            self.fill_small(k, lambda parity: half(parity, k - SMALL_FROM - 1))
            return c
        lax.fori_loop(SMALL_FROM + 1, LAST + 1, body, 0)
        self.drain()
        for back in range(DEPTH.snd):
            self.core_copy(LAST - back, SMALL_ROWS).wait_send()


def reducer_scratch():
    rows, cols, half, count, d = CHUNK_ROWS, CHUNK_COLS, CHUNK_ROWS // 2, LAST + 1, DEPTH
    vmem = lambda *shape: pltpu.VMEM(shape, jnp.float32)
    dma = lambda n: pltpu.SemaphoreType.DMA((n,))
    plain = pltpu.SemaphoreType.REGULAR
    bufs = Bunch(
        own=vmem(d.own, 2, 2, rows, cols), mid=vmem(d.mid, rows, cols), snd=vmem(d.snd, 4, rows, cols),
        r0=vmem(d.r0, 4, rows, cols), rp=vmem(d.rp, 2, 2, PAIR_ROWS, cols), r1x=vmem(d.r1, 2, half, cols),
        r1y=vmem(d.r1, 2, half, cols), r2x=vmem(d.r2, half, cols), r2y=vmem(d.r2, half, cols),
        r3=vmem(d.r3, rows, cols), r4=vmem(d.r4, rows, cols))
    sems = Bunch(
        snd=dma(d.snd), r0=dma(d.r0), sp=dma(d.rp), rp=dma(d.rp), out=dma(count), s1x=dma(d.r1), r1x=dma(d.r1),
        s1y=dma(d.r1), r1y=dma(d.r1), s2x=dma(d.r2), r2x=dma(d.r2), s2y=dma(d.r2), r2y=dma(d.r2), s3=dma(d.r3),
        r3=dma(d.r3), s4=dma(d.r4), r4=dma(d.r4), s5=dma(d.r4), c0=plain, cp=plain, c1x=plain, c1y=plain, c2x=plain,
        c2y=plain, c3=plain, c4=plain)
    return bufs, sems


class PartWriter:
    def __init__(self, bufs, sems, out_ref):
        self.b, self.s, self.out = bufs, sems, out_ref

    def enter(self):
        pass

    def entered(self):
        pass

    def step(self, t, half_product):
        for parity in range(2):
            value = half_product(parity)
            for g in range(4):
                self.b.own[parity, g // 2, g % 2] = value[g * 96:(g + 1) * 96]
        copy = pltpu.make_async_copy(self.b.own, self.out.at[t], self.s.out.at[0])
        copy.start()
        copy.wait()


def regroup(groups, refs):
    result, first = [], 0
    for names in groups:
        result.append(Bunch(**dict(zip(names, refs[first:first + len(names)]))))
        first += len(names)
    return result


def layer_kernel(groups, alone, *refs):
    hbm, out, vm, load, store, bufs, sems = regroup(groups, refs)
    reducer = (PartWriter if alone else Reducer)(bufs, sems, out.chunks)
    layer = Layer(hbm, out, vm, load, store)
    layer.reducer = reducer
    layer.forward(reducer.enter)
    reducer.entered()
    layer.feed_forward()
    layer.backward_cross()
    layer.backward_self()

    if alone:
        def body(t, c):
            layer.advance(t)
            return c
        lax.fori_loop(24, CHUNKS, body, 0)
        entries = vm.memory_keys.shape[0]
        entry = lax.broadcasted_iota(jnp.int32, (4 * MEM_PAD, entries), 1)
        hit = jnp.where(layer.spread_ids(entries) == entry, 1.0, 0.0)
        out.mem_k[...] = tn(hit, vm.dmem_k[...], precision=lax.Precision.HIGHEST)
        out.mem_v[...] = tn(hit, vm.dmem_v[...], precision=lax.Precision.HIGHEST)
        out.gains[...] = vm.dgains[...]
        for h, row in enumerate(layer.bias_rows()):
            out.bias[h:h + 1, :] = row
    else:
        fill_small_rows(layer, vm)

        def body(t, c):
            left, value = layer.place(jnp.where(t > GAP, t - 1, t))
            reducer.move(t)

            @pl.when(t != GAP)
            def _():
                reducer.fill(t, lambda parity: nn(vm.left[left, parity], value()))
            return c
        lax.fori_loop(24, SMALL_FROM, body, 0)

        def half(parity, u):
            left, value = layer.place(CHUNKS - SPLIT + u // 2)
            at = lambda g: pl.ds(pl.multiple_of(g * 96 + lax.rem(u, 2) * SMALL_ROWS, SMALL_ROWS), SMALL_ROWS)
            rows = jnp.concatenate([vm.left[left, parity, at(g)] for g in range(4)], axis=0)
            return nn(rows, value()).reshape(4, SMALL_ROWS, CHUNK_COLS)
        reducer.finish(half, vm.small)
    for copy in layer.stores():
        copy.wait()


def fill_small_rows(layer, vm):
    out_row = lax.broadcasted_iota(jnp.int32, (4 * MEM_PAD, 64), 1)
    entry = 4 * (out_row // 8) + lax.rem(out_row, 4)
    same = layer.spread_ids(64) == entry
    keys_row = lax.rem(out_row // 4, 2) == 0
    hit_k = jnp.where(same & keys_row, 1.0, 0.0)
    hit_v = jnp.where(same & jnp.logical_not(keys_row), 1.0, 0.0)
    memory = (tn(hit_k, vm.dmem_k[...], precision=lax.Precision.HIGHEST)
              + tn(hit_v, vm.dmem_v[...], precision=lax.Precision.HIGHEST))
    bias = jnp.concatenate(layer.bias_rows() + [jnp.zeros((4, LANES), F32)], axis=0)
    gains = jnp.concatenate([vm.dgains[...], jnp.zeros((5, 768), F32)], axis=0)
    for b in range(8):
        block = vm.small.at[b % 2, b // 2]
        for j in range(6):
            row, col = 8 * (j % 4), LANES * (j // 4)
            block[row:row + 8, col:col + LANES] = memory[8 * b:8 * b + 8, j * LANES:(j + 1) * LANES]
        turned = gains if b == 0 else pltpu.roll(gains, 768 - 96 * b, 1)
        block[16:24, LANES:2 * LANES] = turned[:, :LANES]
        block[24:32, LANES:2 * LANES] = jnp.zeros((8, LANES), F32)
        block[0:16, 2 * LANES:] = bias
        block[16:32, 2 * LANES:] = jnp.zeros((16, LANES), F32)
        block[32:, :] = jnp.zeros((SMALL_ROWS - 32, CHUNK_COLS), F32)


def call_grouped(kernel, ins, outs, scratch, **options):
    groups = [list(vars(g)) for g in ins + outs + scratch]
    pairs = lambda gs, i: [v[i] for g in gs for v in vars(g).values()]
    space = lambda gs: [pl.BlockSpec(memory_space=s) for s in pairs(gs, 1)]
    result = pl.pallas_call(
        functools.partial(kernel, groups), out_shape=pairs(outs, 0), in_specs=space(ins), out_specs=space(outs),
        scratch_shapes=[v for g in scratch for v in vars(g).values()], **options)(*pairs(ins, 0))
    return regroup(groups[len(ins):len(ins) + len(outs)], result)[0]


def in_space(space, **values):
    return Bunch(**{name: (value, space) for name, value in values.items()})


def run_layer(alone, hbm):
    rows, width = hbm.tokens.shape
    enc_rows = hbm.encodings.shape[0]
    entries = hbm.memory_keys.shape[0]
    shape = jax.ShapeDtypeStruct
    outs = in_space(pl.ANY, layer_output=shape((rows, width), BF16), grad_tokens=shape((rows, width), BF16),
                    grad_encodings=shape((enc_rows, width), BF16))
    if alone:
        part = shape((entries, width), F32)
        vars(outs).update(vars(in_space(pl.ANY, chunks=shape((CHUNKS, 2, 2, 2, CHUNK_ROWS, CHUNK_COLS), F32))))
        vars(outs).update(vars(in_space(pltpu.VMEM, mem_k=part, mem_v=part, gains=shape((3, width), F32),
                                        bias=shape((12, LANES), F32))))
    else:
        vars(outs).update(vars(in_space(pl.ANY, chunks=shape((CHUNK_ROWS, (CHUNKS + 1) * CHUNK_COLS), F32))))
    loaded = [name for name in vars(hbm) if vars(hbm)[name] is not hbm.ff_in and vars(hbm)[name] is not hbm.ff_out]
    place_of = lambda v: (pltpu.SMEM if v.dtype == jnp.int32 else pltpu.VMEM)(v.shape, v.dtype)
    vm = Bunch(**{name: place_of(vars(hbm)[name]) for name in loaded})
    big = lambda cols, kind: pltpu.VMEM((rows, cols), kind)
    vars(vm).update(
        wi=pltpu.VMEM((2, width, FF_TILE), BF16), wo=pltpu.VMEM((2, FF_TILE, width), BF16),
        hid=big(width, BF16), att=big(width, BF16), att2=big(width, BF16), right=big(RIGHT, BF16),
        left=pltpu.VMEM((10, 2, 384, rows), BF16),
        y1=big(width, F32), y2=big(width, F32), y3=big(width, F32), dh3=big(width, F32),
        act=big(FF_TILE, BF16), dz=big(FF_TILE, BF16),
        bias=pltpu.VMEM((6, LANES, 2 * LANES), F32), dbias=pltpu.VMEM((6, LANES, 2 * LANES), F32),
        gains=pltpu.VMEM((3, width), F32), dgains=pltpu.VMEM((3, width), F32), up=big(width, BF16),
        mem_k=pltpu.VMEM((4, MEM_PAD, width), BF16), mem_v=pltpu.VMEM((4, MEM_PAD, width), BF16),
        dmem_k=pltpu.VMEM((4 * MEM_PAD, width), F32), dmem_v=pltpu.VMEM((4 * MEM_PAD, width), F32),
        grad_encodings=pltpu.VMEM((enc_rows, width), BF16),
        wi_sem=pltpu.SemaphoreType.DMA((2,)), wo_sem=pltpu.SemaphoreType.DMA((2,)))
    one = pltpu.SemaphoreType.DMA
    load = Bunch(**{name: one for name in loaded})
    store = Bunch(layer_output=one, grad_tokens=one, grad_encodings=one)
    bufs, sems = reducer_scratch()
    extra = dict(collective_id=0)
    if alone:
        bufs, sems = Bunch(own=pltpu.VMEM((2, 2, 2, CHUNK_ROWS, CHUNK_COLS), F32)), Bunch(out=pltpu.SemaphoreType.DMA((1,)))
        extra = {}
    else:
        vm.small = pltpu.VMEM((2, 4, SMALL_ROWS, CHUNK_COLS), F32)
    ins = [in_space(pl.ANY, **vars(hbm))]
    return call_grouped(
        lambda groups, *refs: layer_kernel(groups, alone, *refs), ins, [outs], [vm, load, store, bufs, sems],
        compiler_params=pltpu.CompilerParams(has_side_effects=True, vmem_limit_bytes=62 * 2**20, **extra),
        cost_estimate=pl.CostEstimate(flops=30 * 10**9, bytes_accessed=35 * 10**6, transcendentals=5 * 10**6))


FF_IN_AT, FF_OUT_AT, CROSS_OUT_AT, CROSS_Q_AT, CROSS_KV_AT, SELF_OUT_AT, SELF_QKV_AT = 0, 8, 16, 18, 20, 24, 26


def place_kernel(groups, *refs):
    given, out, vm = regroup(groups, refs)
    sems = iter(range(vm.sem.shape[0]))
    copy = lambda src, dst: pltpu.make_async_copy(src, dst, vm.sem.at[next(sems)])
    small_at = slice(CHUNKS * CHUNK_COLS, (CHUNKS + 1) * CHUNK_COLS)
    small = copy(given.chunks.at[0:SMALL_ROWS, small_at], vm.chunks.at[0:SMALL_ROWS, small_at])
    table = copy(given.tables, vm.tables)
    small.start()
    table.start()
    pieces = ((out.ff_in, FF_IN_AT), (out.ff_out, FF_OUT_AT), (out.cross_out, CROSS_OUT_AT), (out.cross_q, CROSS_Q_AT),
              (out.cross_kv, CROSS_KV_AT), (out.self_out, SELF_OUT_AT), (out.self_qkv, SELF_QKV_AT))
    moves = []
    for ref, first in pieces:
        cols = ref.shape[0] * ref.shape[1] // CHUNK_ROWS
        at = slice(first * CHUNK_COLS, first * CHUNK_COLS + cols)
        targets = [(vm.chunks.at[:, at], ref)]
        if first == FF_OUT_AT:
            targets = [(vm.chunks.at[:, (first + k) * CHUNK_COLS:(first + k + 1) * CHUNK_COLS],
                        ref.at[(k // 2) * 96:(k // 2) * 96 + 96, (k % 2) * CHUNK_COLS:(k % 2 + 1) * CHUNK_COLS])
                       for k in range(8)]
        moves.append((copy(given.chunks.at[:, at], vm.chunks.at[:, at]), [copy(*pair) for pair in targets]))
    for src, mid, dst in ((given.layer_output, vm.a, out.layer_output), (given.grad_tokens, vm.b, out.grad_tokens),
                          (given.grad_encodings, vm.c, out.grad_encodings)):
        moves.append((copy(src, mid), [copy(mid, dst)]))
    for into, _ in moves:
        into.start()
    small.wait()
    table.wait()
    sums = vm.chunks[0:SMALL_ROWS, small_at]
    for j in range(6):
        row, col = 8 * (j % 4), LANES * (j // 4)
        vm.mem_k[:, j * LANES:(j + 1) * LANES] = sums[row:row + 4, col:col + LANES]
        vm.mem_v[:, j * LANES:(j + 1) * LANES] = sums[row + 4:row + 8, col:col + LANES]
    for n, gain in enumerate((vm.gain_self, vm.gain_cross, vm.gain_ff)):
        gain[...] = sums[16 + n, LANES:LANES + 96]
    vm.rel_bias[...] = nt(sums[0:16, 2 * LANES:], vm.tables[1], precision=lax.Precision.HIGHEST)[0:12]
    made = [copy(vars(vm)[name], vars(out)[name]) for name in vars(vm) if name in vars(out)]
    for move in made:
        move.start()
    for into, onward in moves:
        into.wait()
        for move in onward:
            move.start()
    for move in made + [move for _, onward in moves for move in onward]:
        move.wait()


def place(done, tables):
    shape = jax.ShapeDtypeStruct
    outs = in_space(
        pl.ANY, layer_output=shape(done.layer_output.shape, BF16), grad_tokens=shape(done.grad_tokens.shape, BF16),
        grad_encodings=shape(done.grad_encodings.shape, BF16), ff_in=shape((96, 3072), F32), ff_out=shape((384, 768), F32),
        cross_out=shape((96, 768), F32), cross_q=shape((96, 768), F32), cross_kv=shape((96, 1536), F32),
        self_out=shape((96, 768), F32), self_qkv=shape((96, 2304), F32))
    small = Bunch(mem_k=(4, 768), mem_v=(4, 768), gain_self=(96,), gain_cross=(96,), gain_ff=(96,), rel_bias=(12, 32))
    vars(outs).update(vars(in_space(pl.ANY, **{name: shape(dims, F32) for name, dims in vars(small).items()})))
    scratch = Bunch(
        chunks=pltpu.VMEM(done.chunks.shape, F32), a=pltpu.VMEM(done.layer_output.shape, BF16),
        b=pltpu.VMEM(done.grad_tokens.shape, BF16), c=pltpu.VMEM(done.grad_encodings.shape, BF16),
        tables=pltpu.VMEM(tables.shape, F32), sem=pltpu.SemaphoreType.DMA((36,)),
        **{name: pltpu.VMEM(dims, F32) for name, dims in vars(small).items()})
    return call_grouped(
        place_kernel, [in_space(pl.ANY, tables=tables, **vars(done))], [outs], [scratch],
        compiler_params=pltpu.CompilerParams(vmem_limit_bytes=62 * 2**20),
        cost_estimate=pl.CostEstimate(flops=0, bytes_accessed=15 * 10**6, transcendentals=0))


def sum_alone(done, tables):
    chunks = done.chunks.transpose(0, 2, 3, 1, 4, 5).reshape(CHUNKS, 768, CHUNK_COLS)

    def whole(first, cols):
        part = chunks[first:first + cols // 384]
        return part.transpose(1, 0, 2).reshape(768, cols)

    ff_out = chunks[8:16].reshape(4, 2, 8, 96, CHUNK_COLS)
    parts = Bunch(
        ff_in=whole(FF_IN_AT, 3072), ff_out=ff_out.transpose(2, 0, 3, 1, 4).reshape(3072, 768),
        cross_out=whole(CROSS_OUT_AT, 768), cross_q=whole(CROSS_Q_AT, 768), cross_kv=whole(CROSS_KV_AT, 1536),
        self_out=whole(SELF_OUT_AT, 768), self_qkv=whole(SELF_QKV_AT, 2304), mem_k=done.mem_k, mem_v=done.mem_v,
        gain_self=done.gains[0], gain_cross=done.gains[1], gain_ff=done.gains[2])
    out = Bunch(**{name: lax.psum(lax.psum_scatter(value, "dp", scatter_dimension=0, tiled=True), "replica")
                   for name, value in vars(parts).items()})
    bias = lax.psum(done.bias, ("dp", "replica"))
    out.rel_bias = lax.dot_general(bias, tables[1], (((1,), (1,)), ((), ())), precision=lax.Precision.HIGHEST)
    out.layer_output, out.grad_tokens, out.grad_encodings = done.layer_output, done.grad_tokens, done.grad_encodings
    return out


def on_device(tokens, encodings, lengths, memory_ids, memory_keys, memory_values, gain_self, gain_cross, gain_ff,
              rel_bias, self_qkv, self_out, cross_q, cross_kv, cross_out, ff_in, ff_out, cotangent):
    width = tokens.shape[-1]
    alone = not (lax.axis_size("dp") == 8 and lax.axis_size("replica") == 4)
    tables = jnp.asarray(bucket_tables(LANES, rel_bias.shape[0]))
    hbm = Bunch(tokens=tokens.reshape(-1, width), encodings=encodings.reshape(-1, width),
                cotangent=cotangent.reshape(-1, width), memory_keys=memory_keys, memory_values=memory_values,
                self_qkv=self_qkv, self_out=self_out, cross_q=cross_q, cross_kv=cross_kv, cross_out=cross_out,
                ff_in=ff_in, ff_out=ff_out, lengths=lengths, ids=memory_ids, gain_self=gain_self,
                gain_cross=gain_cross, gain_ff=gain_ff, rel_bias=rel_bias.T, tables=tables)
    done = run_layer(alone, hbm)
    out = sum_alone(done, tables) if alone else place(done, tables)
    return (
        out.layer_output.reshape(tokens.shape), out.grad_tokens.reshape(tokens.shape),
        out.grad_encodings.reshape(encodings.shape), out.gain_self, out.gain_cross, out.gain_ff, out.rel_bias.T,
        out.self_qkv, out.self_out, out.cross_q, out.cross_kv, out.cross_out, out.ff_in, out.ff_out, out.mem_k,
        out.mem_v)


def solution(mesh):
    split, whole = P(("dp", "replica")), P()
    return jax.shard_map(
        on_device,
        mesh=mesh,
        in_specs=(split,) * 4 + (whole,) * 13 + (split,),
        out_specs=(split,) * 3 + (P("dp"),) * 3 + (whole,) + (P("dp"),) * 9,
        check_vma=False,
    )
```

```python
import functools
import itertools
from types import SimpleNamespace as Bunch

import jax
import jax.numpy as jnp
import numpy as np
from jax import lax
from jax.experimental import pallas as pl
from jax.experimental.pallas import tpu as pltpu
from jax.sharding import PartitionSpec as P

F32, BF16 = jnp.float32, jnp.bfloat16
EPSILON = 1e-06
NEGATIVE = -1000000000.0
MAXDIST = 128
LANES = 128
E3, B2, CQ, EKV, B1, QKV, RIGHT = 0, 768, 1536, 2304, 3840, 4608, 6912
L_H3, L_O2, L_H2, L_ENC, L_O, L_H1, L_R = 0, 1, 2, 3, 4, 5, 6
FF_TILE = 384
MEM_PAD = 16


def nn(a, b, **kw):
    return lax.dot_general(a, b, (((1,), (0,)), ((), ())), preferred_element_type=F32, **kw)


def nt(a, b, **kw):
    return lax.dot_general(a, b, (((1,), (1,)), ((), ())), preferred_element_type=F32, **kw)


def tn(a, b, **kw):
    return lax.dot_general(a, b, (((0,), (0,)), ((), ())), preferred_element_type=F32, **kw)


def bucket_of(apart, buckets, distance):
    exact = buckets // 2
    spread = np.log(np.maximum(apart, 1) / exact) / np.log(distance / exact) * (buckets - exact)
    larger = np.minimum(exact + np.floor(np.maximum(spread, 0.0)).astype(np.int64), buckets - 1)
    return np.where(apart < exact, apart, larger).astype(np.int32)


def bucket_tables(length, buckets):
    lane = np.arange(length)
    spread = [bucket_of((length - lane) % length, buckets, MAXDIST), bucket_of(length - 1 - lane, buckets, MAXDIST)]
    return np.stack([(np.arange(buckets)[:, None] == row[None]).astype(np.float32) for row in spread])


def root_scale(v):
    return lax.rsqrt(jnp.mean(v * v, axis=-1, keepdims=True) + EPSILON)


def normed(v, gain):
    return (v * root_scale(v) * gain).astype(BF16)


def norm_pull(v, gain, w):
    scale = root_scale(v)
    gw = w * gain
    back = scale * gw - v * (scale * scale * scale) * jnp.mean(gw * v, axis=-1, keepdims=True)
    return back, jnp.sum(w * v * scale, axis=0, keepdims=True)


def head_masks():
    lane = lax.broadcasted_iota(jnp.int32, (1, LANES), 1)
    first = jnp.where(lane < LANES // 2, 1.0, 0.0)
    return first.astype(BF16), (1.0 - first).astype(BF16), first > 0.5


def stacked(rows, m0, m1):
    return jnp.concatenate([rows * m0, rows * m1], axis=0)


def pair_softmax(s):
    parts = []
    for part in (s[:, :LANES], s[:, LANES:]):
        e = jnp.exp(part - jnp.max(part, axis=-1, keepdims=True))
        parts.append(e * (1.0 / jnp.sum(e, axis=-1, keepdims=True)))
    return jnp.concatenate(parts, axis=1)


def pair_pull(p, dp):
    parts = []
    for lo in (0, LANES):
        a, b = p[:, lo:lo + LANES], dp[:, lo:lo + LANES]
        parts.append((a * (b - jnp.sum(a * b, axis=-1, keepdims=True))).astype(BF16))
    return jnp.concatenate(parts, axis=1)


class Layer:
    def __init__(self, hbm, out, vm, load, store):
        vars(self).update(vars(vm))
        self.hbm, self.out, self.store = hbm, out, store
        self.layer_output, self.grad_tokens = vm.cotangent, vm.att2
        self.questions, self.length, self.enc_len = 4, 128, 64
        self.rows = self.questions * self.length
        self.load = Bunch(**{name: pltpu.make_async_copy(vars(hbm)[name], vars(vm)[name], sem)
                             for name, sem in vars(load).items()})

    def ff_loads(self, j):
        slot = lax.rem(j, 2)
        at = pl.ds(pl.multiple_of(j * FF_TILE, FF_TILE), FF_TILE)
        return (
            pltpu.make_async_copy(self.hbm.ff_in.at[:, at], self.wi.at[slot], self.wi_sem.at[slot]),
            pltpu.make_async_copy(self.hbm.ff_out.at[at, :], self.wo.at[slot], self.wo_sem.at[slot]),
        )

    def q_rows(self, q, n=128):
        return pl.ds(pl.multiple_of(q * n, n), n)

    def put_left(self, index, q, rows):
        turned = rows.T
        width = turned.shape[1]
        at = self.q_rows(q, width)
        for b in range(8):
            self.left[index, b % 2, (b // 2) * 96:(b // 2 + 1) * 96, at] = turned[b * 96:(b + 1) * 96]

    def bias_tables(self):
        table = nn(self.rel_bias[...], self.tables[0], precision=lax.Precision.HIGHEST)
        for p in range(6):
            for k in range(2):
                row = table[2 * p + k:2 * p + k + 1, :]
                self.bias[p, :, k * LANES:(k + 1) * LANES] = pltpu.roll(
                    jnp.broadcast_to(row, (LANES, LANES)), 0, 1, stride=1, stride_axis=0)

    def memory_rows(self):
        entries = self.memory_keys.shape[0]
        slot = lax.broadcasted_iota(jnp.int32, (MEM_PAD, entries), 0)
        entry = lax.broadcasted_iota(jnp.int32, (MEM_PAD, entries), 1)
        for q in range(self.questions):
            wanted = jnp.full((MEM_PAD, entries), -1, jnp.int32)
            for i in range(self.ids.shape[1]):
                wanted = jnp.where(slot == i, self.ids[q, i], wanted)
            pick = jnp.where(wanted == entry, 1.0, 0.0).astype(BF16)
            self.mem_k[q] = nn(pick, self.memory_keys[...]).astype(BF16)
            self.mem_v[q] = nn(pick, self.memory_values[...]).astype(BF16)

    def causal(self):
        row = lax.broadcasted_iota(jnp.int32, (LANES, 2 * LANES), 0)
        col = lax.rem(lax.broadcasted_iota(jnp.int32, (LANES, 2 * LANES), 1), LANES)
        return col <= row

    def self_probs(self, q2, k2, p, allowed):
        return pair_softmax(jnp.where(allowed, nt(q2, k2) + self.bias[p], NEGATIVE))

    def cross_probs(self, q2, k2, present):
        return pair_softmax(jnp.where(present, nt(q2, k2), -1e30))

    def present(self):
        col = lax.rem(lax.broadcasted_iota(jnp.int32, (1, 2 * LANES), 1), LANES)
        return col < self.enc_len + self.ids.shape[1]

    def cross_side(self, q, p, memory, base):
        enc = self.right[self.q_rows(q, self.enc_len), base + p * LANES:base + (p + 1) * LANES]
        mem = memory[q, :, p * LANES:(p + 1) * LANES]
        return jnp.concatenate([enc, mem, jnp.zeros((LANES - 64 - MEM_PAD, LANES), BF16)], axis=0)

    def forward(self, enter):
        load = self.load
        few = (load.gain_self, load.gain_cross, load.gain_ff, load.rel_bias, load.tables, load.lengths, load.ids)
        for copy in (load.tokens, load.self_qkv) + few + (load.encodings, load.cross_kv):
            copy.start()
        enter()
        for copy in few:
            copy.wait()
        for n, gain in enumerate((self.gain_self, self.gain_cross, self.gain_ff)):
            self.gains[n:n + 1, :] = gain[...].reshape(1, gain.shape[0])
        right = self.right
        self.bias_tables()
        self.load.tokens.wait()

        def norm_one(q, c):
            at = self.q_rows(q)
            self.hid[at] = normed(self.tokens[at].astype(F32), self.gains[0:1])
            return c
        lax.fori_loop(0, 4, norm_one, 0, unroll=4)
        self.load.self_qkv.wait()
        for copy in (load.memory_keys, load.memory_values, load.self_out, load.cross_q, load.cross_out, load.cotangent):
            copy.start()
        for copy in self.ff_loads(0) + self.ff_loads(1):
            copy.start()

        def qkv_tile(j, c):
            at = self.q_rows(j, 768)
            right[:, pl.ds(pl.multiple_of(QKV + j * 768, 768), 768)] = nn(self.hid[...], self.self_qkv[:, at]).astype(BF16)
            return c
        lax.fori_loop(0, 3, qkv_tile, 0, unroll=3)

        self.load.encodings.wait()
        self.load.cross_kv.wait()
        enc_rows = self.questions * self.enc_len

        def ekv_tile(j, c):
            at = self.q_rows(j, 768)
            col = pl.ds(pl.multiple_of(EKV + j * 768, 768), 768)
            right[0:enc_rows, col] = nn(self.encodings[...], self.cross_kv[:, at]).astype(BF16)
            return c
        lax.fori_loop(0, 2, ekv_tile, 0, unroll=2)
        self.load.memory_keys.wait()
        self.load.memory_values.wait()
        self.memory_rows()
        m0, m1, _ = head_masks()
        allowed = self.causal()

        def self_attention(q, c):
            at = self.q_rows(q)
            for p in range(6):
                lo = p * LANES
                q2, k2, v2 = (right[at, QKV + 768 * i + lo:QKV + 768 * i + lo + LANES] for i in range(3))
                probs = self.self_probs(q2, stacked(k2, m0, m1), p, allowed).astype(BF16)
                self.att[at, lo:lo + LANES] = nn(probs, stacked(v2, m0, m1)).astype(BF16)
            return c
        lax.fori_loop(0, 4, self_attention, 0, unroll=4)

        self.load.self_out.wait()

        def out_tile(j, c):
            at = self.q_rows(j, 768)
            self.y1[:, at] = self.tokens[:, at].astype(F32) + nn(self.att[...], self.self_out[:, at])
            return c
        lax.fori_loop(0, 1, out_tile, 0, unroll=1)

        def norm_two(q, c):
            at = self.q_rows(q)
            self.hid[at] = normed(self.y1[at], self.gains[1:2])
            return c
        lax.fori_loop(0, 4, norm_two, 0, unroll=4)
        self.load.cross_q.wait()

        def cq_tile(j, c):
            at = self.q_rows(j, 768)
            right[:, pl.ds(pl.multiple_of(CQ + j * 768, 768), 768)] = nn(self.hid[...], self.cross_q[:, at]).astype(BF16)
            return c
        lax.fori_loop(0, 1, cq_tile, 0, unroll=1)
        present = self.present()

        def cross_attention(q, c):
            at = self.q_rows(q)
            for p in range(6):
                lo = p * LANES
                keys = self.cross_side(q, p, self.mem_k, EKV)
                vals = self.cross_side(q, p, self.mem_v, EKV + 768)
                probs = self.cross_probs(right[at, CQ + lo:CQ + lo + LANES], stacked(keys, m0, m1), present)
                self.att2[at, lo:lo + LANES] = nn(probs.astype(BF16), stacked(vals, m0, m1)).astype(BF16)
            return c
        lax.fori_loop(0, 4, cross_attention, 0, unroll=4)
        self.load.cross_out.wait()

        def out2_tile(j, c):
            at = self.q_rows(j, 768)
            self.y2[:, at] = self.y1[:, at] + nn(self.att2[...], self.cross_out[:, at])
            return c
        lax.fori_loop(0, 1, out2_tile, 0, unroll=1)
        self.load.cotangent.wait()

        def norm_three(q, c):
            at = self.q_rows(q)
            h3 = normed(self.y2[at], self.gains[2:3])
            self.hid[at] = h3
            self.put_left(L_H3, q, h3)
            valid = lax.broadcasted_iota(jnp.int32, (LANES, 1), 0) < self.lengths[q]
            cot = jnp.where(valid, self.cotangent[at].astype(F32), 0.0)
            right[at, E3:E3 + 768] = cot.astype(BF16)
            return c
        lax.fori_loop(0, 4, norm_three, 0, unroll=4)

    def feed_forward(self):
        right = self.right
        self.y3[...] = self.y2[...]
        self.dh3[...] = jnp.zeros_like(self.dh3)

        def tile(j, c):
            slot = lax.rem(j, 2)
            for copy in self.ff_loads(j):
                copy.wait()
            for i in range(0, self.rows, 256):
                at = slice(i, i + 256)
                z = nn(self.hid[at], self.wi[slot])
                dr = nt(right[at, E3:E3 + 768], self.wo[slot]).astype(BF16).astype(F32)
                cdf = 0.5 * (1.0 + lax.erf(z * 0.7071067811865476))
                pdf = jnp.exp(-0.5 * z * z) * 0.3989422804014327
                self.act[at] = (z * cdf).astype(BF16)
                self.dz[at] = (dr * (cdf + z * pdf)).astype(BF16)
            act = self.act[...]
            dz = self.dz[...]

            self.advance(j, 0, lambda: dz)
            turned = act.T
            for g in range(4):
                at = pl.ds(pl.multiple_of((j // 2) * 96, 96), 96)
                self.left[L_R + g, lax.rem(j, 2), at, :] = turned[g * 96:(g + 1) * 96]
            self.y3[...] += nn(act, self.wo[slot])
            self.dh3[...] += nt(dz, self.wi[slot])

            @pl.when(j + 2 < 8)
            def _():
                for copy in self.ff_loads(j + 2):
                    copy.start()
            return c
        lax.fori_loop(0, 8, tile, 0)

        def finish(q, c):
            at = self.q_rows(q)
            valid = lax.broadcasted_iota(jnp.int32, (LANES, 1), 0) < self.lengths[q]
            self.layer_output[at] = jnp.where(valid, self.y3[at], 0.0).astype(BF16)
            return c
        lax.fori_loop(0, 4, finish, 0, unroll=4)
        self.stores()[0].start()

    def stores(self):
        return [pltpu.make_async_copy(vars(self)[name], vars(self.out)[name], sem) for name, sem in vars(self.store).items()]

    def put_lefts(self, index, rows):
        turned = rows.T
        for b in range(8):
            self.left[index, b % 2, (b // 2) * 96:(b // 2 + 1) * 96, 0:rows.shape[0]] = turned[b * 96:(b + 1) * 96]

    def row_blocks(self):
        return [slice(q * LANES, (q + 1) * LANES) for q in range(self.questions)]

    def in_steps(self, first, parts):
        count = sum(n for n, _ in parts)

        def step(i, c):
            at = 0
            for n, part in parts:
                pl.when((i >= at) & (i < at + n))(functools.partial(part, i - at))
                at += n
            self.advance(first + i)
            return c
        lax.fori_loop(0, count, step, 0)

    def backward_cross(self):
        right = self.right
        m0, m1, low_lanes = head_masks()
        present = self.present()
        enc_rows = self.questions * self.enc_len

        def pick(both):
            return jnp.where(low_lanes, both[:LANES], both[LANES:])

        def before(_):
            total = jnp.zeros((1, 768), F32)
            for at in self.row_blocks():
                back, gain = norm_pull(self.y2[at], self.gains[2:3], self.dh3[at])
                total += gain
                e2 = right[at, E3:E3 + 768].astype(F32) + back
                self.y3[at] = e2
                right[at, B2:B2 + 768] = e2.astype(BF16)
            self.dgains[2:3] = total
            self.up[...] = nt(right[:, B2:B2 + 768], self.cross_out[...]).astype(BF16)

        def attention(q):
            at = self.q_rows(q)
            enc_at = self.q_rows(q, self.enc_len)
            mem_at = self.q_rows(q, MEM_PAD)
            for p in range(6):
                lo = p * LANES
                pair = slice(lo, lo + LANES)
                keys = stacked(self.cross_side(q, p, self.mem_k, EKV), m0, m1)
                vals = stacked(self.cross_side(q, p, self.mem_v, EKV + 768), m0, m1)
                cq = right[at, CQ + lo:CQ + lo + LANES]
                probs = self.cross_probs(cq, keys, present)
                up = self.up[at, pair]
                dvals = pick(tn(probs.astype(BF16), up))
                ds = pair_pull(probs, nt(up, vals))
                dkeys = pick(tn(ds, cq))
                right[at, CQ + lo:CQ + lo + LANES] = nn(ds, keys).astype(BF16)
                right[enc_at, EKV + lo:EKV + lo + LANES] = dkeys[:64].astype(BF16)
                right[enc_at, EKV + 768 + lo:EKV + 768 + lo + LANES] = dvals[:64].astype(BF16)
                self.dmem_k[mem_at, pair] = dkeys[64:64 + MEM_PAD]
                self.dmem_v[mem_at, pair] = dvals[64:64 + MEM_PAD]

        def after(_):
            self.dh3[...] = nt(right[:, CQ:CQ + 768], self.cross_q[...])
            total = jnp.zeros((1, 768), F32)
            for at in self.row_blocks():
                back, gain = norm_pull(self.y1[at], self.gains[1:2], self.dh3[at])
                total += gain
                self.y3[at] += back
            self.dgains[1:2] = total

        def turn(_):
            for at in self.row_blocks():
                self.hid[at] = normed(self.y1[at], self.gains[1:2])
            self.put_lefts(L_H2, self.hid[...])
            self.put_lefts(L_O2, self.att2[...])

        def encodings(_):
            self.put_lefts(L_ENC, self.encodings[...])
            self.left[L_ENC, :, :, enc_rows:] = jnp.zeros((2, 384, self.rows - enc_rows), BF16)
            right[enc_rows:, EKV:EKV + 1536] = jnp.zeros((self.rows - enc_rows, 1536), BF16)
            self.grad_encodings[...] = nt(right[0:enc_rows, EKV:EKV + 1536], self.cross_kv[...]).astype(BF16)

        self.in_steps(8, ((1, before), (4, attention), (1, after), (1, turn), (1, encodings)))

    def backward_self(self):
        right = self.right
        m0, m1, low_lanes = head_masks()
        allowed = self.causal()

        def pick(both):
            return jnp.where(low_lanes, both[:LANES], both[LANES:])

        def before(_):
            self.dbias[...] = jnp.zeros_like(self.dbias)
            right[:, B1:B1 + 768] = self.y3[...].astype(BF16)
            self.up[...] = nt(right[:, B1:B1 + 768], self.self_out[...]).astype(BF16)

        def attention(q):
            at = self.q_rows(q)
            for p in range(6):
                lo = p * LANES
                q2, k2, v2 = (right[at, QKV + 768 * i + lo:QKV + 768 * i + lo + LANES] for i in range(3))
                keys = stacked(k2, m0, m1)
                probs = self.self_probs(q2, keys, p, allowed)
                up = self.up[at, lo:lo + LANES]
                dval = pick(tn(probs.astype(BF16), up))
                ds = pair_pull(probs, nt(up, stacked(v2, m0, m1)))
                self.dbias[p] += ds.astype(F32)
                right[at, QKV + lo:QKV + lo + LANES] = nn(ds, keys).astype(BF16)
                right[at, QKV + 768 + lo:QKV + 768 + lo + LANES] = pick(tn(ds, q2)).astype(BF16)
                right[at, QKV + 1536 + lo:QKV + 1536 + lo + LANES] = dval.astype(BF16)

        def after(_):
            self.dh3[...] = nt(right[:, QKV:QKV + 2304], self.self_qkv[...])

        def finish(_):
            total = jnp.zeros((1, 768), F32)
            for at in self.row_blocks():
                tok = self.tokens[at].astype(F32)
                back, gain = norm_pull(tok, self.gains[0:1], self.dh3[at])
                total += gain
                self.grad_tokens[at] = (self.y3[at] + back).astype(BF16)
            self.dgains[0:1] = total

        def turn(_):
            for at in self.row_blocks():
                self.hid[at] = normed(self.tokens[at].astype(F32), self.gains[0:1])
            self.put_lefts(L_H1, self.hid[...])
            self.put_lefts(L_O, self.att[...])

        self.in_steps(16, ((1, before), (4, attention), (1, after), (1, finish), (1, turn)))
        for copy in self.stores()[1:]:
            copy.start()

    def bias_rows(self):
        row = lax.broadcasted_iota(jnp.int32, (LANES, LANES), 0)
        col = lax.broadcasted_iota(jnp.int32, (LANES, LANES), 1)
        flip = jnp.where(row + col == LANES - 1, 1.0, 0.0)
        out = []
        for p in range(6):
            turned = nn(flip, self.dbias[p], precision=lax.Precision.HIGHEST)
            for k in range(2):
                rolled = pltpu.roll(turned[:, k * LANES:(k + 1) * LANES], 0, 1, stride=1, stride_axis=0)
                out.append(jnp.sum(rolled, axis=0, keepdims=True))
        return out

    def spread_ids(self, width):
        slot = lax.broadcasted_iota(jnp.int32, (4 * MEM_PAD, width), 0)
        wanted = jnp.full((4 * MEM_PAD, width), -1, jnp.int32)
        for q in range(self.questions):
            for i in range(self.ids.shape[1]):
                wanted = jnp.where(slot == q * MEM_PAD + i, self.ids[q, i], wanted)
        return wanted

    def advance(self, t, fixed=None, right=None):
        left, value = self.place(t)
        if fixed is not None:
            left, value = fixed, right

        def product(parity):
            return nn(self.left[left, parity], value())
        self.reducer.step(t, product)

    def place(self, d):
        u = d - 16
        late = jnp.where(u < 4, 1 + u // 2, jnp.where(u < 8, 3, jnp.where(u < 10, 4, 5)))
        left = jnp.where(d < 16, L_R + (d - 8) // 2, late)
        col = pl.multiple_of(jnp.where(d < 16, E3 + lax.rem(d, 2) * 384, B2 + u * 384), LANES)
        return left, lambda: self.right[:, pl.ds(col, 384)]


MESH_ID = pl.DeviceIdType.MESH
CHUNK_ROWS, CHUNK_COLS, PAIR_ROWS, SMALL_ROWS, SUM_ROWS = 96, 384, 48, 48, 32
PERIOD, GAP, LAST_PAIR, SMALL_FROM, LAST = 5, 26, 21, 29, 37
CHUNKS, SPLIT = 32, 4
DEPTH = Bunch(own=12, mid=10, snd=3, r0=3, rp=2, r1=6, r2=5, r3=5, r4=5)
LAG = Bunch(one=1, two=3, three=2, four=2, five=2, six=3)
LATE = Bunch(one=1, two=3, three=2, four=2, five=3, six=3)


def after(lags):
    return list(itertools.accumulate(vars(lags).values()))


def data_of(k):
    pair = (lax.rem(k, PERIOD) == 1) & (k <= GAP)
    return jnp.where(pair, k - PERIOD, jnp.where(k > GAP, k - 1, k))


def rows_of(k):
    return CHUNK_ROWS if k < SMALL_FROM else SUM_ROWS if k == SMALL_FROM else SMALL_ROWS


class Reducer:
    def __init__(self, bufs, sems, out_ref):
        self.b, self.s, self.out = bufs, sems, out_ref
        dp, z = lax.axis_index("dp"), lax.axis_index("replica")
        here = Bunch(dp=dp, replica=z)
        self.core = lax.rem(dp, 2)
        self.x = lax.rem(dp // 2, 2)
        self.y = dp // 4
        self.inner = lax.rem((z + 1) // 2, 2) == 1
        self.end = lax.rem((z + 1) // 2, 2) == 0
        self.near = pl.multiple_of(PAIR_ROWS * lax.rem(z, 2), PAIR_ROWS)
        self.far = pl.multiple_of(PAIR_ROWS * (1 - lax.rem(z, 2)), PAIR_ROWS)
        self.to_core = dict(vars(here), dp=dp + 1 - 2 * self.core)
        self.to_x = dict(vars(here), dp=dp + 2 - 4 * self.x)
        self.to_y = dict(vars(here), dp=dp + 4 - 8 * self.y)
        self.to_pair = dict(vars(here), replica=z + 1 - 2 * lax.rem(z, 2))
        self.to_mid = dict(vars(here), replica=3 - z)

    def enter(self):
        bar = pltpu.get_barrier_semaphore()
        for target in (self.to_core, self.to_x, self.to_y, self.to_pair, self.to_mid):
            pl.semaphore_signal(bar, inc=1, device_id=target, device_id_type=MESH_ID)

    def entered(self):
        pl.semaphore_wait(pltpu.get_barrier_semaphore(), 5)

    def copy(self, src, dst, send, recv, target):
        return pltpu.make_async_remote_copy(
            src_ref=src, dst_ref=dst, send_sem=send, recv_sem=recv, device_id=target, device_id_type=MESH_ID)

    def core_copy(self, k, n):
        a, r, rows = lax.rem(k, DEPTH.snd), lax.rem(k, DEPTH.r0), pl.ds(0, n)
        return self.copy(self.b.snd.at[a, :, rows], self.b.r0.at[r, :, rows], self.s.snd.at[a], self.s.r0.at[r],
                         self.to_core)

    def pair_copy(self, d):
        o, r = lax.rem(d + PERIOD, DEPTH.own), lax.rem(d // PERIOD, DEPTH.rp)
        return self.copy(self.b.own.at[o, :, :, pl.ds(self.far, PAIR_ROWS)], self.b.rp.at[r], self.s.sp.at[r],
                         self.s.rp.at[r], self.to_pair)

    def first_copies(self, k, n, base):
        o, r = lax.rem(k, DEPTH.own), lax.rem(k, DEPTH.r1)
        half = n // 2
        low, high, into = pl.ds(base, half), pl.ds(base + half, half), pl.ds(0, half)
        return (
            self.copy(self.b.own.at[o, :, 1 - self.x, low], self.b.r1x.at[r, :, into], self.s.s1x.at[r],
                      self.s.r1x.at[r], self.to_x),
            self.copy(self.b.own.at[o, 1 - self.y, :, high], self.b.r1y.at[r, :, into], self.s.s1y.at[r],
                      self.s.r1y.at[r], self.to_y),
        )

    def second_copies(self, k, n, base):
        o, r = lax.rem(k, DEPTH.own), lax.rem(k, DEPTH.r2)
        half = n // 2
        low, high, into = pl.ds(base, half), pl.ds(base + half, half), pl.ds(0, half)
        return (
            self.copy(self.b.own.at[o, self.y, 1 - self.x, high], self.b.r2x.at[r, into], self.s.s2x.at[r],
                      self.s.r2x.at[r], self.to_x),
            self.copy(self.b.own.at[o, 1 - self.y, self.x, low], self.b.r2y.at[r, into], self.s.s2y.at[r],
                      self.s.r2y.at[r], self.to_y),
        )

    def mine(self, k, n, base=0):
        return self.b.mid.at[lax.rem(k, DEPTH.mid), pl.ds(base, n)]

    def inward_copy(self, k, n, base):
        r = lax.rem(k, DEPTH.r3)
        return self.copy(self.mine(k, n, base), self.b.r3.at[r, pl.ds(0, n)], self.s.s3.at[r], self.s.r3.at[r],
                         self.to_pair)

    def middle_copy(self, k, n):
        r = lax.rem(k, DEPTH.r4)
        return self.copy(self.mine(k, n), self.b.r4.at[r, pl.ds(0, n)], self.s.s4.at[r], self.s.r4.at[r], self.to_mid)

    def result(self, k, n):
        if n == SUM_ROWS:
            row, d = 0, CHUNKS
        elif n == SMALL_ROWS:
            u = k - SMALL_FROM - 1
            row, d = lax.rem(u, 2) * SMALL_ROWS, CHUNKS - SPLIT + u // 2
        else:
            row, d = 0, data_of(k)
        return self.out.at[pl.ds(pl.multiple_of(row, 8), n), pl.ds(pl.multiple_of(d * CHUNK_COLS, LANES), CHUNK_COLS)]

    def outward_copy(self, k, n):
        r = lax.rem(k, DEPTH.r4)
        return self.copy(self.mine(k, n), self.result(k, n), self.s.s5.at[r], self.s.out.at[k], self.to_pair)

    def keep_copy(self, k, n):
        return pltpu.make_async_copy(self.mine(k, n), self.result(k, n), self.s.out.at[k])

    def grant(self, sem, k, depth, target):
        @pl.when(k + depth <= LAST)
        def _():
            pl.semaphore_signal(sem, inc=1, device_id=target, device_id_type=MESH_ID)

    def need(self, sem, k, depth):
        @pl.when((k >= depth) & (k != depth + 1))
        def _():
            pl.semaphore_wait(sem, 1)

    def before(self, t):
        return t - jnp.where(t == GAP + DEPTH.snd, 2 * DEPTH.snd, DEPTH.snd)

    def fill(self, t, half_product):
        n = CHUNK_ROWS
        early = (lax.rem(t, PERIOD) == 1) & (t <= LAST_PAIR)
        a, o = lax.rem(t, DEPTH.snd), lax.rem(jnp.where(early, t + PERIOD, t), DEPTH.own)

        @pl.when(t >= DEPTH.snd)
        def _():
            self.core_copy(self.before(t), n).wait_send()

        away = half_product(1 - self.core)
        for g in range(4):
            self.b.snd[a, g] = away[g * n:(g + 1) * n]

        @pl.when((t >= DEPTH.r0) & (t != GAP + DEPTH.r0))
        def _():
            pl.semaphore_wait(self.s.c0, 1)
        self.core_copy(t, n).start()
        here = half_product(self.core)
        for g in range(4):
            self.b.own[o, g // 2, g % 2] = here[g * n:(g + 1) * n]

    def fill_small(self, k, n, part):
        a, o = lax.rem(k, DEPTH.snd), lax.rem(k, DEPTH.own)

        @pl.when(k - DEPTH.snd < SMALL_FROM)
        def _():
            self.core_copy(self.before(k), CHUNK_ROWS).wait_send()

        @pl.when(k - DEPTH.snd == SMALL_FROM)
        def _():
            self.core_copy(k - DEPTH.snd, SUM_ROWS).wait_send()

        @pl.when(k - DEPTH.snd > SMALL_FROM)
        def _():
            self.core_copy(k - DEPTH.snd, SMALL_ROWS).wait_send()
        self.b.snd[a, :, 0:n, :] = part(1 - self.core)

        @pl.when(k != GAP + DEPTH.r0)
        def _():
            pl.semaphore_wait(self.s.c0, 1)
        self.core_copy(k, n).start()
        here = part(self.core)
        for g in range(4):
            self.b.own[o, g // 2, g % 2, 0:n, :] = here[g]

    def add_core(self, d, o, n):
        r = lax.rem(d, DEPTH.r0)
        self.core_copy(d, n).wait_recv()
        for g in range(4):
            self.b.own[o, g // 2, g % 2, 0:n] += self.b.r0[r, g, 0:n]

        @pl.when((d + DEPTH.r0 <= LAST) & (d + DEPTH.r0 != GAP))
        def _():
            pl.semaphore_signal(self.s.c0, inc=1, device_id=self.to_core, device_id_type=MESH_ID)

    def start_first(self, k, n, base):
        self.need(self.s.c1x, k, DEPTH.r1)
        self.need(self.s.c1y, k, DEPTH.r1)
        for copy in self.first_copies(k, n, base):
            copy.start()

    def stage_one(self, k, n):
        self.add_core(k, lax.rem(k, DEPTH.own), n)
        self.start_first(k, n, 0)

    def stage_pair(self, d):
        self.add_core(d, lax.rem(d + PERIOD, DEPTH.own), CHUNK_ROWS)

        @pl.when(d // PERIOD >= DEPTH.rp)
        def _():
            pl.semaphore_wait(self.s.cp, 1)
        self.pair_copy(d).start()

    def stage_one_pair(self, k):
        d = k - PERIOD
        o, r = lax.rem(k, DEPTH.own), lax.rem(d // PERIOD, DEPTH.rp)
        self.pair_copy(d).wait()
        rows = pl.ds(self.near, PAIR_ROWS)
        for g in range(4):
            self.b.own[o, g // 2, g % 2, rows] += self.b.rp[r, g // 2, g % 2]

        @pl.when(d + DEPTH.rp * PERIOD <= LAST_PAIR)
        def _():
            pl.semaphore_signal(self.s.cp, inc=1, device_id=self.to_pair, device_id_type=MESH_ID)
        self.start_first(k, PAIR_ROWS, self.near)

    def stage_two(self, k, n, base):
        o, r, half = lax.rem(k, DEPTH.own), lax.rem(k, DEPTH.r1), n // 2
        low, high = pl.ds(base, half), pl.ds(base + half, half)
        by_x, by_y = self.first_copies(k, n, base)
        on_x, on_y = self.second_copies(k, n, base)
        self.need(self.s.c2x, k, DEPTH.r2)
        self.need(self.s.c2y, k, DEPTH.r2)
        by_x.wait_recv()
        for g in range(2):
            self.b.own[o, g, self.x, low, :] += self.b.r1x[r, g, 0:half]
        on_y.start()
        by_y.wait_recv()
        for g in range(2):
            self.b.own[o, self.y, g, high, :] += self.b.r1y[r, g, 0:half]
        on_x.start()
        self.grant(self.s.c1x, k, DEPTH.r1, self.to_x)
        self.grant(self.s.c1y, k, DEPTH.r1, self.to_y)
        by_x.wait_send()
        by_y.wait_send()

    def stage_three(self, k, n, base):
        o, r, half = lax.rem(k, DEPTH.own), lax.rem(k, DEPTH.r2), n // 2
        low, high = pl.ds(base, half), pl.ds(base + half, half)
        m = lax.rem(k, DEPTH.mid)
        by_x, by_y = self.second_copies(k, n, base)
        by_x.wait_recv()
        self.b.mid[m, high, :] = self.b.own[o, self.y, self.x, high, :] + self.b.r2x[r, 0:half]
        by_y.wait_recv()
        self.b.mid[m, low, :] = self.b.own[o, self.y, self.x, low, :] + self.b.r2y[r, 0:half]

        @pl.when(self.end)
        def _():
            self.need(self.s.c3, k, DEPTH.r3)
            self.inward_copy(k, n, base).start()
        self.grant(self.s.c2x, k, DEPTH.r2, self.to_x)
        self.grant(self.s.c2y, k, DEPTH.r2, self.to_y)
        by_x.wait_send()
        by_y.wait_send()

    def stage_four(self, k, n, paired):
        r = lax.rem(k, DEPTH.r3)
        part = PAIR_ROWS if paired else n

        @pl.when(self.end)
        def _():
            self.inward_copy(k, part, self.near if paired else 0).wait_send()

        @pl.when(self.inner)
        def _():
            self.inward_copy(k, part, 0).wait_recv()
            if paired:
                self.b.mid[lax.rem(k, DEPTH.mid), pl.ds(self.far, part), :] = self.b.r3[r, 0:part]
            else:
                self.mine(k, n)[...] += self.b.r3[r, 0:n]
            self.need(self.s.c4, k, DEPTH.r4)
            self.middle_copy(k, n).start()
            self.grant(self.s.c3, k, DEPTH.r3, self.to_pair)

    def stage_five(self, k, n):
        r = lax.rem(k, DEPTH.r4)

        @pl.when(self.inner)
        def _():
            self.middle_copy(k, n).wait()
            self.mine(k, n)[...] += self.b.r4[r, 0:n]
            self.outward_copy(k, n).start()
            self.keep_copy(k, n).start()
            self.grant(self.s.c4, k, DEPTH.r4, self.to_mid)

    def stage_six(self, k, n):
        @pl.when(self.inner)
        def _():
            self.outward_copy(k, n).wait_send()
        self.keep_copy(k, n).wait()

    def stages(self):
        pair = PAIR_ROWS
        return (
            (lambda n, k: self.stage_one(k, n), self.stage_one_pair),
            (lambda n, k: self.stage_two(k, n, 0), lambda k: self.stage_two(k, pair, self.near)),
            (lambda n, k: self.stage_three(k, n, 0), lambda k: self.stage_three(k, pair, self.near)),
            (lambda n, k: self.stage_four(k, n, False), lambda k: self.stage_four(k, CHUNK_ROWS, True)),
            (lambda n, k: self.stage_five(k, n), None),
            (lambda n, k: self.stage_six(k, n), None),
        )

    def move(self, t):
        for behind, (usual, paired) in reversed(list(zip(after(LAG), self.stages()))):
            k = t - behind
            odd = (lax.rem(k + PERIOD, PERIOD) == 1) & (k <= GAP)
            plain = (k >= 0) & (k < SMALL_FROM) & (k != 1)
            if paired is not None:
                plain = plain & jnp.logical_not(odd)
                pl.when(odd & (k > 1))(functools.partial(paired, k))
            pl.when(plain)(functools.partial(usual, CHUNK_ROWS, k))
            pl.when(k == SMALL_FROM)(functools.partial(usual, SUM_ROWS, k))
            pl.when((k > SMALL_FROM) & (k <= LAST))(functools.partial(usual, SMALL_ROWS, k))
        d = t - LAG.one
        pl.when((lax.rem(d + PERIOD, PERIOD) == 1) & (d >= 0) & (d <= LAST_PAIR))(functools.partial(self.stage_pair, d))

    def drain(self):
        left = []
        for number, (due, order) in enumerate(zip(after(LAG), after(LATE))):
            left += [(k + order, -number, k) for k in range(LAST + 1) if k + due > LAST]
        for _, number, k in sorted(left):
            usual, paired = self.stages()[-number]
            if k % PERIOD == 1 and k <= GAP and paired is not None:
                paired(jnp.int32(k))
            else:
                usual(rows_of(k), jnp.int32(k))

    def step(self, t, half_product):
        self.move(t)
        self.fill(t, half_product)

    def finish(self, half, small):
        self.move(SMALL_FROM)
        self.fill_small(jnp.int32(SMALL_FROM), SUM_ROWS, lambda parity: small[parity])

        def body(k, c):
            self.move(k)
            self.fill_small(k, SMALL_ROWS, lambda parity: half(parity, k - SMALL_FROM - 1))
            return c
        lax.fori_loop(SMALL_FROM + 1, LAST + 1, body, 0)
        self.drain()
        for back in range(DEPTH.snd):
            self.core_copy(LAST - back, SMALL_ROWS).wait_send()


def reducer_scratch():
    rows, cols, half, count, d = CHUNK_ROWS, CHUNK_COLS, CHUNK_ROWS // 2, LAST + 1, DEPTH
    vmem = lambda *shape: pltpu.VMEM(shape, jnp.float32)
    dma = lambda n: pltpu.SemaphoreType.DMA((n,))
    plain = pltpu.SemaphoreType.REGULAR
    bufs = Bunch(
        own=vmem(d.own, 2, 2, rows, cols), mid=vmem(d.mid, rows, cols), snd=vmem(d.snd, 4, rows, cols),
        r0=vmem(d.r0, 4, rows, cols), rp=vmem(d.rp, 2, 2, PAIR_ROWS, cols), r1x=vmem(d.r1, 2, half, cols),
        r1y=vmem(d.r1, 2, half, cols), r2x=vmem(d.r2, half, cols), r2y=vmem(d.r2, half, cols),
        r3=vmem(d.r3, rows, cols), r4=vmem(d.r4, rows, cols))
    sems = Bunch(
        snd=dma(d.snd), r0=dma(d.r0), sp=dma(d.rp), rp=dma(d.rp), out=dma(count), s1x=dma(d.r1), r1x=dma(d.r1),
        s1y=dma(d.r1), r1y=dma(d.r1), s2x=dma(d.r2), r2x=dma(d.r2), s2y=dma(d.r2), r2y=dma(d.r2), s3=dma(d.r3),
        r3=dma(d.r3), s4=dma(d.r4), r4=dma(d.r4), s5=dma(d.r4), c0=plain, cp=plain, c1x=plain, c1y=plain, c2x=plain,
        c2y=plain, c3=plain, c4=plain)
    return bufs, sems


class PartWriter:
    def __init__(self, bufs, sems, out_ref):
        self.b, self.s, self.out = bufs, sems, out_ref

    def enter(self):
        pass

    def entered(self):
        pass

    def step(self, t, half_product):
        for parity in range(2):
            value = half_product(parity)
            for g in range(4):
                self.b.own[parity, g // 2, g % 2] = value[g * 96:(g + 1) * 96]
        copy = pltpu.make_async_copy(self.b.own, self.out.at[t], self.s.out.at[0])
        copy.start()
        copy.wait()


def regroup(groups, refs):
    result, first = [], 0
    for names in groups:
        result.append(Bunch(**dict(zip(names, refs[first:first + len(names)]))))
        first += len(names)
    return result


def layer_kernel(groups, alone, *refs):
    hbm, out, vm, load, store, bufs, sems = regroup(groups, refs)
    reducer = (PartWriter if alone else Reducer)(bufs, sems, out.chunks)
    layer = Layer(hbm, out, vm, load, store)
    layer.reducer = reducer
    layer.forward(reducer.enter)
    reducer.entered()
    layer.feed_forward()
    layer.backward_cross()
    layer.backward_self()

    if alone:
        def body(t, c):
            layer.advance(t)
            return c
        lax.fori_loop(24, CHUNKS, body, 0)
        entries = vm.memory_keys.shape[0]
        entry = lax.broadcasted_iota(jnp.int32, (4 * MEM_PAD, entries), 1)
        hit = jnp.where(layer.spread_ids(entries) == entry, 1.0, 0.0)
        out.mem_k[...] = tn(hit, vm.dmem_k[...], precision=lax.Precision.HIGHEST)
        out.mem_v[...] = tn(hit, vm.dmem_v[...], precision=lax.Precision.HIGHEST)
        out.gains[...] = vm.dgains[...]
        for h, row in enumerate(layer.bias_rows()):
            out.bias[h:h + 1, :] = row
    else:
        fill_small_rows(layer, vm)

        def body(t, c):
            left, value = layer.place(jnp.where(t > GAP, t - 1, t))
            reducer.move(t)

            @pl.when(t != GAP)
            def _():
                reducer.fill(t, lambda parity: nn(vm.left[left, parity], value()))
            return c
        lax.fori_loop(24, SMALL_FROM, body, 0)

        def half(parity, u):
            left, value = layer.place(CHUNKS - SPLIT + u // 2)
            at = lambda g: pl.ds(pl.multiple_of(g * 96 + lax.rem(u, 2) * SMALL_ROWS, SMALL_ROWS), SMALL_ROWS)
            rows = jnp.concatenate([vm.left[left, parity, at(g)] for g in range(4)], axis=0)
            return nn(rows, value()).reshape(4, SMALL_ROWS, CHUNK_COLS)
        reducer.finish(half, vm.small)
    for copy in layer.stores():
        copy.wait()


def fill_small_rows(layer, vm):
    out_row = lax.broadcasted_iota(jnp.int32, (4 * MEM_PAD, 64), 1)
    entry = 4 * (out_row // 8) + lax.rem(out_row, 4)
    same = layer.spread_ids(64) == entry
    keys_row = lax.rem(out_row // 4, 2) == 0
    hit_k = jnp.where(same & keys_row, 1.0, 0.0)
    hit_v = jnp.where(same & jnp.logical_not(keys_row), 1.0, 0.0)
    memory = (tn(hit_k, vm.dmem_k[...], precision=lax.Precision.HIGHEST)
              + tn(hit_v, vm.dmem_v[...], precision=lax.Precision.HIGHEST))
    bias = jnp.concatenate(layer.bias_rows() + [jnp.zeros((4, LANES), F32)], axis=0)
    gains = jnp.concatenate([vm.dgains[...], jnp.zeros((5, 768), F32)], axis=0)
    for b in range(8):
        block = vm.small.at[b % 2, b // 2]
        for j in range(6):
            row, col = 8 * (j % 4), LANES * (j // 4)
            block[row:row + 8, col:col + LANES] = memory[8 * b:8 * b + 8, j * LANES:(j + 1) * LANES]
        turned = gains if b == 0 else pltpu.roll(gains, 768 - 96 * b, 1)
        block[16:24, LANES:2 * LANES] = turned[:, :LANES]
        block[24:32, LANES:2 * LANES] = jnp.zeros((8, LANES), F32)
        block[0:16, 2 * LANES:] = bias
        block[16:32, 2 * LANES:] = jnp.zeros((16, LANES), F32)


def call_grouped(kernel, ins, outs, scratch, **options):
    groups = [list(vars(g)) for g in ins + outs + scratch]
    pairs = lambda gs, i: [v[i] for g in gs for v in vars(g).values()]
    space = lambda gs: [pl.BlockSpec(memory_space=s) for s in pairs(gs, 1)]
    result = pl.pallas_call(
        functools.partial(kernel, groups), out_shape=pairs(outs, 0), in_specs=space(ins), out_specs=space(outs),
        scratch_shapes=[v for g in scratch for v in vars(g).values()], **options)(*pairs(ins, 0))
    return regroup(groups[len(ins):len(ins) + len(outs)], result)[0]


def in_space(space, **values):
    return Bunch(**{name: (value, space) for name, value in values.items()})


def run_layer(alone, hbm):
    rows, width = hbm.tokens.shape
    enc_rows = hbm.encodings.shape[0]
    entries = hbm.memory_keys.shape[0]
    shape = jax.ShapeDtypeStruct
    outs = in_space(pl.ANY, layer_output=shape((rows, width), BF16), grad_tokens=shape((rows, width), BF16),
                    grad_encodings=shape((enc_rows, width), BF16))
    if alone:
        part = shape((entries, width), F32)
        vars(outs).update(vars(in_space(pl.ANY, chunks=shape((CHUNKS, 2, 2, 2, CHUNK_ROWS, CHUNK_COLS), F32))))
        vars(outs).update(vars(in_space(pltpu.VMEM, mem_k=part, mem_v=part, gains=shape((3, width), F32),
                                        bias=shape((12, LANES), F32))))
    else:
        vars(outs).update(vars(in_space(pl.ANY, chunks=shape((CHUNK_ROWS, (CHUNKS + 1) * CHUNK_COLS), F32))))
    loaded = [name for name in vars(hbm) if vars(hbm)[name] is not hbm.ff_in and vars(hbm)[name] is not hbm.ff_out]
    place_of = lambda v: (pltpu.SMEM if v.dtype == jnp.int32 else pltpu.VMEM)(v.shape, v.dtype)
    vm = Bunch(**{name: place_of(vars(hbm)[name]) for name in loaded})
    big = lambda cols, kind: pltpu.VMEM((rows, cols), kind)
    vars(vm).update(
        wi=pltpu.VMEM((2, width, FF_TILE), BF16), wo=pltpu.VMEM((2, FF_TILE, width), BF16),
        hid=big(width, BF16), att=big(width, BF16), att2=big(width, BF16), right=big(RIGHT, BF16),
        left=pltpu.VMEM((10, 2, 384, rows), BF16),
        y1=big(width, F32), y2=big(width, F32), y3=big(width, F32), dh3=big(width, F32),
        act=big(FF_TILE, BF16), dz=big(FF_TILE, BF16),
        bias=pltpu.VMEM((6, LANES, 2 * LANES), F32), dbias=pltpu.VMEM((6, LANES, 2 * LANES), F32),
        gains=pltpu.VMEM((3, width), F32), dgains=pltpu.VMEM((3, width), F32), up=big(width, BF16),
        mem_k=pltpu.VMEM((4, MEM_PAD, width), BF16), mem_v=pltpu.VMEM((4, MEM_PAD, width), BF16),
        dmem_k=pltpu.VMEM((4 * MEM_PAD, width), F32), dmem_v=pltpu.VMEM((4 * MEM_PAD, width), F32),
        grad_encodings=pltpu.VMEM((enc_rows, width), BF16),
        wi_sem=pltpu.SemaphoreType.DMA((2,)), wo_sem=pltpu.SemaphoreType.DMA((2,)))
    one = pltpu.SemaphoreType.DMA
    load = Bunch(**{name: one for name in loaded})
    store = Bunch(layer_output=one, grad_tokens=one, grad_encodings=one)
    bufs, sems = reducer_scratch()
    extra = dict(collective_id=0)
    if alone:
        bufs, sems = Bunch(own=pltpu.VMEM((2, 2, 2, CHUNK_ROWS, CHUNK_COLS), F32)), Bunch(out=pltpu.SemaphoreType.DMA((1,)))
        extra = {}
    else:
        vm.small = pltpu.VMEM((2, 4, SUM_ROWS, CHUNK_COLS), F32)
    ins = [in_space(pl.ANY, **vars(hbm))]
    return call_grouped(
        lambda groups, *refs: layer_kernel(groups, alone, *refs), ins, [outs], [vm, load, store, bufs, sems],
        compiler_params=pltpu.CompilerParams(has_side_effects=True, vmem_limit_bytes=62 * 2**20, **extra),
        cost_estimate=pl.CostEstimate(flops=30 * 10**9, bytes_accessed=35 * 10**6, transcendentals=5 * 10**6))


FF_IN_AT, FF_OUT_AT, CROSS_OUT_AT, CROSS_Q_AT, CROSS_KV_AT, SELF_OUT_AT, SELF_QKV_AT = 0, 8, 16, 18, 20, 24, 26


def place_kernel(groups, *refs):
    given, out, vm = regroup(groups, refs)
    sems = iter(range(vm.sem.shape[0]))
    copy = lambda src, dst: pltpu.make_async_copy(src, dst, vm.sem.at[next(sems)])
    small_at = slice(CHUNKS * CHUNK_COLS, (CHUNKS + 1) * CHUNK_COLS)
    small = copy(given.chunks.at[0:SUM_ROWS, small_at], vm.chunks.at[0:SUM_ROWS, small_at])
    table = copy(given.tables, vm.tables)
    small.start()
    table.start()
    pieces = ((out.ff_in, FF_IN_AT), (out.ff_out, FF_OUT_AT), (out.cross_out, CROSS_OUT_AT), (out.cross_q, CROSS_Q_AT),
              (out.cross_kv, CROSS_KV_AT), (out.self_out, SELF_OUT_AT), (out.self_qkv, SELF_QKV_AT))
    moves = []
    for ref, first in pieces:
        cols = ref.shape[0] * ref.shape[1] // CHUNK_ROWS
        at = slice(first * CHUNK_COLS, first * CHUNK_COLS + cols)
        targets = [(vm.chunks.at[:, at], ref)]
        if first == FF_OUT_AT:
            targets = [(vm.chunks.at[:, (first + k) * CHUNK_COLS:(first + k + 1) * CHUNK_COLS],
                        ref.at[(k // 2) * 96:(k // 2) * 96 + 96, (k % 2) * CHUNK_COLS:(k % 2 + 1) * CHUNK_COLS])
                       for k in range(8)]
        moves.append((copy(given.chunks.at[:, at], vm.chunks.at[:, at]), [copy(*pair) for pair in targets]))
    for src, mid, dst in ((given.layer_output, vm.a, out.layer_output), (given.grad_tokens, vm.b, out.grad_tokens),
                          (given.grad_encodings, vm.c, out.grad_encodings)):
        moves.append((copy(src, mid), [copy(mid, dst)]))
    for into, _ in moves:
        into.start()
    small.wait()
    table.wait()
    sums = vm.chunks[0:SUM_ROWS, small_at]
    for j in range(6):
        row, col = 8 * (j % 4), LANES * (j // 4)
        vm.mem_k[:, j * LANES:(j + 1) * LANES] = sums[row:row + 4, col:col + LANES]
        vm.mem_v[:, j * LANES:(j + 1) * LANES] = sums[row + 4:row + 8, col:col + LANES]
    for n, gain in enumerate((vm.gain_self, vm.gain_cross, vm.gain_ff)):
        gain[...] = sums[16 + n, LANES:LANES + 96]
    vm.rel_bias[...] = nt(sums[0:16, 2 * LANES:], vm.tables[1], precision=lax.Precision.HIGHEST)[0:12]
    made = [copy(vars(vm)[name], vars(out)[name]) for name in vars(vm) if name in vars(out)]
    for move in made:
        move.start()
    for into, onward in moves:
        into.wait()
        for move in onward:
            move.start()
    for move in made + [move for _, onward in moves for move in onward]:
        move.wait()


def place(done, tables):
    shape = jax.ShapeDtypeStruct
    outs = in_space(
        pl.ANY, layer_output=shape(done.layer_output.shape, BF16), grad_tokens=shape(done.grad_tokens.shape, BF16),
        grad_encodings=shape(done.grad_encodings.shape, BF16), ff_in=shape((96, 3072), F32), ff_out=shape((384, 768), F32),
        cross_out=shape((96, 768), F32), cross_q=shape((96, 768), F32), cross_kv=shape((96, 1536), F32),
        self_out=shape((96, 768), F32), self_qkv=shape((96, 2304), F32))
    small = Bunch(mem_k=(4, 768), mem_v=(4, 768), gain_self=(96,), gain_cross=(96,), gain_ff=(96,), rel_bias=(12, 32))
    vars(outs).update(vars(in_space(pl.ANY, **{name: shape(dims, F32) for name, dims in vars(small).items()})))
    scratch = Bunch(
        chunks=pltpu.VMEM(done.chunks.shape, F32), a=pltpu.VMEM(done.layer_output.shape, BF16),
        b=pltpu.VMEM(done.grad_tokens.shape, BF16), c=pltpu.VMEM(done.grad_encodings.shape, BF16),
        tables=pltpu.VMEM(tables.shape, F32), sem=pltpu.SemaphoreType.DMA((36,)),
        **{name: pltpu.VMEM(dims, F32) for name, dims in vars(small).items()})
    return call_grouped(
        place_kernel, [in_space(pl.ANY, tables=tables, **vars(done))], [outs], [scratch],
        compiler_params=pltpu.CompilerParams(vmem_limit_bytes=62 * 2**20),
        cost_estimate=pl.CostEstimate(flops=0, bytes_accessed=15 * 10**6, transcendentals=0))


def sum_alone(done, tables):
    chunks = done.chunks.transpose(0, 2, 3, 1, 4, 5).reshape(CHUNKS, 768, CHUNK_COLS)

    def whole(first, cols):
        part = chunks[first:first + cols // 384]
        return part.transpose(1, 0, 2).reshape(768, cols)

    ff_out = chunks[8:16].reshape(4, 2, 8, 96, CHUNK_COLS)
    parts = Bunch(
        ff_in=whole(FF_IN_AT, 3072), ff_out=ff_out.transpose(2, 0, 3, 1, 4).reshape(3072, 768),
        cross_out=whole(CROSS_OUT_AT, 768), cross_q=whole(CROSS_Q_AT, 768), cross_kv=whole(CROSS_KV_AT, 1536),
        self_out=whole(SELF_OUT_AT, 768), self_qkv=whole(SELF_QKV_AT, 2304), mem_k=done.mem_k, mem_v=done.mem_v,
        gain_self=done.gains[0], gain_cross=done.gains[1], gain_ff=done.gains[2])
    out = Bunch(**{name: lax.psum(lax.psum_scatter(value, "dp", scatter_dimension=0, tiled=True), "replica")
                   for name, value in vars(parts).items()})
    bias = lax.psum(done.bias, ("dp", "replica"))
    out.rel_bias = lax.dot_general(bias, tables[1], (((1,), (1,)), ((), ())), precision=lax.Precision.HIGHEST)
    out.layer_output, out.grad_tokens, out.grad_encodings = done.layer_output, done.grad_tokens, done.grad_encodings
    return out


def on_device(tokens, encodings, lengths, memory_ids, memory_keys, memory_values, gain_self, gain_cross, gain_ff,
              rel_bias, self_qkv, self_out, cross_q, cross_kv, cross_out, ff_in, ff_out, cotangent):
    width = tokens.shape[-1]
    alone = not (lax.axis_size("dp") == 8 and lax.axis_size("replica") == 4)
    tables = jnp.asarray(bucket_tables(LANES, rel_bias.shape[0]))
    hbm = Bunch(tokens=tokens.reshape(-1, width), encodings=encodings.reshape(-1, width),
                cotangent=cotangent.reshape(-1, width), memory_keys=memory_keys, memory_values=memory_values,
                self_qkv=self_qkv, self_out=self_out, cross_q=cross_q, cross_kv=cross_kv, cross_out=cross_out,
                ff_in=ff_in, ff_out=ff_out, lengths=lengths, ids=memory_ids, gain_self=gain_self,
                gain_cross=gain_cross, gain_ff=gain_ff, rel_bias=rel_bias.T, tables=tables)
    done = run_layer(alone, hbm)
    out = sum_alone(done, tables) if alone else place(done, tables)
    return (
        out.layer_output.reshape(tokens.shape), out.grad_tokens.reshape(tokens.shape),
        out.grad_encodings.reshape(encodings.shape), out.gain_self, out.gain_cross, out.gain_ff, out.rel_bias.T,
        out.self_qkv, out.self_out, out.cross_q, out.cross_kv, out.cross_out, out.ff_in, out.ff_out, out.mem_k,
        out.mem_v)


def solution(mesh):
    split, whole = P(("dp", "replica")), P()
    return jax.shard_map(
        on_device,
        mesh=mesh,
        in_specs=(split,) * 4 + (whole,) * 13 + (split,),
        out_specs=(split,) * 3 + (P("dp"),) * 3 + (whole,) + (P("dp"),) * 9,
        check_vma=False,
    )
```
